32 devices in a mesh: range: 2 (over y), radial: 16 (over z, x, core).
Axes of the slice: x: 2, y: 2, z: 4, core: 2. Of those that a mesh axis runs over, the one named last changes fastest.
Arguments:
- field_start: bfloat16 [2, 1024, 1024], P(None, 'radial'), may hold values from -6 to 6
- phase_table: float32 [16, 1024], replicated, may hold values from -1.5 to 1.5
- profile_index: int32 [2, 2], replicated, may hold values from 0 to 15
- group_power: float32 [2], replicated, may hold values from 0.3 to 3
- group_slot: int32 [2], replicated, may hold values from 0 to 1, each once
- source_shift: int32 [2, 16], P('range'), may hold values from 0 to 15
- slot_sub: int32 [2, 16, 16], P('range'), may hold values from 0 to 3
- tile_count: int32 [2, 16], P('range'), may hold values from 1 to 16, as said below
- row_weights: bfloat16 [2, 16, 16, 16, 256], P('range', 'radial'), may hold values from -0.375 to 0.375
- col_weights: bfloat16 [2, 16, 16, 256, 256], P('range', 'radial'), may hold values from -0.375 to 0.375
Outputs:
- interference: float32 [2, 16, 256, 256], P('range', 'radial')
The draws below stay inside these ranges and needn't reach their ends.
Inputs may be any that keep to these rules, and one draw needn't show every extreme that they name: `tile_count`: in every slab some tile uses all 16 slots.
All inputs are finite; a program needn't handle non-finite values.
Results may differ from the reference program's by a relative error of at most 0.04.
Values may be sent and summed in bfloat16 or wider, within the bound.
No kernel may reach another device: no remote copies, remote signals or barrier semaphores. Data moves between devices by JAX's collectives and lax.ppermute only.
A program may use at most 64 MiB of HBM per device.

```python
import math
import jax
import jax.numpy as jnp
from jax import lax

H = 1024
R_DEV = 64
STEPS = 2
VB = 128
SUB = 16
PIX = 256
K_MAX = 16
CAP = 2
GROUP_RADIALS = 512
PROFILES = 16
SLABS = 2
TILES = 16
RADIALS = 1024
GROUPS = 2
NSUB = 4
CHANNELS = 256
N_RADIAL = 16


def draw_tile_count(key, part):
    first_key, second_key = jax.random.split(jax.random.fold_in(key, 7))
    base = jax.random.randint(first_key, (SLABS, TILES), 1, K_MAX + 1)
    chosen = jax.random.randint(second_key, (SLABS,), 0, TILES)
    filled = jnp.arange(TILES)[None, :] == chosen[:, None]
    return jnp.where(filled, K_MAX, base).astype(jnp.int32)


def plant(values, stream_key, low, high):
    longest = values.shape.index(max(values.shape))
    spots = []
    for shift in (0, 1):
        where = [jax.random.randint(jax.random.fold_in(stream_key, axis), (), 0, length) for axis, length in enumerate(values.shape)]
        where[longest] = (where[longest] + shift) % values.shape[longest]
        spots.append(tuple(where))
    return values.at[spots[0]].set(low).at[spots[1]].set(high)


def block_levels(stream_key, extent, cuts, low, high):
    def one(position, parts):
        draws = jax.random.uniform(jax.random.fold_in(jax.random.fold_in(stream_key, 6), position), (parts,), jnp.float32, low / len(cuts), high / len(cuts))
        return jnp.repeat(jnp.exp(draws), extent[position] // parts).reshape((-1,) + (1,) * (len(extent) - position - 1))

    gain = one(*cuts[0])
    for cut in cuts[1:]:
        gain = gain * one(*cut)
    return gain


def normal_values(own_key, shape, spread, most, shards=(), kind=jnp.bfloat16):
    drawn = spread * jax.random.normal(own_key, shape, jnp.float32)
    if shards:
        drawn = drawn * block_levels(own_key, shape, shards, -0.22, 0.18)
    return jnp.clip(drawn, -most, most).astype(kind)


def setup_inputs(seed: int = 0) -> dict:
    keys = jax.random.split(jax.random.key(seed), 11)
    field_start = normal_values(keys[0], (2, RADIALS, H), 1.0, 6.0, ((1, 16),))
    phase_table = jnp.clip(jax.random.uniform(keys[1], (PROFILES, H), jnp.float32, -1.5, 1.5), -1.5, 1.5)
    profile_index = plant(jax.random.randint(keys[2], (SLABS, STEPS), 0, PROFILES), jax.random.fold_in(keys[2], 1), 0, PROFILES - 1).astype(jnp.int32)
    group_power = jnp.clip(jnp.exp(jax.random.uniform(keys[3], (GROUPS,), jnp.float32, math.log(0.3), math.log(3.0))), 0.3, 3.0)
    group_slot = jax.random.permutation(keys[4], GROUPS).astype(jnp.int32)
    source_shift = plant(jax.random.randint(keys[5], (SLABS, TILES), 0, TILES), jax.random.fold_in(keys[5], 1), 0, TILES - 1).astype(jnp.int32)
    slot_sub = plant(jax.random.randint(keys[6], (SLABS, TILES, K_MAX), 0, NSUB), jax.random.fold_in(keys[6], 1), 0, NSUB - 1).astype(jnp.int32)
    tile_count = draw_tile_count(jax.random.fold_in(keys[10], 71), 0)
    row_weights = normal_values(keys[8], (SLABS, TILES, K_MAX, SUB, PIX), (K_MAX * SUB) ** -0.5, 0.375, ((0, 2), (1, 16)))
    col_weights = normal_values(keys[9], (SLABS, TILES, K_MAX, CHANNELS, PIX), CHANNELS ** -0.5, 0.375, ((0, 2), (1, 16)))
    return {"field_start": field_start, "phase_table": phase_table, "profile_index": profile_index, "group_power": group_power, "group_slot": group_slot, "source_shift": source_shift, "slot_sub": slot_sub, "tile_count": tile_count, "row_weights": row_weights, "col_weights": col_weights}


spread_angle = 6.0
absorb_rate = 0.5

def dft_tables(height):
    index_row = jnp.arange(height, dtype=jnp.int32)
    product = index_row[:, None] * index_row[None, :] % height
    angle = 2.0 * math.pi / height * product.astype(jnp.float32)
    factor = 1.0 / math.sqrt(height)
    return ((jnp.cos(angle) * factor).astype(jnp.bfloat16), (jnp.sin(angle) * factor).astype(jnp.bfloat16))

def spectral_phase(height):
    index_row = jnp.arange(height, dtype=jnp.int32)
    folded = jnp.minimum(index_row, height - index_row).astype(jnp.float32)
    theta = -spread_angle * (2.0 * folded / height) ** 2
    return (jnp.cos(theta), jnp.sin(theta))

def absorber_profile(height):
    level = jnp.arange(height, dtype=jnp.int32).astype(jnp.float32)
    depth = jnp.maximum(0.0, (level - 0.9375 * height) / (0.0625 * height))
    return jnp.exp(-absorb_rate * depth * depth)

def march_slab(field, radial_gain, phases, cosine_table, sine_table, spectral_cos, spectral_sin, absorber, band):
    real_part = field[0]
    imag_part = field[1]
    row_total = real_part.shape[0]
    bands = []
    for step_index in range(phases.shape[0]):
        phase_cos = jnp.cos(phases[step_index])
        phase_sin = jnp.sin(phases[step_index])
        real_wide = real_part.astype(jnp.float32)
        imag_wide = imag_part.astype(jnp.float32)
        screened = jnp.concatenate([real_wide * phase_cos - imag_wide * phase_sin, real_wide * phase_sin + imag_wide * phase_cos], 0).astype(jnp.bfloat16)
        with_cos = jnp.dot(screened, cosine_table, preferred_element_type=jnp.float32)
        with_sin = jnp.dot(screened, sine_table, preferred_element_type=jnp.float32)
        spec_real = with_cos[:row_total] + with_sin[row_total:]
        spec_imag = with_cos[row_total:] - with_sin[:row_total]
        moved = jnp.concatenate([spec_real * spectral_cos - spec_imag * spectral_sin, spec_real * spectral_sin + spec_imag * spectral_cos], 0).astype(jnp.bfloat16)
        back_cos = jnp.dot(moved, cosine_table, preferred_element_type=jnp.float32)
        back_sin = jnp.dot(moved, sine_table, preferred_element_type=jnp.float32)
        real_part = ((back_cos[:row_total] - back_sin[row_total:]) * absorber).astype(jnp.bfloat16)
        imag_part = ((back_cos[row_total:] + back_sin[:row_total]) * absorber).astype(jnp.bfloat16)
        real_low = real_part.astype(jnp.float32)[:, :band]
        imag_low = imag_part.astype(jnp.float32)[:, :band]
        bands.append((radial_gain[:, None] * (real_low * real_low + imag_low * imag_low)).astype(jnp.bfloat16))
    return (jnp.stack([real_part, imag_part]), jnp.concatenate(bands, axis=1))

def reference(field_start, phase_table, profile_index, group_power, group_slot, source_shift, slot_sub, tile_count, row_weights, col_weights):
    cosine_table, sine_table = dft_tables(H)
    spectral_cos, spectral_sin = spectral_phase(H)
    absorber = absorber_profile(H)
    radial_ids = jnp.arange(RADIALS, dtype=jnp.int32)
    radial_gain = group_power[group_slot[radial_ids // GROUP_RADIALS]]
    field = field_start
    polar_list = []
    for slab_index in range(SLABS):
        phases = phase_table[profile_index[slab_index]]
        field, polar_block = march_slab(field, radial_gain, phases, cosine_table, sine_table, spectral_cos, spectral_sin, absorber, VB)
        polar_list.append(polar_block)
    polar = jnp.stack(polar_list)

    def one_slab(operands):
        polar_block, shift_row, sub_rows, count_row, row_part, col_part = operands
        slot_ids = jnp.arange(K_MAX, dtype=jnp.int32)
        tile_ids = jnp.arange(TILES, dtype=jnp.int32)
        source = (tile_ids[:, None] + shift_row[:, None] + (slot_ids // CAP)[None, :]) % N_RADIAL
        row_index = source[:, :, None] * R_DEV + sub_rows[:, :, None] * SUB + jnp.arange(SUB, dtype=jnp.int32)[None, None, :]
        pieces = polar_block[row_index]
        is_live = slot_ids[None, :] < count_row[:, None]
        pieces = jnp.where(is_live[:, :, None, None], pieces, jnp.zeros_like(pieces))
        mixed = jnp.einsum('tksc,tkcp->tksp', pieces.astype(jnp.float32), col_part.astype(jnp.float32)).astype(jnp.bfloat16)
        return jnp.einsum('tksp,tksq->tpq', row_part.astype(jnp.float32), mixed.astype(jnp.float32))
    return lax.map(one_slab, (polar, source_shift, slot_sub, tile_count, row_weights, col_weights))
```

```python
import functools
import math

import jax
import jax.numpy as jnp
import numpy as np
from jax import lax
from jax.experimental import pallas as pl
from jax.experimental.pallas import tpu as pltpu
from jax.sharding import PartitionSpec as P

VB = 128
SUB = 16
K_MAX = 16
CAP = 2
GROUP_RADIALS = 512
RADIX = 4

spread_angle = 6.0
absorb_rate = 0.5


def march_constants(height):
    quarter = height // RADIX
    index = np.arange(quarter)
    angle = 2.0 * np.pi / quarter * (index[:, None] * index[None, :] % quarter)
    factor = 1.0 / math.sqrt(height)
    cosine, sine = np.cos(angle) * factor, np.sin(angle) * factor
    weights = np.block([[cosine, -sine], [sine, cosine]]).astype(jnp.bfloat16)
    turn = 2.0 * np.pi / height * (np.arange(RADIX)[:, None] * index[None, :])
    level = np.arange(height)
    folded = np.minimum(level, height - level).astype(np.float64)
    theta = -spread_angle * (2.0 * folded / height) ** 2
    theta = theta.reshape(quarter, RADIX).T
    depth = np.maximum(0.0, (level - 0.9375 * height) / (0.0625 * height))
    absorber = np.exp(-absorb_rate * depth * depth).reshape(1, height)
    waves = np.concatenate([np.cos(turn), np.sin(turn), np.cos(theta), np.sin(theta)], 0)
    return weights, waves.astype(np.float32), absorber.astype(np.float32)


def cos_sin(angle):
    square = angle * angle
    cosine = jnp.full_like(angle, 1.0 / math.factorial(14) * -1.0)
    for order in (12, 10, 8, 6, 4, 2, 0):
        cosine = cosine * square + (-1.0) ** (order // 2) / math.factorial(order)
    sine = jnp.full_like(angle, 1.0 / math.factorial(13))
    for order in (11, 9, 7, 5, 3, 1):
        sine = sine * square + (-1.0) ** (order // 2) / math.factorial(order)
    return cosine, sine * angle


def march_kernel(
    steps,
    slabs,
    profile_ref,
    power_ref,
    slot_ref,
    field_ref,
    phase_ref,
    weight_ref,
    wave_ref,
    absorb_ref,
    polar_ref,
    phase_rows,
    screen_cos,
    screen_sin,
    real_ref,
    imag_ref,
    mixed_ref,
    moved_ref,
):
    rows, height = field_ref.shape[1:]
    quarter = height // RADIX
    slab = lax.axis_index("range")
    first_radial = lax.axis_index("radial") * rows
    gain = power_ref[slot_ref[first_radial // GROUP_RADIALS]]
    total = slabs * steps
    for place in range(total):
        phase_rows[place : place + 1, :] = phase_ref[
            pl.ds(profile_ref[place // steps, place % steps], 1), :
        ]
    cosine, sine = cos_sin(phase_rows[...])
    damp = jnp.where(lax.broadcasted_iota(jnp.int32, cosine.shape, 0) == 0, 1.0, absorb_ref[...])
    cosine, sine = cosine * damp, sine * damp
    for place in range(total):
        screen_cos[place] = jnp.broadcast_to(cosine[place : place + 1, :], (16, height))
        screen_sin[place] = jnp.broadcast_to(sine[place : place + 1, :], (16, height))
    real_ref[...] = field_ref[0].astype(jnp.float32)
    imag_ref[...] = field_ref[1].astype(jnp.float32)

    def one_step(place, step):
        for row in range(0, rows, 16):
            for lane in range(0, quarter, 128):
                parts = []
                for q in range(RADIX):
                    spot = (slice(row, row + 16), slice(q * quarter + lane, q * quarter + lane + 128))
                    phase_cos = screen_cos[place, :, spot[1]]
                    phase_sin = screen_sin[place, :, spot[1]]
                    real, imag = real_ref[spot], imag_ref[spot]
                    parts.append(
                        (real * phase_cos - imag * phase_sin, real * phase_sin + imag * phase_cos)
                    )
                (r0, i0), (r1, i1), (r2, i2), (r3, i3) = parts
                sr02, si02, dr02, di02 = r0 + r2, i0 + i2, r0 - r2, i0 - i2
                sr13, si13, dr13, di13 = r1 + r3, i1 + i3, r1 - r3, i1 - i3
                forward = (
                    (sr02 + sr13, si02 + si13),
                    (dr02 + di13, di02 - dr13),
                    (sr02 - sr13, si02 - si13),
                    (dr02 - di13, di02 + dr13),
                )
                for j, (real, imag) in enumerate(forward):
                    if j:
                        turn_cos = wave_ref[j : j + 1, lane : lane + 128]
                        turn_sin = wave_ref[RADIX + j : RADIX + j + 1, lane : lane + 128]
                        real, imag = (
                            real * turn_cos + imag * turn_sin,
                            imag * turn_cos - real * turn_sin,
                        )
                    spot = slice(j * rows + row, j * rows + row + 16)
                    mixed_ref[spot, lane : lane + 128] = real.astype(jnp.bfloat16)
                    mixed_ref[spot, quarter + lane : quarter + lane + 128] = imag.astype(jnp.bfloat16)
        spectrum = jnp.dot(mixed_ref[...], weight_ref[...], preferred_element_type=jnp.float32)
        for j in range(RADIX):
            theta_cos = wave_ref[2 * RADIX + j : 2 * RADIX + j + 1, :]
            theta_sin = wave_ref[3 * RADIX + j : 3 * RADIX + j + 1, :]
            real = spectrum[j * rows : (j + 1) * rows, :quarter]
            imag = spectrum[j * rows : (j + 1) * rows, quarter:]
            spot = slice(j * rows, (j + 1) * rows)
            moved_ref[spot, quarter:] = (real * theta_cos - imag * theta_sin).astype(jnp.bfloat16)
            moved_ref[spot, :quarter] = (real * theta_sin + imag * theta_cos).astype(jnp.bfloat16)
        back = jnp.dot(moved_ref[...], weight_ref[...], preferred_element_type=jnp.float32)
        for row in range(0, rows, 16):
            for lane in range(0, quarter, 128):
                parts = []
                for j in range(RADIX):
                    spot = slice(j * rows + row, j * rows + row + 16)
                    imag = back[spot, lane : lane + 128]
                    real = back[spot, quarter + lane : quarter + lane + 128]
                    if j:
                        turn_cos = wave_ref[j : j + 1, lane : lane + 128]
                        turn_sin = wave_ref[RADIX + j : RADIX + j + 1, lane : lane + 128]
                        real, imag = (
                            real * turn_cos - imag * turn_sin,
                            imag * turn_cos + real * turn_sin,
                        )
                    parts.append((real, imag))
                (r0, i0), (r1, i1), (r2, i2), (r3, i3) = parts
                sr02, si02, dr02, di02 = r0 + r2, i0 + i2, r0 - r2, i0 - i2
                sr13, si13, dr13, di13 = r1 + r3, i1 + i3, r1 - r3, i1 - i3
                inverse = (
                    (sr02 + sr13, si02 + si13),
                    (dr02 - di13, di02 + dr13),
                    (sr02 - sr13, si02 - si13),
                    (dr02 + di13, di02 - dr13),
                )
                for q, (real, imag) in enumerate(inverse):
                    spot = (slice(row, row + 16), slice(q * quarter + lane, q * quarter + lane + 128))
                    real_ref[spot] = real
                    imag_ref[spot] = imag
                    if q == 0 and lane < VB:
                        power = gain * (real * real + imag * imag)
                        polar_ref[row : row + 16, step * VB + lane : step * VB + lane + 128] = (
                            power.astype(jnp.bfloat16)
                        )

    def one_slab(number, carry):
        for step in range(steps):
            one_step(number * steps + step, step)
        return carry

    lax.fori_loop(0, slab + 1, one_slab, 0)


def march(field, phase_table, profile_index, group_power, group_slot):
    rows, height = field.shape[1:]
    slabs, steps = profile_index.shape
    weights, waves, absorber = march_constants(height)
    padded = -(-slabs * steps // 8) * 8
    smem = pl.BlockSpec(memory_space=pltpu.SMEM)
    vmem = pl.BlockSpec(memory_space=pltpu.VMEM)
    return pl.pallas_call(
        functools.partial(march_kernel, steps, slabs),
        out_shape=jax.ShapeDtypeStruct((rows, steps * VB), jnp.bfloat16),
        in_specs=[smem] * 3 + [vmem] * 5,
        out_specs=vmem,
        scratch_shapes=[
            pltpu.VMEM((padded, height), jnp.float32),
            pltpu.VMEM((slabs * steps, 16, height), jnp.float32),
            pltpu.VMEM((slabs * steps, 16, height), jnp.float32),
            pltpu.VMEM((rows, height), jnp.float32),
            pltpu.VMEM((rows, height), jnp.float32),
            pltpu.VMEM((rows * RADIX, 2 * height // RADIX), jnp.bfloat16),
            pltpu.VMEM((rows * RADIX, 2 * height // RADIX), jnp.bfloat16),
        ],
        compiler_params=pltpu.CompilerParams(vmem_limit_bytes=24 * 1024 * 1024),
        name="march",
    )(profile_index, group_power, group_slot, field, phase_table, weights, waves, absorber)


def tile_kernel(places, shift_ref, sub_ref, count_ref, place_ref, *refs):
    part_refs = refs[: len(places)]
    row_ref, col_ref, out_ref, polar_ref, mixed_ref = refs[len(places) :]
    tile = lax.axis_index("radial")
    devices = lax.axis_size("radial")
    local_rows = polar_ref.shape[0] // devices
    for number, part_ref in enumerate(part_refs):
        size = places[number]
        for piece in range(part_ref.shape[0] // size):
            start = pl.multiple_of(place_ref[number, piece] * local_rows, local_rows)
            polar_ref[pl.ds(start, size), :] = part_ref[piece * size : (piece + 1) * size, :]
    own_shift = shift_ref[0, tile]
    own_count = count_ref[0, tile]
    for slot in range(K_MAX):
        source = lax.rem(tile + own_shift + slot // CAP, devices)
        start = pl.multiple_of(source * local_rows + sub_ref[0, tile, slot] * SUB, SUB)
        block = polar_ref[pl.ds(start, SUB), :]
        block = jnp.where(slot < own_count, block, jnp.zeros_like(block))
        mixed = jnp.dot(block, col_ref[slot], preferred_element_type=jnp.float32)
        mixed_ref[slot * SUB : (slot + 1) * SUB, :] = mixed.astype(jnp.bfloat16)
    out_ref[...] = lax.dot_general(
        row_ref[...], mixed_ref[...], (((0,), (0,)), ((), ())), preferred_element_type=jnp.float32
    )


def tile_sum(parts, source_shift, slot_sub, tile_count, row_weights, col_weights, devices):
    pixels = row_weights.shape[-1]
    channels = col_weights.shape[-2]
    local_rows = sum(part.shape[0] for part, _, _ in parts) // devices
    most = max(len(places) for _, _, places in parts)
    table = jnp.stack(
        [jnp.stack([jnp.asarray(p, jnp.int32) for p in places + [0] * (most - len(places))]) for _, _, places in parts]
    )
    smem = pl.BlockSpec(memory_space=pltpu.SMEM)
    vmem = pl.BlockSpec(memory_space=pltpu.VMEM)
    return pl.pallas_call(
        functools.partial(tile_kernel, [size for _, size, _ in parts]),
        out_shape=jax.ShapeDtypeStruct((pixels, pixels), jnp.float32),
        in_specs=[smem] * 4 + [vmem] * (len(parts) + 2),
        out_specs=vmem,
        scratch_shapes=[
            pltpu.VMEM((devices * local_rows, channels), jnp.bfloat16),
            pltpu.VMEM((K_MAX * SUB, pixels), jnp.bfloat16),
        ],
        compiler_params=pltpu.CompilerParams(vmem_limit_bytes=24 * 1024 * 1024),
        name="tile_sum",
    )(
        source_shift,
        slot_sub,
        tile_count,
        table,
        *[part for part, _, _ in parts],
        row_weights.reshape(K_MAX * SUB, pixels),
        col_weights.reshape(K_MAX, channels, pixels),
    )


def swap(value, distance, devices):
    return lax.ppermute(value, "radial", [(i, i ^ distance) for i in range(devices)])


def gather_parts(polar, devices):
    local_rows = polar.shape[0]
    if devices != 16:
        whole = lax.all_gather(polar, "radial", axis=0, tiled=True)
        return [(whole, whole.shape[0], [0])]
    index = lax.axis_index("radial")
    core, chip = index % 2, index // 2
    sibling = swap(polar, 1, devices)
    pair = jnp.where(
        core == 0, jnp.concatenate([polar, sibling], 0), jnp.concatenate([sibling, polar], 0)
    )
    mine, theirs, size = [], [], 2 * local_rows
    held = []
    for pair_step in range(3):
        near, far = 2 * pair_step + 1, 2 * pair_step + 2
        routes = [(i, i ^ (2 * (near if i % 2 == 0 else far))) for i in range(devices)]
        held.append(lax.ppermute(pair, "radial", routes))
        mine.append(2 * (chip ^ jnp.where(core == 0, near, far)))
        theirs.append(2 * (chip ^ jnp.where(core == 0, far, near)))
    last = swap(polar, 14, devices)
    bundle = jnp.concatenate(held + [last], 0)
    other = swap(bundle, 1, devices)
    last_chip = 2 * (chip ^ 7)
    parts = [(polar, local_rows, [index]), (sibling, local_rows, [index ^ 1])]
    parts += [(h, size, [place]) for h, place in zip(held, mine)]
    parts.append((last, local_rows, [last_chip + core]))
    parts.append((other[: 3 * size], size, theirs))
    parts.append((other[3 * size :], local_rows, [last_chip + (1 - core)]))
    return parts


def per_device(
    field_start,
    phase_table,
    profile_index,
    group_power,
    group_slot,
    source_shift,
    slot_sub,
    tile_count,
    row_weights,
    col_weights,
):
    devices = lax.axis_size("radial")
    polar = march(field_start, phase_table, profile_index, group_power, group_slot)
    parts = gather_parts(polar, devices)
    tile_value = tile_sum(
        parts, source_shift, slot_sub, tile_count, row_weights, col_weights, devices
    )
    return tile_value.reshape((1, 1) + tile_value.shape)


def solution(mesh):
    return jax.shard_map(
        per_device,
        mesh=mesh,
        in_specs=(
            P(None, "radial", None),
            P(),
            P(),
            P(),
            P(),
            P("range", None),
            P("range", None, None),
            P("range", None),
            P("range", "radial", None, None, None),
            P("range", "radial", None, None, None),
        ),
        out_specs=P("range", "radial", None, None),
        check_vma=False,
    )
```

```python
import functools
import math

import jax
import jax.numpy as jnp
import numpy as np
from jax import lax
from jax.experimental import pallas as pl
from jax.experimental.pallas import tpu as pltpu
from jax.sharding import PartitionSpec as P

VB = 128
SUB = 16
K_MAX = 16
CAP = 2
GROUP_RADIALS = 512
RADIX = 4

spread_angle = 6.0
absorb_rate = 0.5


def march_constants(height):
    quarter = height // RADIX
    index = np.arange(quarter)
    angle = 2.0 * np.pi / quarter * (index[:, None] * index[None, :] % quarter)
    factor = 1.0 / math.sqrt(height)
    cosine, sine = np.cos(angle) * factor, np.sin(angle) * factor
    weights = np.block([[cosine, -sine], [sine, cosine]]).astype(jnp.bfloat16)
    turn = 2.0 * np.pi / height * (np.arange(RADIX)[:, None] * index[None, :])
    level = np.arange(height)
    folded = np.minimum(level, height - level).astype(np.float64)
    theta = -spread_angle * (2.0 * folded / height) ** 2
    theta = theta.reshape(quarter, RADIX).T
    depth = np.maximum(0.0, (level - 0.9375 * height) / (0.0625 * height))
    absorber = np.exp(-absorb_rate * depth * depth).reshape(RADIX, quarter)
    waves = np.concatenate([np.cos(turn), np.sin(turn), np.cos(theta), np.sin(theta), absorber], 0)
    waves = np.pad(waves, ((0, -len(waves) % 8), (0, 0)))
    return weights, waves.astype(np.float32)


def cos_sin(angle):
    square = angle * angle
    cosine = jnp.full_like(angle, 1.0 / math.factorial(14) * -1.0)
    for order in (12, 10, 8, 6, 4, 2, 0):
        cosine = cosine * square + (-1.0) ** (order // 2) / math.factorial(order)
    sine = jnp.full_like(angle, 1.0 / math.factorial(13))
    for order in (11, 9, 7, 5, 3, 1):
        sine = sine * square + (-1.0) ** (order // 2) / math.factorial(order)
    return cosine, sine * angle


def march_kernel(
    steps,
    slabs,
    profile_hbm,
    power_hbm,
    slot_hbm,
    shift_hbm,
    sub_hbm,
    count_hbm,
    field_hbm,
    phase_hbm,
    weight_hbm,
    wave_hbm,
    polar_ref,
    pick_ref,
    profile_ref,
    power_ref,
    slot_ref,
    shift_ref,
    sub_ref,
    count_ref,
    field_ref,
    phase_ref,
    weight_ref,
    wave_ref,
    phase_rows,
    screen_cos,
    screen_sin,
    real_ref,
    imag_ref,
    mixed_ref,
    moved_ref,
    sems,
):
    pairs = (
        (profile_hbm, profile_ref),
        (phase_hbm, phase_ref),
        (wave_hbm, wave_ref),
        (field_hbm, field_ref),
        (weight_hbm, weight_ref),
        (power_hbm, power_ref),
        (slot_hbm, slot_ref),
        (shift_hbm, shift_ref),
        (sub_hbm, sub_ref),
        (count_hbm, count_ref),
    )
    copies = [
        pltpu.make_async_copy(source, target, sems.at[number])
        for number, (source, target) in enumerate(pairs)
    ]
    for copy in copies:
        copy.start()
    rows, height = field_ref.shape[1:]
    quarter = height // RADIX
    slab = lax.axis_index("range")
    tile = lax.axis_index("radial")
    devices = lax.axis_size("radial")
    total = slabs * steps
    for copy in copies[:3]:
        copy.wait()
    for place in range(total):
        phase_rows[place : place + 1, :] = phase_ref[
            pl.ds(profile_ref[place // steps, place % steps], 1), :
        ]
    for q in range(RADIX):
        lanes = slice(q * quarter, (q + 1) * quarter)
        cosine, sine = cos_sin(phase_rows[:, lanes])
        absorber = wave_ref[4 * RADIX + q : 4 * RADIX + q + 1, :]
        damp = jnp.where(lax.broadcasted_iota(jnp.int32, cosine.shape, 0) == 0, 1.0, absorber)
        cosine, sine = cosine * damp, sine * damp
        for place in range(total):
            screen_cos[place, :, lanes] = jnp.broadcast_to(cosine[place : place + 1], (16, quarter))
            screen_sin[place, :, lanes] = jnp.broadcast_to(sine[place : place + 1], (16, quarter))
    for copy in copies[3:]:
        copy.wait()
    gain = power_ref[slot_ref[tile * rows // GROUP_RADIALS]]
    real_ref[...] = field_ref[0].astype(jnp.float32)
    imag_ref[...] = field_ref[1].astype(jnp.float32)

    shape = (SUB, pick_ref.shape[1])
    offset = lax.broadcasted_iota(jnp.int32, shape, 1) - lax.broadcasted_iota(jnp.int32, shape, 0)
    for slot in range(K_MAX):
        source = lax.rem(tile + shift_ref[0, tile] + slot // CAP, devices)
        start = source * rows + sub_ref[0, tile, slot] * SUB
        start = jnp.where(slot < count_ref[0, tile], start, -height * devices)
        pick_ref[slot * SUB : (slot + 1) * SUB, :] = jnp.where(offset == start, 1.0, 0.0).astype(
            jnp.bfloat16
        )

    def one_step(place, step):
        for row in range(0, rows, 16):
            for lane in range(0, quarter, 128):
                parts = []
                for q in range(RADIX):
                    spot = (slice(row, row + 16), slice(q * quarter + lane, q * quarter + lane + 128))
                    phase_cos = screen_cos[place, :, spot[1]]
                    phase_sin = screen_sin[place, :, spot[1]]
                    real, imag = real_ref[spot], imag_ref[spot]
                    parts.append(
                        (real * phase_cos - imag * phase_sin, real * phase_sin + imag * phase_cos)
                    )
                (r0, i0), (r1, i1), (r2, i2), (r3, i3) = parts
                sr02, si02, dr02, di02 = r0 + r2, i0 + i2, r0 - r2, i0 - i2
                sr13, si13, dr13, di13 = r1 + r3, i1 + i3, r1 - r3, i1 - i3
                forward = (
                    (sr02 + sr13, si02 + si13),
                    (dr02 + di13, di02 - dr13),
                    (sr02 - sr13, si02 - si13),
                    (dr02 - di13, di02 + dr13),
                )
                for j, (real, imag) in enumerate(forward):
                    if j:
                        turn_cos = wave_ref[j : j + 1, lane : lane + 128]
                        turn_sin = wave_ref[RADIX + j : RADIX + j + 1, lane : lane + 128]
                        real, imag = (
                            real * turn_cos + imag * turn_sin,
                            imag * turn_cos - real * turn_sin,
                        )
                    spot = slice(j * rows + row, j * rows + row + 16)
                    mixed_ref[spot, lane : lane + 128] = real.astype(jnp.bfloat16)
                    mixed_ref[spot, quarter + lane : quarter + lane + 128] = imag.astype(jnp.bfloat16)
        spectrum = jnp.dot(mixed_ref[...], weight_ref[...], preferred_element_type=jnp.float32)
        for j in range(RADIX):
            theta_cos = wave_ref[2 * RADIX + j : 2 * RADIX + j + 1, :]
            theta_sin = wave_ref[3 * RADIX + j : 3 * RADIX + j + 1, :]
            real = spectrum[j * rows : (j + 1) * rows, :quarter]
            imag = spectrum[j * rows : (j + 1) * rows, quarter:]
            spot = slice(j * rows, (j + 1) * rows)
            moved_ref[spot, quarter:] = (real * theta_cos - imag * theta_sin).astype(jnp.bfloat16)
            moved_ref[spot, :quarter] = (real * theta_sin + imag * theta_cos).astype(jnp.bfloat16)
        back = jnp.dot(moved_ref[...], weight_ref[...], preferred_element_type=jnp.float32)
        for row in range(0, rows, 16):
            for lane in range(0, quarter, 128):
                parts = []
                for j in range(RADIX):
                    spot = slice(j * rows + row, j * rows + row + 16)
                    imag = back[spot, lane : lane + 128]
                    real = back[spot, quarter + lane : quarter + lane + 128]
                    if j:
                        turn_cos = wave_ref[j : j + 1, lane : lane + 128]
                        turn_sin = wave_ref[RADIX + j : RADIX + j + 1, lane : lane + 128]
                        real, imag = (
                            real * turn_cos - imag * turn_sin,
                            imag * turn_cos + real * turn_sin,
                        )
                    parts.append((real, imag))
                (r0, i0), (r1, i1), (r2, i2), (r3, i3) = parts
                sr02, si02, dr02, di02 = r0 + r2, i0 + i2, r0 - r2, i0 - i2
                sr13, si13, dr13, di13 = r1 + r3, i1 + i3, r1 - r3, i1 - i3
                inverse = (
                    (sr02 + sr13, si02 + si13),
                    (dr02 - di13, di02 + dr13),
                    (sr02 - sr13, si02 - si13),
                    (dr02 + di13, di02 - dr13),
                )
                for q, (real, imag) in enumerate(inverse):
                    spot = (slice(row, row + 16), slice(q * quarter + lane, q * quarter + lane + 128))
                    real_ref[spot] = real
                    imag_ref[spot] = imag
                    if q == 0 and lane < VB:
                        power = gain * (real * real + imag * imag)
                        polar_ref[row : row + 16, step * VB + lane : step * VB + lane + 128] = (
                            power.astype(jnp.bfloat16)
                        )

    def one_slab(number, carry):
        for step in range(steps):
            one_step(number * steps + step, step)
        return carry

    lax.fori_loop(0, slab + 1, one_slab, 0)


def march(
    field, phase_table, profile_index, group_power, group_slot, source_shift, slot_sub, tile_count
):
    rows, height = field.shape[1:]
    slabs, steps = profile_index.shape
    weights, waves = march_constants(height)
    operands = [profile_index, group_power, group_slot, source_shift, slot_sub, tile_count]
    places = [pltpu.SMEM] * len(operands)
    operands += [field, phase_table, weights, waves]
    places += [pltpu.VMEM] * 4
    radials = rows * lax.axis_size("radial")
    return pl.pallas_call(
        functools.partial(march_kernel, steps, slabs),
        out_shape=[
            jax.ShapeDtypeStruct((rows, steps * VB), jnp.bfloat16),
            jax.ShapeDtypeStruct((K_MAX * SUB, radials), jnp.bfloat16),
        ],
        in_specs=[pl.BlockSpec(memory_space=pltpu.HBM)] * len(operands),
        out_specs=[pl.BlockSpec(memory_space=pltpu.VMEM)] * 2,
        scratch_shapes=[place(o.shape, o.dtype) for place, o in zip(places, operands)]
        + [
            pltpu.VMEM((-(-slabs * steps // 8) * 8, height), jnp.float32),
            pltpu.VMEM((slabs * steps, 16, height), jnp.float32),
            pltpu.VMEM((slabs * steps, 16, height), jnp.float32),
            pltpu.VMEM((rows, height), jnp.float32),
            pltpu.VMEM((rows, height), jnp.float32),
            pltpu.VMEM((rows * RADIX, 2 * height // RADIX), jnp.bfloat16),
            pltpu.VMEM((rows * RADIX, 2 * height // RADIX), jnp.bfloat16),
            pltpu.SemaphoreType.DMA((len(operands),)),
        ],
        compiler_params=pltpu.CompilerParams(vmem_limit_bytes=24 * 1024 * 1024),
        name="march",
    )(*[pltpu.with_memory_space_constraint(o, pltpu.HBM) for o in operands])


def tile_kernel(places, pick_ref, *refs):
    part_refs = refs[: len(places)]
    row_ref, col_ref, out_ref, polar_ref, mixed_ref = refs[len(places) :]
    chip = lax.axis_index("radial") // 2
    core = lax.axis_index("radial") % 2
    for (even, odd), part_ref in zip(places, part_refs):
        size = part_ref.shape[0]
        start = jnp.where(core == 0, chip ^ even, chip ^ odd) * size
        if size == polar_ref.shape[0]:
            start = 0
        polar_ref[pl.ds(start, size), :] = part_ref[...]
    blocks = jnp.dot(pick_ref[...], polar_ref[...], preferred_element_type=jnp.float32)
    blocks = blocks.astype(jnp.bfloat16)
    for slot in range(K_MAX):
        block = blocks[slot * SUB : (slot + 1) * SUB]
        mixed = jnp.dot(block, col_ref[slot], preferred_element_type=jnp.float32)
        mixed_ref[slot * SUB : (slot + 1) * SUB, :] = mixed.astype(jnp.bfloat16)
    out_ref[...] = lax.dot_general(
        row_ref[...], mixed_ref[...], (((0,), (0,)), ((), ())), preferred_element_type=jnp.float32
    )


def tile_sum(pick, parts, places, row_weights, col_weights):
    pixels = row_weights.shape[-1]
    channels = col_weights.shape[-2]
    vmem = pl.BlockSpec(memory_space=pltpu.VMEM)
    return pl.pallas_call(
        functools.partial(tile_kernel, places),
        out_shape=jax.ShapeDtypeStruct((pixels, pixels), jnp.float32),
        in_specs=[vmem] * (len(parts) + 3),
        out_specs=vmem,
        scratch_shapes=[
            pltpu.VMEM((pick.shape[1], channels), jnp.bfloat16),
            pltpu.VMEM((K_MAX * SUB, pixels), jnp.bfloat16),
        ],
        compiler_params=pltpu.CompilerParams(vmem_limit_bytes=24 * 1024 * 1024),
        name="tile_sum",
    )(
        pick,
        *parts,
        row_weights.reshape(K_MAX * SUB, pixels),
        col_weights.reshape(K_MAX, channels, pixels),
    )


def swap(value, distance, devices):
    return lax.ppermute(value, "radial", [(i, i ^ distance) for i in range(devices)])


def gather_parts(polar, devices):
    if devices != 16:
        return [lax.all_gather(polar, "radial", axis=0, tiled=True)], [(0, 0)]
    core = lax.axis_index("radial") % 2
    size = 2 * polar.shape[0]

    def in_order(own, other):
        return jnp.where(
            core == 0, jnp.concatenate([own, other], 0), jnp.concatenate([other, own], 0)
        )

    pair = in_order(polar, swap(polar, 1, devices))
    held = []
    for even, odd in ((1, 2), (3, 4), (5, 6)):
        routes = [(i, i ^ (2 * (odd if i % 2 else even))) for i in range(devices)]
        held.append(lax.ppermute(pair, "radial", routes))
    last = swap(polar, 14, devices)
    other = swap(jnp.concatenate(held + [last], 0), 1, devices)
    parts = [pair] + held + [other[i * size : (i + 1) * size] for i in range(3)]
    parts.append(in_order(last, other[3 * size :]))
    places = [(0, 0), (1, 2), (3, 4), (5, 6), (2, 1), (4, 3), (6, 5), (7, 7)]
    return parts, places


def per_device(
    field_start,
    phase_table,
    profile_index,
    group_power,
    group_slot,
    source_shift,
    slot_sub,
    tile_count,
    row_weights,
    col_weights,
):
    devices = lax.axis_size("radial")
    polar, pick = march(
        field_start,
        phase_table,
        profile_index,
        group_power,
        group_slot,
        source_shift,
        slot_sub,
        tile_count,
    )
    parts, places = gather_parts(polar, devices)
    tile_value = tile_sum(pick, parts, places, row_weights, col_weights)
    return tile_value.reshape((1, 1) + tile_value.shape)


def solution(mesh):
    return jax.shard_map(
        per_device,
        mesh=mesh,
        in_specs=(
            P(None, "radial", None),
            P(),
            P(),
            P(),
            P(),
            P("range", None),
            P("range", None, None),
            P("range", None),
            P("range", "radial", None, None, None),
            P("range", "radial", None, None, None),
        ),
        out_specs=P("range", "radial", None, None),
        check_vma=False,
    )
```

```python
import functools
import math

import jax
import jax.numpy as jnp
import numpy as np
from jax import lax
from jax.experimental import pallas as pl
from jax.experimental.pallas import tpu as pltpu
from jax.sharding import PartitionSpec as P

VB = 128
SUB = 16
K_MAX = 16
CAP = 2
GROUP_RADIALS = 512
RADIX = 4

spread_angle = 6.0
absorb_rate = 0.5


def march_constants(height):
    quarter = height // RADIX
    index = np.arange(quarter)
    angle = 2.0 * np.pi / quarter * (index[:, None] * index[None, :] % quarter)
    factor = 1.0 / math.sqrt(height)
    cosine, sine = np.cos(angle) * factor, np.sin(angle) * factor
    weights = np.block([[cosine, -sine], [sine, cosine]]).astype(jnp.bfloat16)
    turn = 2.0 * np.pi / height * (np.arange(RADIX)[:, None] * index[None, :])
    level = np.arange(height)
    folded = np.minimum(level, height - level).astype(np.float64)
    theta = -spread_angle * (2.0 * folded / height) ** 2
    theta = theta.reshape(quarter, RADIX).T
    depth = np.maximum(0.0, (level - 0.9375 * height) / (0.0625 * height))
    absorber = np.exp(-absorb_rate * depth * depth).reshape(RADIX, quarter)
    waves = np.concatenate([np.cos(turn), np.sin(turn), np.cos(theta), np.sin(theta), absorber], 0)
    waves = np.pad(waves, ((0, -len(waves) % 8), (0, 0)))
    return weights, waves.astype(np.float32)


def cos_sin(angle):
    square = angle * angle
    cosine = jnp.full_like(angle, 1.0 / math.factorial(14) * -1.0)
    for order in (12, 10, 8, 6, 4, 2, 0):
        cosine = cosine * square + (-1.0) ** (order // 2) / math.factorial(order)
    sine = jnp.full_like(angle, 1.0 / math.factorial(13))
    for order in (11, 9, 7, 5, 3, 1):
        sine = sine * square + (-1.0) ** (order // 2) / math.factorial(order)
    return cosine, sine * angle


def march_kernel(
    steps,
    slabs,
    profile_hbm,
    power_hbm,
    slot_hbm,
    shift_hbm,
    sub_hbm,
    count_hbm,
    field_hbm,
    phase_hbm,
    weight_hbm,
    wave_hbm,
    row_hbm,
    col_hbm,
    polar_ref,
    pick_ref,
    turned_ref,
    col_ref,
    profile_ref,
    power_ref,
    slot_ref,
    shift_ref,
    sub_ref,
    count_ref,
    field_ref,
    phase_ref,
    weight_ref,
    wave_ref,
    row_ref,
    phase_rows,
    screen_cos,
    screen_sin,
    real_ref,
    imag_ref,
    mixed_ref,
    moved_ref,
    sems,
):
    pairs = (
        (profile_hbm, profile_ref),
        (phase_hbm, phase_ref),
        (wave_hbm, wave_ref),
        (field_hbm, field_ref),
        (weight_hbm, weight_ref),
        (power_hbm, power_ref),
        (slot_hbm, slot_ref),
        (shift_hbm, shift_ref),
        (sub_hbm, sub_ref),
        (count_hbm, count_ref),
        (row_hbm, row_ref),
        (col_hbm, col_ref),
    )
    copies = [
        pltpu.make_async_copy(source, target, sems.at[number])
        for number, (source, target) in enumerate(pairs)
    ]
    for copy in copies[:-1]:
        copy.start()
    rows, height = field_ref.shape[1:]
    quarter = height // RADIX
    slab = lax.axis_index("range")
    tile = lax.axis_index("radial")
    devices = lax.axis_size("radial")
    total = slabs * steps
    for copy in copies[:3]:
        copy.wait()
    for place in range(total):
        phase_rows[place : place + 1, :] = phase_ref[
            pl.ds(profile_ref[place // steps, place % steps], 1), :
        ]
    for q in range(RADIX):
        lanes = slice(q * quarter, (q + 1) * quarter)
        cosine, sine = cos_sin(phase_rows[:, lanes])
        absorber = wave_ref[4 * RADIX + q : 4 * RADIX + q + 1, :]
        damp = jnp.where(lax.broadcasted_iota(jnp.int32, cosine.shape, 0) == 0, 1.0, absorber)
        cosine, sine = cosine * damp, sine * damp
        for place in range(total):
            screen_cos[place, :, lanes] = jnp.broadcast_to(cosine[place : place + 1], (16, quarter))
            screen_sin[place, :, lanes] = jnp.broadcast_to(sine[place : place + 1], (16, quarter))
    for copy in copies[5:-1]:
        copy.wait()
    gain = power_ref[slot_ref[tile * rows // GROUP_RADIALS]]
    shape = (SUB, pick_ref.shape[1])
    offset = lax.broadcasted_iota(jnp.int32, shape, 1) - lax.broadcasted_iota(jnp.int32, shape, 0)
    for slot in range(K_MAX):
        source = lax.rem(tile + shift_ref[0, tile] + slot // CAP, devices)
        start = source * rows + sub_ref[0, tile, slot] * SUB
        start = jnp.where(slot < count_ref[0, tile], start, -height * devices)
        pick_ref[slot * SUB : (slot + 1) * SUB, :] = jnp.where(offset == start, 1.0, 0.0).astype(
            jnp.bfloat16
        )

    turned_ref[...] = row_ref[...].T
    for copy in copies[3:5]:
        copy.wait()
    copies[-1].start()
    real_ref[...] = field_ref[0].astype(jnp.float32)
    imag_ref[...] = field_ref[1].astype(jnp.float32)

    def one_step(place, step):
        for row in range(0, rows, 16):
            for lane in range(0, quarter, 128):
                parts = []
                for q in range(RADIX):
                    spot = (slice(row, row + 16), slice(q * quarter + lane, q * quarter + lane + 128))
                    phase_cos = screen_cos[place, :, spot[1]]
                    phase_sin = screen_sin[place, :, spot[1]]
                    real, imag = real_ref[spot], imag_ref[spot]
                    parts.append(
                        (real * phase_cos - imag * phase_sin, real * phase_sin + imag * phase_cos)
                    )
                (r0, i0), (r1, i1), (r2, i2), (r3, i3) = parts
                sr02, si02, dr02, di02 = r0 + r2, i0 + i2, r0 - r2, i0 - i2
                sr13, si13, dr13, di13 = r1 + r3, i1 + i3, r1 - r3, i1 - i3
                forward = (
                    (sr02 + sr13, si02 + si13),
                    (dr02 + di13, di02 - dr13),
                    (sr02 - sr13, si02 - si13),
                    (dr02 - di13, di02 + dr13),
                )
                for j, (real, imag) in enumerate(forward):
                    if j:
                        turn_cos = wave_ref[j : j + 1, lane : lane + 128]
                        turn_sin = wave_ref[RADIX + j : RADIX + j + 1, lane : lane + 128]
                        real, imag = (
                            real * turn_cos + imag * turn_sin,
                            imag * turn_cos - real * turn_sin,
                        )
                    spot = slice(j * rows + row, j * rows + row + 16)
                    mixed_ref[spot, lane : lane + 128] = real.astype(jnp.bfloat16)
                    mixed_ref[spot, quarter + lane : quarter + lane + 128] = imag.astype(jnp.bfloat16)
        spectrum = jnp.dot(mixed_ref[...], weight_ref[...], preferred_element_type=jnp.float32)
        for j in range(RADIX):
            theta_cos = wave_ref[2 * RADIX + j : 2 * RADIX + j + 1, :]
            theta_sin = wave_ref[3 * RADIX + j : 3 * RADIX + j + 1, :]
            real = spectrum[j * rows : (j + 1) * rows, :quarter]
            imag = spectrum[j * rows : (j + 1) * rows, quarter:]
            spot = slice(j * rows, (j + 1) * rows)
            moved_ref[spot, quarter:] = (real * theta_cos - imag * theta_sin).astype(jnp.bfloat16)
            moved_ref[spot, :quarter] = (real * theta_sin + imag * theta_cos).astype(jnp.bfloat16)
        back = jnp.dot(moved_ref[...], weight_ref[...], preferred_element_type=jnp.float32)
        for row in range(0, rows, 16):
            for lane in range(0, quarter, 128):
                parts = []
                for j in range(RADIX):
                    spot = slice(j * rows + row, j * rows + row + 16)
                    imag = back[spot, lane : lane + 128]
                    real = back[spot, quarter + lane : quarter + lane + 128]
                    if j:
                        turn_cos = wave_ref[j : j + 1, lane : lane + 128]
                        turn_sin = wave_ref[RADIX + j : RADIX + j + 1, lane : lane + 128]
                        real, imag = (
                            real * turn_cos - imag * turn_sin,
                            imag * turn_cos + real * turn_sin,
                        )
                    parts.append((real, imag))
                (r0, i0), (r1, i1), (r2, i2), (r3, i3) = parts
                sr02, si02, dr02, di02 = r0 + r2, i0 + i2, r0 - r2, i0 - i2
                sr13, si13, dr13, di13 = r1 + r3, i1 + i3, r1 - r3, i1 - i3
                inverse = (
                    (sr02 + sr13, si02 + si13),
                    (dr02 - di13, di02 + dr13),
                    (sr02 - sr13, si02 - si13),
                    (dr02 + di13, di02 - dr13),
                )
                for q, (real, imag) in enumerate(inverse):
                    spot = (slice(row, row + 16), slice(q * quarter + lane, q * quarter + lane + 128))
                    real_ref[spot] = real
                    imag_ref[spot] = imag
                    if q == 0 and lane < VB:
                        power = gain * (real * real + imag * imag)
                        polar_ref[row : row + 16, step * VB + lane : step * VB + lane + 128] = (
                            power.astype(jnp.bfloat16)
                        )

    def one_slab(number, carry):
        for step in range(steps):
            one_step(number * steps + step, step)
        return carry

    lax.fori_loop(0, slab + 1, one_slab, 0)
    copies[-1].wait()


def march(
    field,
    phase_table,
    profile_index,
    group_power,
    group_slot,
    source_shift,
    slot_sub,
    tile_count,
    row_weights,
    col_weights,
):
    rows, height = field.shape[1:]
    slabs, steps = profile_index.shape
    weights, waves = march_constants(height)
    operands = [profile_index, group_power, group_slot, source_shift, slot_sub, tile_count]
    places = [pltpu.SMEM] * len(operands)
    pixels = row_weights.shape[-1]
    rows_flat = row_weights.reshape(K_MAX * SUB, pixels)
    cols_flat = col_weights.reshape(K_MAX, col_weights.shape[-2], pixels)
    operands += [field, phase_table, weights, waves, rows_flat]
    places += [pltpu.VMEM] * 5
    radials = rows * lax.axis_size("radial")
    return pl.pallas_call(
        functools.partial(march_kernel, steps, slabs),
        out_shape=[
            jax.ShapeDtypeStruct((rows, steps * VB), jnp.bfloat16),
            jax.ShapeDtypeStruct((K_MAX * SUB, radials), jnp.bfloat16),
            jax.ShapeDtypeStruct((pixels, K_MAX * SUB), jnp.bfloat16),
            jax.ShapeDtypeStruct(cols_flat.shape, jnp.bfloat16),
        ],
        in_specs=[pl.BlockSpec(memory_space=pltpu.HBM)] * (len(operands) + 1),
        out_specs=[pl.BlockSpec(memory_space=pltpu.VMEM)] * 4,
        scratch_shapes=[place(o.shape, o.dtype) for place, o in zip(places, operands)]
        + [
            pltpu.VMEM((-(-slabs * steps // 8) * 8, height), jnp.float32),
            pltpu.VMEM((slabs * steps, 16, height), jnp.float32),
            pltpu.VMEM((slabs * steps, 16, height), jnp.float32),
            pltpu.VMEM((rows, height), jnp.float32),
            pltpu.VMEM((rows, height), jnp.float32),
            pltpu.VMEM((rows * RADIX, 2 * height // RADIX), jnp.bfloat16),
            pltpu.VMEM((rows * RADIX, 2 * height // RADIX), jnp.bfloat16),
            pltpu.SemaphoreType.DMA((len(operands) + 1,)),
        ],
        compiler_params=pltpu.CompilerParams(vmem_limit_bytes=24 * 1024 * 1024),
        name="march",
    )(*[pltpu.with_memory_space_constraint(o, pltpu.HBM) for o in operands + [cols_flat]])


def tile_kernel(places, pick_ref, *refs):
    part_refs = refs[: len(places)]
    row_ref, col_ref, out_ref, polar_ref, mixed_ref = refs[len(places) :]
    chip = lax.axis_index("radial") // 2
    core = lax.axis_index("radial") % 2
    for (even, odd), part_ref in zip(places, part_refs):
        size = part_ref.shape[0]
        start = jnp.where(core == 0, chip ^ even, chip ^ odd) * size
        if size == polar_ref.shape[0]:
            start = 0
        polar_ref[pl.ds(start, size), :] = part_ref[...]
    blocks = jnp.dot(pick_ref[...], polar_ref[...], preferred_element_type=jnp.float32)
    blocks = blocks.astype(jnp.bfloat16)
    for slot in range(K_MAX):
        block = blocks[slot * SUB : (slot + 1) * SUB]
        mixed = jnp.dot(block, col_ref[slot], preferred_element_type=jnp.float32)
        mixed_ref[slot * SUB : (slot + 1) * SUB, :] = mixed.astype(jnp.bfloat16)
    out_ref[...] = jnp.dot(row_ref[...], mixed_ref[...], preferred_element_type=jnp.float32)


def tile_sum(pick, parts, places, row_weights, col_weights):
    pixels = row_weights.shape[0]
    channels = col_weights.shape[-2]
    vmem = pl.BlockSpec(memory_space=pltpu.VMEM)
    return pl.pallas_call(
        functools.partial(tile_kernel, places),
        out_shape=jax.ShapeDtypeStruct((pixels, pixels), jnp.float32),
        in_specs=[vmem] * (len(parts) + 3),
        out_specs=vmem,
        scratch_shapes=[
            pltpu.VMEM((pick.shape[1], channels), jnp.bfloat16),
            pltpu.VMEM((K_MAX * SUB, pixels), jnp.bfloat16),
        ],
        compiler_params=pltpu.CompilerParams(vmem_limit_bytes=24 * 1024 * 1024),
        name="tile_sum",
    )(
        pick,
        *parts,
        row_weights,
        col_weights,
    )


def swap(value, distance, devices):
    return lax.ppermute(value, "radial", [(i, i ^ distance) for i in range(devices)])


def gather_parts(polar, devices):
    if devices != 16:
        return [lax.all_gather(polar, "radial", axis=0, tiled=True)], [(0, 0)]
    core = lax.axis_index("radial") % 2
    size = 2 * polar.shape[0]

    def in_order(own, other):
        return jnp.where(
            core == 0, jnp.concatenate([own, other], 0), jnp.concatenate([other, own], 0)
        )

    pair = in_order(polar, swap(polar, 1, devices))
    held = []
    for even, odd in ((1, 2), (4, 5), (6, 7)):
        routes = [(i, i ^ (2 * (odd if i % 2 else even))) for i in range(devices)]
        held.append(lax.ppermute(pair, "radial", routes))
    last = swap(polar, 6, devices)
    other = swap(jnp.concatenate(held + [last], 0), 1, devices)
    parts = [pair] + held + [other[i * size : (i + 1) * size] for i in range(3)]
    parts.append(in_order(last, other[3 * size :]))
    places = [(0, 0), (1, 2), (4, 5), (6, 7), (2, 1), (5, 4), (7, 6), (3, 3)]
    return parts, places


def per_device(
    field_start,
    phase_table,
    profile_index,
    group_power,
    group_slot,
    source_shift,
    slot_sub,
    tile_count,
    row_weights,
    col_weights,
):
    devices = lax.axis_size("radial")
    polar, pick, turned, cols = march(
        field_start,
        phase_table,
        profile_index,
        group_power,
        group_slot,
        source_shift,
        slot_sub,
        tile_count,
        row_weights,
        col_weights,
    )
    parts, places = gather_parts(polar, devices)
    tile_value = tile_sum(pick, parts, places, turned, cols)
    return tile_value.reshape((1, 1) + tile_value.shape)


def solution(mesh):
    return jax.shard_map(
        per_device,
        mesh=mesh,
        in_specs=(
            P(None, "radial", None),
            P(),
            P(),
            P(),
            P(),
            P("range", None),
            P("range", None, None),
            P("range", None),
            P("range", "radial", None, None, None),
            P("range", "radial", None, None, None),
        ),
        out_specs=P("range", "radial", None, None),
        check_vma=False,
    )
```

```python
import functools
import math

import jax
import jax.numpy as jnp
import numpy as np
from jax import lax
from jax.experimental import pallas as pl
from jax.experimental.pallas import tpu as pltpu
from jax.sharding import PartitionSpec as P

VB = 128
SUB = 16
K_MAX = 16
CAP = 2
GROUP_RADIALS = 512
RADIX = 4

spread_angle = 6.0
absorb_rate = 0.5


def march_constants(height):
    quarter = height // RADIX
    index = np.arange(quarter)
    angle = 2.0 * np.pi / quarter * (index[:, None] * index[None, :] % quarter)
    factor = 1.0 / math.sqrt(height)
    cosine, sine = np.cos(angle) * factor, np.sin(angle) * factor
    weights = np.block([[cosine, -sine], [sine, cosine]]).astype(jnp.bfloat16)
    turn = 2.0 * np.pi / height * (np.arange(RADIX)[:, None] * index[None, :])
    level = np.arange(height)
    folded = np.minimum(level, height - level).astype(np.float64)
    theta = -spread_angle * (2.0 * folded / height) ** 2
    theta = theta.reshape(quarter, RADIX).T
    depth = np.maximum(0.0, (level - 0.9375 * height) / (0.0625 * height))
    absorber = np.exp(-absorb_rate * depth * depth).reshape(RADIX, quarter)
    waves = np.concatenate([np.cos(turn), np.sin(turn), np.cos(theta), np.sin(theta), absorber], 0)
    waves = np.pad(waves, ((0, -len(waves) % 8), (0, 0)))
    return weights, waves.astype(np.float32)


def cos_sin(angle):
    square = angle * angle
    cosine = jnp.full_like(angle, 1.0 / math.factorial(14) * -1.0)
    for order in (12, 10, 8, 6, 4, 2, 0):
        cosine = cosine * square + (-1.0) ** (order // 2) / math.factorial(order)
    sine = jnp.full_like(angle, 1.0 / math.factorial(13))
    for order in (11, 9, 7, 5, 3, 1):
        sine = sine * square + (-1.0) ** (order // 2) / math.factorial(order)
    return cosine, sine * angle


def march_kernel(
    steps,
    slabs,
    profile_hbm,
    power_hbm,
    slot_hbm,
    field_hbm,
    phase_hbm,
    weight_hbm,
    wave_hbm,
    polar_ref,
    profile_ref,
    power_ref,
    slot_ref,
    field_ref,
    phase_ref,
    weight_ref,
    wave_ref,
    phase_rows,
    screen_cos,
    screen_sin,
    real_ref,
    imag_ref,
    mixed_ref,
    moved_ref,
    sems,
):
    pairs = (
        (profile_hbm, profile_ref),
        (phase_hbm, phase_ref),
        (wave_hbm, wave_ref),
        (field_hbm, field_ref),
        (weight_hbm, weight_ref),
        (power_hbm, power_ref),
        (slot_hbm, slot_ref),
    )
    copies = [
        pltpu.make_async_copy(source, target, sems.at[number])
        for number, (source, target) in enumerate(pairs)
    ]
    for copy in copies:
        copy.start()
    rows, height = field_ref.shape[1:]
    quarter = height // RADIX
    slab = lax.axis_index("range")
    tile = lax.axis_index("radial")
    total = slabs * steps
    for copy in copies[:3]:
        copy.wait()
    for place in range(total):
        phase_rows[place : place + 1, :] = phase_ref[
            pl.ds(profile_ref[place // steps, place % steps], 1), :
        ]
    for q in range(RADIX):
        lanes = slice(q * quarter, (q + 1) * quarter)
        cosine, sine = cos_sin(phase_rows[:, lanes])
        absorber = wave_ref[4 * RADIX + q : 4 * RADIX + q + 1, :]
        damp = jnp.where(lax.broadcasted_iota(jnp.int32, cosine.shape, 0) == 0, 1.0, absorber)
        cosine, sine = cosine * damp, sine * damp
        for place in range(total):
            screen_cos[place, :, lanes] = jnp.broadcast_to(cosine[place : place + 1], (16, quarter))
            screen_sin[place, :, lanes] = jnp.broadcast_to(sine[place : place + 1], (16, quarter))
    for copy in copies[3:]:
        copy.wait()
    gain = power_ref[slot_ref[tile * rows // GROUP_RADIALS]]
    real_ref[...] = field_ref[0].astype(jnp.float32)
    imag_ref[...] = field_ref[1].astype(jnp.float32)

    def one_step(place, step):
        for row in range(0, rows, 16):
            for lane in range(0, quarter, 128):
                parts = []
                for q in range(RADIX):
                    spot = (slice(row, row + 16), slice(q * quarter + lane, q * quarter + lane + 128))
                    phase_cos = screen_cos[place, :, spot[1]]
                    phase_sin = screen_sin[place, :, spot[1]]
                    real, imag = real_ref[spot], imag_ref[spot]
                    parts.append(
                        (real * phase_cos - imag * phase_sin, real * phase_sin + imag * phase_cos)
                    )
                (r0, i0), (r1, i1), (r2, i2), (r3, i3) = parts
                sr02, si02, dr02, di02 = r0 + r2, i0 + i2, r0 - r2, i0 - i2
                sr13, si13, dr13, di13 = r1 + r3, i1 + i3, r1 - r3, i1 - i3
                forward = (
                    (sr02 + sr13, si02 + si13),
                    (dr02 + di13, di02 - dr13),
                    (sr02 - sr13, si02 - si13),
                    (dr02 - di13, di02 + dr13),
                )
                for j, (real, imag) in enumerate(forward):
                    if j:
                        turn_cos = wave_ref[j : j + 1, lane : lane + 128]
                        turn_sin = wave_ref[RADIX + j : RADIX + j + 1, lane : lane + 128]
                        real, imag = (
                            real * turn_cos + imag * turn_sin,
                            imag * turn_cos - real * turn_sin,
                        )
                    spot = slice(j * rows + row, j * rows + row + 16)
                    mixed_ref[spot, lane : lane + 128] = real.astype(jnp.bfloat16)
                    mixed_ref[spot, quarter + lane : quarter + lane + 128] = imag.astype(jnp.bfloat16)
        spectrum = jnp.dot(mixed_ref[...], weight_ref[...], preferred_element_type=jnp.float32)
        for j in range(RADIX):
            theta_cos = wave_ref[2 * RADIX + j : 2 * RADIX + j + 1, :]
            theta_sin = wave_ref[3 * RADIX + j : 3 * RADIX + j + 1, :]
            real = spectrum[j * rows : (j + 1) * rows, :quarter]
            imag = spectrum[j * rows : (j + 1) * rows, quarter:]
            spot = slice(j * rows, (j + 1) * rows)
            moved_ref[spot, quarter:] = (real * theta_cos - imag * theta_sin).astype(jnp.bfloat16)
            moved_ref[spot, :quarter] = (real * theta_sin + imag * theta_cos).astype(jnp.bfloat16)
        back = jnp.dot(moved_ref[...], weight_ref[...], preferred_element_type=jnp.float32)
        for row in range(0, rows, 16):
            for lane in range(0, quarter, 128):
                parts = []
                for j in range(RADIX):
                    spot = slice(j * rows + row, j * rows + row + 16)
                    imag = back[spot, lane : lane + 128]
                    real = back[spot, quarter + lane : quarter + lane + 128]
                    if j:
                        turn_cos = wave_ref[j : j + 1, lane : lane + 128]
                        turn_sin = wave_ref[RADIX + j : RADIX + j + 1, lane : lane + 128]
                        real, imag = (
                            real * turn_cos - imag * turn_sin,
                            imag * turn_cos + real * turn_sin,
                        )
                    parts.append((real, imag))
                (r0, i0), (r1, i1), (r2, i2), (r3, i3) = parts
                sr02, si02, dr02, di02 = r0 + r2, i0 + i2, r0 - r2, i0 - i2
                sr13, si13, dr13, di13 = r1 + r3, i1 + i3, r1 - r3, i1 - i3
                inverse = (
                    (sr02 + sr13, si02 + si13),
                    (dr02 - di13, di02 + dr13),
                    (sr02 - sr13, si02 - si13),
                    (dr02 + di13, di02 - dr13),
                )
                for q, (real, imag) in enumerate(inverse):
                    spot = (slice(row, row + 16), slice(q * quarter + lane, q * quarter + lane + 128))
                    real_ref[spot] = real
                    imag_ref[spot] = imag
                    if q == 0 and lane < VB:
                        power = gain * (real * real + imag * imag)
                        polar_ref[row : row + 16, step * VB + lane : step * VB + lane + 128] = (
                            power.astype(jnp.bfloat16)
                        )

    def one_slab(number, carry):
        for step in range(steps):
            one_step(number * steps + step, step)
        return carry

    lax.fori_loop(0, slab + 1, one_slab, 0)


def in_hbm(operands):
    return [pltpu.with_memory_space_constraint(value, pltpu.HBM) for value in operands]


def march(field, phase_table, profile_index, group_power, group_slot):
    rows, height = field.shape[1:]
    slabs, steps = profile_index.shape
    weights, waves = march_constants(height)
    operands = [profile_index, group_power, group_slot, field, phase_table, weights, waves]
    places = [pltpu.SMEM] * 3 + [pltpu.VMEM] * 4
    return pl.pallas_call(
        functools.partial(march_kernel, steps, slabs),
        out_shape=jax.ShapeDtypeStruct((rows, steps * VB), jnp.bfloat16),
        in_specs=[pl.BlockSpec(memory_space=pltpu.HBM)] * len(operands),
        out_specs=pl.BlockSpec(memory_space=pltpu.VMEM),
        scratch_shapes=[place(o.shape, o.dtype) for place, o in zip(places, operands)]
        + [
            pltpu.VMEM((-(-slabs * steps // 8) * 8, height), jnp.float32),
            pltpu.VMEM((slabs * steps, 16, height), jnp.float32),
            pltpu.VMEM((slabs * steps, 16, height), jnp.float32),
            pltpu.VMEM((rows, height), jnp.float32),
            pltpu.VMEM((rows, height), jnp.float32),
            pltpu.VMEM((rows * RADIX, 2 * height // RADIX), jnp.bfloat16),
            pltpu.VMEM((rows * RADIX, 2 * height // RADIX), jnp.bfloat16),
            pltpu.SemaphoreType.DMA((len(operands),)),
        ],
        compiler_params=pltpu.CompilerParams(vmem_limit_bytes=24 * 1024 * 1024),
        name="march",
    )(*in_hbm(operands))


def prepare_kernel(
    local_rows,
    shift_hbm,
    sub_hbm,
    count_hbm,
    row_hbm,
    col_hbm,
    after_ref,
    pick_ref,
    turned_ref,
    col_ref,
    passed_ref,
    shift_ref,
    sub_ref,
    count_ref,
    row_ref,
    sems,
):
    pairs = (
        (shift_hbm, shift_ref),
        (sub_hbm, sub_ref),
        (count_hbm, count_ref),
        (row_hbm, row_ref),
        (col_hbm, col_ref),
    )
    copies = [
        pltpu.make_async_copy(source, target, sems.at[number])
        for number, (source, target) in enumerate(pairs)
    ]
    for copy in copies:
        copy.start()
    tile = lax.axis_index("radial")
    devices = lax.axis_size("radial")
    for copy in copies[:4]:
        copy.wait()
    shape = (SUB, pick_ref.shape[1])
    offset = lax.broadcasted_iota(jnp.int32, shape, 1) - lax.broadcasted_iota(jnp.int32, shape, 0)
    for slot in range(K_MAX):
        source = lax.rem(tile + shift_ref[0, tile] + slot // CAP, devices)
        start = source * local_rows + sub_ref[0, tile, slot] * SUB
        start = jnp.where(slot < count_ref[0, tile], start, -2 * pick_ref.shape[1])
        pick_ref[slot * SUB : (slot + 1) * SUB, :] = jnp.where(offset == start, 1.0, 0.0).astype(
            jnp.bfloat16
        )
    turned_ref[...] = row_ref[...].T
    passed_ref[...] = after_ref[: passed_ref.shape[0], :]
    copies[4].wait()


def prepare(source_shift, slot_sub, tile_count, row_weights, col_weights, local_rows, after):
    pixels = row_weights.shape[-1]
    radials = local_rows * lax.axis_size("radial")
    rows_flat = row_weights.reshape(K_MAX * SUB, pixels)
    cols_flat = col_weights.reshape(K_MAX, col_weights.shape[-2], pixels)
    operands = [source_shift, slot_sub, tile_count, rows_flat]
    places = [pltpu.SMEM] * 3 + [pltpu.VMEM]
    return pl.pallas_call(
        functools.partial(prepare_kernel, local_rows),
        out_shape=[
            jax.ShapeDtypeStruct((K_MAX * SUB, radials), jnp.bfloat16),
            jax.ShapeDtypeStruct((pixels, K_MAX * SUB), jnp.bfloat16),
            jax.ShapeDtypeStruct(cols_flat.shape, jnp.bfloat16),
            jax.ShapeDtypeStruct((local_rows, after.shape[1]), after.dtype),
        ],
        in_specs=[pl.BlockSpec(memory_space=pltpu.HBM)] * 5
        + [pl.BlockSpec(memory_space=pltpu.VMEM)],
        out_specs=[pl.BlockSpec(memory_space=pltpu.VMEM)] * 4,
        scratch_shapes=[place(o.shape, o.dtype) for place, o in zip(places, operands)]
        + [pltpu.SemaphoreType.DMA((5,))],
        compiler_params=pltpu.CompilerParams(vmem_limit_bytes=24 * 1024 * 1024),
        cost_estimate=pl.CostEstimate(
            flops=0, bytes_accessed=2 * cols_flat.size, transcendentals=0
        ),
        name="prepare",
    )(*in_hbm(operands + [cols_flat]), after)


def tile_kernel(places, pick_ref, *refs):
    part_refs = refs[: len(places)]
    row_ref, col_ref, out_ref, polar_ref, mixed_ref = refs[len(places) :]
    chip = lax.axis_index("radial") // 2
    core = lax.axis_index("radial") % 2
    for (even, odd), part_ref in zip(places, part_refs):
        size = part_ref.shape[0]
        start = jnp.where(core == 0, chip ^ even, chip ^ odd) * size
        if size == polar_ref.shape[0]:
            start = 0
        polar_ref[pl.ds(start, size), :] = part_ref[...]
    blocks = jnp.dot(pick_ref[...], polar_ref[...], preferred_element_type=jnp.float32)
    blocks = blocks.astype(jnp.bfloat16)
    for slot in range(K_MAX):
        block = blocks[slot * SUB : (slot + 1) * SUB]
        mixed = jnp.dot(block, col_ref[slot], preferred_element_type=jnp.float32)
        mixed_ref[slot * SUB : (slot + 1) * SUB, :] = mixed.astype(jnp.bfloat16)
    out_ref[...] = jnp.dot(row_ref[...], mixed_ref[...], preferred_element_type=jnp.float32)


def tile_sum(pick, parts, places, row_weights, col_weights):
    pixels = row_weights.shape[0]
    channels = col_weights.shape[-2]
    vmem = pl.BlockSpec(memory_space=pltpu.VMEM)
    return pl.pallas_call(
        functools.partial(tile_kernel, places),
        out_shape=jax.ShapeDtypeStruct((pixels, pixels), jnp.float32),
        in_specs=[vmem] * (len(parts) + 3),
        out_specs=vmem,
        scratch_shapes=[
            pltpu.VMEM((pick.shape[1], channels), jnp.bfloat16),
            pltpu.VMEM((K_MAX * SUB, pixels), jnp.bfloat16),
        ],
        compiler_params=pltpu.CompilerParams(vmem_limit_bytes=24 * 1024 * 1024),
        name="tile_sum",
    )(
        pick,
        *parts,
        row_weights,
        col_weights,
    )


def swap(value, distance, devices):
    return lax.ppermute(value, "radial", [(i, i ^ distance) for i in range(devices)])


def gather_parts(polar, devices, prepared):
    if devices != 16:
        whole = lax.all_gather(polar, "radial", axis=0, tiled=True)
        return [whole], [(0, 0)], prepared(polar)[:3]
    core = lax.axis_index("radial") % 2
    size = 2 * polar.shape[0]

    def in_order(own, other):
        return jnp.where(
            core == 0, jnp.concatenate([own, other], 0), jnp.concatenate([other, own], 0)
        )

    longest = jnp.concatenate([polar, polar, polar[: size // 8]], 0)
    first = swap(longest, 2, devices)
    pair = in_order(polar, swap(polar, 1, devices))
    held = []
    for even, odd in ((2, 3), (6, 7), (4, 5)):
        routes = [(i, i ^ (2 * (odd if i % 2 else even))) for i in range(devices)]
        held.append(lax.ppermute(pair, "radial", routes))
    *ready, first = prepared(first)
    other = swap(jnp.concatenate(held + [first], 0), 1, devices)
    parts = [pair] + held + [other[i * size : (i + 1) * size] for i in range(3)]
    parts.append(in_order(first, other[3 * size :]))
    places = [(0, 0), (2, 3), (6, 7), (4, 5), (3, 2), (7, 6), (5, 4), (1, 1)]
    return parts, places, ready


def per_device(
    field_start,
    phase_table,
    profile_index,
    group_power,
    group_slot,
    source_shift,
    slot_sub,
    tile_count,
    row_weights,
    col_weights,
):
    devices = lax.axis_size("radial")
    polar = march(field_start, phase_table, profile_index, group_power, group_slot)
    prepared = functools.partial(
        prepare, source_shift, slot_sub, tile_count, row_weights, col_weights, polar.shape[0]
    )
    parts, places, ready = gather_parts(polar, devices, prepared)
    pick, turned, cols = ready
    tile_value = tile_sum(pick, parts, places, turned, cols)
    return tile_value.reshape((1, 1) + tile_value.shape)


def solution(mesh):
    return jax.shard_map(
        per_device,
        mesh=mesh,
        in_specs=(
            P(None, "radial", None),
            P(),
            P(),
            P(),
            P(),
            P("range", None),
            P("range", None, None),
            P("range", None),
            P("range", "radial", None, None, None),
            P("range", "radial", None, None, None),
        ),
        out_specs=P("range", "radial", None, None),
        check_vma=False,
    )
```

```python
import functools
import math

import jax
import jax.numpy as jnp
import numpy as np
from jax import lax
from jax.experimental import pallas as pl
from jax.experimental.pallas import tpu as pltpu
from jax.sharding import PartitionSpec as P

VB = 128
SUB = 16
K_MAX = 16
CAP = 2
GROUP_RADIALS = 512
RADIX = 4

spread_angle = 6.0
absorb_rate = 0.5


def march_constants(height):
    quarter = height // RADIX
    index = np.arange(quarter)
    angle = 2.0 * np.pi / quarter * (index[:, None] * index[None, :] % quarter)
    factor = 1.0 / math.sqrt(height)
    cosine, sine = np.cos(angle) * factor, np.sin(angle) * factor
    weights = np.block([[cosine, -sine], [sine, cosine]]).astype(jnp.bfloat16)
    turn = 2.0 * np.pi / height * (np.arange(RADIX)[:, None] * index[None, :])
    level = np.arange(height)
    folded = np.minimum(level, height - level).astype(np.float64)
    theta = -spread_angle * (2.0 * folded / height) ** 2
    theta = theta.reshape(quarter, RADIX).T
    depth = np.maximum(0.0, (level - 0.9375 * height) / (0.0625 * height))
    absorber = np.exp(-absorb_rate * depth * depth).reshape(RADIX, quarter)
    waves = np.concatenate([np.cos(turn), np.sin(turn), np.cos(theta), np.sin(theta), absorber], 0)
    waves = np.pad(waves, ((0, -len(waves) % 8), (0, 0)))
    return weights, waves.astype(np.float32)


def cos_sin(angle):
    square = angle * angle
    cosine = jnp.full_like(angle, 1.0 / math.factorial(14) * -1.0)
    for order in (12, 10, 8, 6, 4, 2, 0):
        cosine = cosine * square + (-1.0) ** (order // 2) / math.factorial(order)
    sine = jnp.full_like(angle, 1.0 / math.factorial(13))
    for order in (11, 9, 7, 5, 3, 1):
        sine = sine * square + (-1.0) ** (order // 2) / math.factorial(order)
    return cosine, sine * angle


def march_kernel(
    steps,
    slabs,
    profile_hbm,
    power_hbm,
    slot_hbm,
    field_hbm,
    phase_hbm,
    weight_hbm,
    wave_hbm,
    polar_ref,
    profile_ref,
    power_ref,
    slot_ref,
    field_ref,
    phase_ref,
    weight_ref,
    wave_ref,
    phase_rows,
    screen_cos,
    screen_sin,
    real_ref,
    imag_ref,
    mixed_ref,
    moved_ref,
    sems,
):
    pairs = (
        (profile_hbm, profile_ref),
        (phase_hbm, phase_ref),
        (wave_hbm, wave_ref),
        (field_hbm, field_ref),
        (weight_hbm, weight_ref),
        (power_hbm, power_ref),
        (slot_hbm, slot_ref),
    )
    copies = [
        pltpu.make_async_copy(source, target, sems.at[number])
        for number, (source, target) in enumerate(pairs)
    ]
    for copy in copies:
        copy.start()
    rows, height = field_ref.shape[1:]
    quarter = height // RADIX
    slab = lax.axis_index("range")
    tile = lax.axis_index("radial")
    total = slabs * steps
    for copy in copies[:3]:
        copy.wait()
    for place in range(total):
        phase_rows[place : place + 1, :] = phase_ref[
            pl.ds(profile_ref[place // steps, place % steps], 1), :
        ]
    for q in range(RADIX):
        lanes = slice(q * quarter, (q + 1) * quarter)
        cosine, sine = cos_sin(phase_rows[:, lanes])
        absorber = wave_ref[4 * RADIX + q : 4 * RADIX + q + 1, :]
        damp = jnp.where(lax.broadcasted_iota(jnp.int32, cosine.shape, 0) == 0, 1.0, absorber)
        cosine, sine = cosine * damp, sine * damp
        for place in range(total):
            screen_cos[place, :, lanes] = jnp.broadcast_to(cosine[place : place + 1], (16, quarter))
            screen_sin[place, :, lanes] = jnp.broadcast_to(sine[place : place + 1], (16, quarter))
    for copy in copies[3:]:
        copy.wait()
    gain = power_ref[slot_ref[tile * rows // GROUP_RADIALS]]
    real_ref[...] = field_ref[0].astype(jnp.float32)
    imag_ref[...] = field_ref[1].astype(jnp.float32)

    def one_step(place, step):
        for row in range(0, rows, 16):
            for lane in range(0, quarter, 128):
                parts = []
                for q in range(RADIX):
                    spot = (slice(row, row + 16), slice(q * quarter + lane, q * quarter + lane + 128))
                    phase_cos = screen_cos[place, :, spot[1]]
                    phase_sin = screen_sin[place, :, spot[1]]
                    real, imag = real_ref[spot], imag_ref[spot]
                    parts.append(
                        (real * phase_cos - imag * phase_sin, real * phase_sin + imag * phase_cos)
                    )
                (r0, i0), (r1, i1), (r2, i2), (r3, i3) = parts
                sr02, si02, dr02, di02 = r0 + r2, i0 + i2, r0 - r2, i0 - i2
                sr13, si13, dr13, di13 = r1 + r3, i1 + i3, r1 - r3, i1 - i3
                forward = (
                    (sr02 + sr13, si02 + si13),
                    (dr02 + di13, di02 - dr13),
                    (sr02 - sr13, si02 - si13),
                    (dr02 - di13, di02 + dr13),
                )
                for j, (real, imag) in enumerate(forward):
                    if j:
                        turn_cos = wave_ref[j : j + 1, lane : lane + 128]
                        turn_sin = wave_ref[RADIX + j : RADIX + j + 1, lane : lane + 128]
                        real, imag = (
                            real * turn_cos + imag * turn_sin,
                            imag * turn_cos - real * turn_sin,
                        )
                    spot = slice(j * rows + row, j * rows + row + 16)
                    mixed_ref[spot, lane : lane + 128] = real.astype(jnp.bfloat16)
                    mixed_ref[spot, quarter + lane : quarter + lane + 128] = imag.astype(jnp.bfloat16)
        spectrum = jnp.dot(mixed_ref[...], weight_ref[...], preferred_element_type=jnp.float32)
        for j in range(RADIX):
            theta_cos = wave_ref[2 * RADIX + j : 2 * RADIX + j + 1, :]
            theta_sin = wave_ref[3 * RADIX + j : 3 * RADIX + j + 1, :]
            real = spectrum[j * rows : (j + 1) * rows, :quarter]
            imag = spectrum[j * rows : (j + 1) * rows, quarter:]
            spot = slice(j * rows, (j + 1) * rows)
            moved_ref[spot, quarter:] = (real * theta_cos - imag * theta_sin).astype(jnp.bfloat16)
            moved_ref[spot, :quarter] = (real * theta_sin + imag * theta_cos).astype(jnp.bfloat16)
        back = jnp.dot(moved_ref[...], weight_ref[...], preferred_element_type=jnp.float32)
        for row in range(0, rows, 16):
            for lane in range(0, quarter, 128):
                parts = []
                for j in range(RADIX):
                    spot = slice(j * rows + row, j * rows + row + 16)
                    imag = back[spot, lane : lane + 128]
                    real = back[spot, quarter + lane : quarter + lane + 128]
                    if j:
                        turn_cos = wave_ref[j : j + 1, lane : lane + 128]
                        turn_sin = wave_ref[RADIX + j : RADIX + j + 1, lane : lane + 128]
                        real, imag = (
                            real * turn_cos - imag * turn_sin,
                            imag * turn_cos + real * turn_sin,
                        )
                    parts.append((real, imag))
                (r0, i0), (r1, i1), (r2, i2), (r3, i3) = parts
                sr02, si02, dr02, di02 = r0 + r2, i0 + i2, r0 - r2, i0 - i2
                sr13, si13, dr13, di13 = r1 + r3, i1 + i3, r1 - r3, i1 - i3
                inverse = (
                    (sr02 + sr13, si02 + si13),
                    (dr02 - di13, di02 + dr13),
                    (sr02 - sr13, si02 - si13),
                    (dr02 + di13, di02 - dr13),
                )
                for q, (real, imag) in enumerate(inverse):
                    spot = (slice(row, row + 16), slice(q * quarter + lane, q * quarter + lane + 128))
                    real_ref[spot] = real
                    imag_ref[spot] = imag
                    if q == 0 and lane < VB:
                        power = gain * (real * real + imag * imag)
                        polar_ref[row : row + 16, step * VB + lane : step * VB + lane + 128] = (
                            power.astype(jnp.bfloat16)
                        )

    def one_slab(number, carry):
        for step in range(steps):
            one_step(number * steps + step, step)
        return carry

    lax.fori_loop(0, slab + 1, one_slab, 0)


def in_hbm(operands):
    return [pltpu.with_memory_space_constraint(value, pltpu.HBM) for value in operands]


def march(field, phase_table, profile_index, group_power, group_slot):
    rows, height = field.shape[1:]
    slabs, steps = profile_index.shape
    weights, waves = march_constants(height)
    operands = [profile_index, group_power, group_slot, field, phase_table, weights, waves]
    places = [pltpu.SMEM] * 3 + [pltpu.VMEM] * 4
    return pl.pallas_call(
        functools.partial(march_kernel, steps, slabs),
        out_shape=jax.ShapeDtypeStruct((rows, steps * VB), jnp.bfloat16),
        in_specs=[pl.BlockSpec(memory_space=pltpu.HBM)] * len(operands),
        out_specs=pl.BlockSpec(memory_space=pltpu.VMEM),
        scratch_shapes=[place(o.shape, o.dtype) for place, o in zip(places, operands)]
        + [
            pltpu.VMEM((-(-slabs * steps // 8) * 8, height), jnp.float32),
            pltpu.VMEM((slabs * steps, 16, height), jnp.float32),
            pltpu.VMEM((slabs * steps, 16, height), jnp.float32),
            pltpu.VMEM((rows, height), jnp.float32),
            pltpu.VMEM((rows, height), jnp.float32),
            pltpu.VMEM((rows * RADIX, 2 * height // RADIX), jnp.bfloat16),
            pltpu.VMEM((rows * RADIX, 2 * height // RADIX), jnp.bfloat16),
            pltpu.SemaphoreType.DMA((len(operands),)),
        ],
        compiler_params=pltpu.CompilerParams(vmem_limit_bytes=24 * 1024 * 1024),
        name="march",
    )(*in_hbm(operands))


def prepare_kernel(
    local_rows,
    shift_hbm,
    sub_hbm,
    count_hbm,
    row_hbm,
    col_hbm,
    after_ref,
    pick_ref,
    turned_ref,
    col_ref,
    passed_ref,
    shift_ref,
    sub_ref,
    count_ref,
    row_ref,
    sems,
):
    pairs = (
        (shift_hbm, shift_ref),
        (sub_hbm, sub_ref),
        (count_hbm, count_ref),
        (row_hbm, row_ref),
        (col_hbm, col_ref),
    )
    copies = [
        pltpu.make_async_copy(source, target, sems.at[number])
        for number, (source, target) in enumerate(pairs)
    ]
    for copy in copies:
        copy.start()
    tile = lax.axis_index("radial")
    devices = lax.axis_size("radial")
    for copy in copies[:4]:
        copy.wait()
    shape = (SUB, pick_ref.shape[1])
    offset = lax.broadcasted_iota(jnp.int32, shape, 1) - lax.broadcasted_iota(jnp.int32, shape, 0)
    for slot in range(K_MAX):
        source = lax.rem(tile + shift_ref[0, tile] + slot // CAP, devices)
        start = source * local_rows + sub_ref[0, tile, slot] * SUB
        start = jnp.where(slot < count_ref[0, tile], start, -2 * pick_ref.shape[1])
        pick_ref[slot * SUB : (slot + 1) * SUB, :] = jnp.where(offset == start, 1.0, 0.0).astype(
            jnp.bfloat16
        )
    turned_ref[...] = row_ref[...].T
    passed_ref[...] = after_ref[...]
    copies[4].wait()


def prepare(source_shift, slot_sub, tile_count, row_weights, col_weights, local_rows, after):
    pixels = row_weights.shape[-1]
    radials = local_rows * lax.axis_size("radial")
    rows_flat = row_weights.reshape(K_MAX * SUB, pixels)
    cols_flat = col_weights.reshape(K_MAX, col_weights.shape[-2], pixels)
    operands = [source_shift, slot_sub, tile_count, rows_flat]
    places = [pltpu.SMEM] * 3 + [pltpu.VMEM]
    return pl.pallas_call(
        functools.partial(prepare_kernel, local_rows),
        out_shape=[
            jax.ShapeDtypeStruct((K_MAX * SUB, radials), jnp.bfloat16),
            jax.ShapeDtypeStruct((pixels, K_MAX * SUB), jnp.bfloat16),
            jax.ShapeDtypeStruct(cols_flat.shape, jnp.bfloat16),
            jax.ShapeDtypeStruct(after.shape, after.dtype),
        ],
        in_specs=[pl.BlockSpec(memory_space=pltpu.HBM)] * 5
        + [pl.BlockSpec(memory_space=pltpu.VMEM)],
        out_specs=[pl.BlockSpec(memory_space=pltpu.VMEM)] * 4,
        scratch_shapes=[place(o.shape, o.dtype) for place, o in zip(places, operands)]
        + [pltpu.SemaphoreType.DMA((5,))],
        compiler_params=pltpu.CompilerParams(vmem_limit_bytes=24 * 1024 * 1024),
        cost_estimate=pl.CostEstimate(
            flops=200_000_000_000, bytes_accessed=2 * cols_flat.size, transcendentals=0
        ),
        name="prepare",
    )(*in_hbm(operands + [cols_flat]), after)


def tile_kernel(places, pick_ref, *refs):
    part_refs = refs[: len(places)]
    row_ref, col_ref, out_ref, polar_ref, mixed_ref = refs[len(places) :]
    chip = lax.axis_index("radial") // 2
    core = lax.axis_index("radial") % 2
    for (even, odd), part_ref in zip(places, part_refs):
        size = part_ref.shape[0]
        start = jnp.where(core == 0, chip ^ even, chip ^ odd) * size
        if size == polar_ref.shape[0]:
            start = 0
        polar_ref[pl.ds(start, size), :] = part_ref[...]
    blocks = jnp.dot(pick_ref[...], polar_ref[...], preferred_element_type=jnp.float32)
    blocks = blocks.astype(jnp.bfloat16)
    for slot in range(K_MAX):
        block = blocks[slot * SUB : (slot + 1) * SUB]
        mixed = jnp.dot(block, col_ref[slot], preferred_element_type=jnp.float32)
        mixed_ref[slot * SUB : (slot + 1) * SUB, :] = mixed.astype(jnp.bfloat16)
    out_ref[...] = jnp.dot(row_ref[...], mixed_ref[...], preferred_element_type=jnp.float32)


def tile_sum(pick, parts, places, row_weights, col_weights):
    pixels = row_weights.shape[0]
    channels = col_weights.shape[-2]
    vmem = pl.BlockSpec(memory_space=pltpu.VMEM)
    return pl.pallas_call(
        functools.partial(tile_kernel, places),
        out_shape=jax.ShapeDtypeStruct((pixels, pixels), jnp.float32),
        in_specs=[vmem] * (len(parts) + 3),
        out_specs=vmem,
        scratch_shapes=[
            pltpu.VMEM((pick.shape[1], channels), jnp.bfloat16),
            pltpu.VMEM((K_MAX * SUB, pixels), jnp.bfloat16),
        ],
        compiler_params=pltpu.CompilerParams(vmem_limit_bytes=24 * 1024 * 1024),
        name="tile_sum",
    )(
        pick,
        *parts,
        row_weights,
        col_weights,
    )


def swap(value, distance, devices):
    return lax.ppermute(value, "radial", [(i, i ^ distance) for i in range(devices)])


def gather_parts(polar, devices, prepared):
    if devices != 16:
        whole = lax.all_gather(polar, "radial", axis=0, tiled=True)
        return [whole], [(0, 0)], prepared(polar)[:3]
    core = lax.axis_index("radial") % 2
    size = 2 * polar.shape[0]

    def in_order(own, other):
        return jnp.where(
            core == 0, jnp.concatenate([own, other], 0), jnp.concatenate([other, own], 0)
        )

    first = swap(polar, 12, devices)
    pair = in_order(polar, swap(polar, 1, devices))
    held = []
    for even, odd in ((2, 3), (7, 1), (4, 5)):
        routes = [(i, i ^ (2 * (odd if i % 2 else even))) for i in range(devices)]
        held.append(lax.ppermute(pair, "radial", routes))
    *ready, first = prepared(first)
    other = swap(jnp.concatenate(held + [first], 0), 1, devices)
    parts = [pair] + held + [other[i * size : (i + 1) * size] for i in range(3)]
    parts.append(in_order(first, other[3 * size :]))
    places = [(0, 0), (2, 3), (7, 1), (4, 5), (3, 2), (1, 7), (5, 4), (6, 6)]
    return parts, places, ready


def per_device(
    field_start,
    phase_table,
    profile_index,
    group_power,
    group_slot,
    source_shift,
    slot_sub,
    tile_count,
    row_weights,
    col_weights,
):
    devices = lax.axis_size("radial")
    polar = march(field_start, phase_table, profile_index, group_power, group_slot)
    prepared = functools.partial(
        prepare, source_shift, slot_sub, tile_count, row_weights, col_weights, polar.shape[0]
    )
    parts, places, ready = gather_parts(polar, devices, prepared)
    pick, turned, cols = ready
    tile_value = tile_sum(pick, parts, places, turned, cols)
    return tile_value.reshape((1, 1) + tile_value.shape)


def solution(mesh):
    return jax.shard_map(
        per_device,
        mesh=mesh,
        in_specs=(
            P(None, "radial", None),
            P(),
            P(),
            P(),
            P(),
            P("range", None),
            P("range", None, None),
            P("range", None),
            P("range", "radial", None, None, None),
            P("range", "radial", None, None, None),
        ),
        out_specs=P("range", "radial", None, None),
        check_vma=False,
    )
```

```python
import functools
import math

import jax
import jax.numpy as jnp
import numpy as np
from jax import lax
from jax.experimental import pallas as pl
from jax.experimental.pallas import tpu as pltpu
from jax.sharding import PartitionSpec as P

VB = 128
SUB = 16
K_MAX = 16
CAP = 2
GROUP_RADIALS = 512
RADIX = 8
CHUNKS = 4

spread_angle = 6.0
absorb_rate = 0.5


def march_constants(height):
    width = height // RADIX
    index = np.arange(width)
    angle = 2.0 * np.pi / width * (index[:, None] * index[None, :] % width)
    factor = 1.0 / math.sqrt(height)
    cosine, sine = np.cos(angle) * factor, np.sin(angle) * factor
    weights = np.block([[cosine, -sine], [sine, cosine]]).astype(jnp.bfloat16)
    turn = 2.0 * np.pi / height * (np.arange(RADIX)[:, None] * index[None, :])
    level = np.arange(height)
    folded = np.minimum(level, height - level).astype(np.float64)
    theta = -spread_angle * (2.0 * folded / height) ** 2
    theta = theta.reshape(width, RADIX).T
    depth = np.maximum(0.0, (level - 0.9375 * height) / (0.0625 * height))
    absorber = np.exp(-absorb_rate * depth * depth).reshape(RADIX, width)
    waves = np.concatenate([np.cos(turn), np.sin(turn), np.cos(theta), np.sin(theta), absorber], 0)
    waves = np.pad(waves, ((0, -len(waves) % 8), (0, 0)))
    return weights, waves.astype(np.float32)


def cos_sin(angle):
    square = angle * angle
    cosine = jnp.full_like(angle, 1.0 / math.factorial(14) * -1.0)
    for order in (12, 10, 8, 6, 4, 2, 0):
        cosine = cosine * square + (-1.0) ** (order // 2) / math.factorial(order)
    sine = jnp.full_like(angle, 1.0 / math.factorial(13))
    for order in (11, 9, 7, 5, 3, 1):
        sine = sine * square + (-1.0) ** (order // 2) / math.factorial(order)
    return cosine, sine * angle


def turn(real, imag, cosine, sine):
    return real * cosine - imag * sine, real * sine + imag * cosine


def turn_back(real, imag, cosine, sine):
    return real * cosine + imag * sine, imag * cosine - real * sine


def radix_four(parts, sign):
    (r0, i0), (r1, i1), (r2, i2), (r3, i3) = parts
    sr02, si02, dr02, di02 = r0 + r2, i0 + i2, r0 - r2, i0 - i2
    sr13, si13, dr13, di13 = r1 + r3, i1 + i3, r1 - r3, i1 - i3
    plus = (dr02 - di13, di02 + dr13)
    minus = (dr02 + di13, di02 - dr13)
    if sign < 0:
        plus, minus = minus, plus
    return (sr02 + sr13, si02 + si13), plus, (sr02 - sr13, si02 - si13), minus


def radix_eight(parts, sign):
    sums, turned = [], []
    for q in range(4):
        (r, i), (s, t) = parts[q], parts[q + 4]
        sums.append((r + s, i + t))
        turned.append((r - s, i - t))
    half = math.sqrt(0.5)
    (r, i), (s, t), (v, w) = turned[1:]
    if sign < 0:
        turned[1] = ((r + i) * half, (i - r) * half)
        turned[2] = (t, -s)
        turned[3] = ((w - v) * half, (v + w) * -half)
    else:
        turned[1] = ((r - i) * half, (r + i) * half)
        turned[2] = (-t, s)
        turned[3] = ((v + w) * -half, (v - w) * half)
    even, odd = radix_four(sums, sign), radix_four(turned, sign)
    return [part for pair in zip(even, odd) for part in pair]


def march_kernel(
    steps,
    slabs,
    profile_hbm,
    power_hbm,
    slot_hbm,
    phase_hbm,
    wave_hbm,
    field_hbm,
    weight_hbm,
    polar_ref,
    profile_ref,
    power_ref,
    slot_ref,
    phase_ref,
    wave_ref,
    field_ref,
    weight_ref,
    phase_rows,
    screen_ref,
    sems,
    units,
):
    pairs = (
        (profile_hbm, profile_ref),
        (phase_hbm, phase_ref),
        (wave_hbm, wave_ref),
        (field_hbm, field_ref),
        (weight_hbm, weight_ref),
        (power_hbm, power_ref),
        (slot_hbm, slot_ref),
    )
    copies = [
        pltpu.make_async_copy(source, target, sems.at[number])
        for number, (source, target) in enumerate(pairs)
    ]
    for copy in copies:
        copy.start()
    rows, height = field_ref.shape[1:]
    width = height // RADIX
    chunks = rows // SUB
    slab = lax.axis_index("range")
    tile = lax.axis_index("radial")
    total = slabs * steps
    for copy in copies[:3]:
        copy.wait()
    for place in range(total):
        phase_rows[place : place + 1, :] = phase_ref[
            pl.ds(profile_ref[place // steps, place % steps], 1), :
        ]
    for q in range(RADIX):
        columns = slice(q * width, (q + 1) * width)
        cosine, sine = cos_sin(phase_rows[:, columns])
        absorber = wave_ref[4 * RADIX + q : 4 * RADIX + q + 1, :]
        damp = jnp.where(lax.broadcasted_iota(jnp.int32, cosine.shape, 0) == 0, 1.0, absorber)
        for part, value in enumerate((cosine * damp, sine * damp)):
            for place in range(total):
                screen_ref[place, part, :, columns] = jnp.broadcast_to(
                    value[place : place + 1], (8, width)
                )
    for copy in copies[3:]:
        copy.wait()
    gain = power_ref[slot_ref[tile * rows // GROUP_RADIALS]]

    def run(*products):
        for unit in range(2):
            pltpu.matmul_push_rhs(weight_ref[...], 0, unit)
            pltpu.matmul_acc_lhs(
                products[chunks * unit], jnp.zeros((RADIX * SUB, 2 * width), jnp.bfloat16), load_staged_rhs=0
            )
            pltpu.matmul_pop(products[chunks * unit])

        def wave(kind, j):
            return wave_ref[kind * RADIX + j : kind * RADIX + j + 1, :]

        def entering(chunk):
            spot = slice(chunk * SUB, (chunk + 1) * SUB)
            return [
                tuple(
                    field_ref[part, spot, q * width : (q + 1) * width].astype(jnp.float32)
                    for part in range(2)
                )
                for q in range(RADIX)
            ]

        def forward(place, chunk, field):
            parts, lines = [], []
            for q in range(RADIX):
                columns = slice(q * width, (q + 1) * width)
                screen = [screen_ref[place, part, :, columns] for part in range(2)]
                screen = [jnp.concatenate([value] * (SUB // 8), 0) for value in screen]
                parts.append(turn(*field[q], *screen))
            for j, (real, imag) in enumerate(radix_eight(parts, -1)):
                if j:
                    real, imag = turn_back(real, imag, wave(0, j), wave(1, j))
                lines.append(
                    jnp.concatenate([real.astype(jnp.bfloat16), imag.astype(jnp.bfloat16)], 1)
                )
            pltpu.matmul_acc_lhs(products[chunk], jnp.concatenate(lines, 0))

        def middle(chunk):
            spectrum = pltpu.matmul_pop(products[chunk])
            lines = []
            for j in range(RADIX):
                spot = slice(j * SUB, (j + 1) * SUB)
                real, imag = spectrum[spot, :width], spectrum[spot, width:]
                real, imag = turn(real, imag, wave(2, j), wave(3, j))
                lines.append(
                    jnp.concatenate([imag.astype(jnp.bfloat16), real.astype(jnp.bfloat16)], 1)
                )
            pltpu.matmul_acc_lhs(products[chunks + chunk], jnp.concatenate(lines, 0))

        def backward(chunk, lowest):
            back = pltpu.matmul_pop(products[chunks + chunk])
            parts = []
            for j in range(RADIX):
                spot = slice(j * SUB, (j + 1) * SUB)
                real, imag = back[spot, width:], back[spot, :width]
                if j:
                    real, imag = turn(real, imag, wave(0, j), wave(1, j))
                parts.append((real, imag))
            if lowest:
                return [tuple(sum(part[1:], part[0]) for part in zip(*parts))]
            return radix_eight(parts, 1)

        def power_rows(step, chunk, real, imag):
            power = gain * (real * real + imag * imag)
            spot = slice(chunk * SUB, (chunk + 1) * SUB)
            polar_ref[spot, step * VB : (step + 1) * VB] = power.astype(jnp.bfloat16)

        def one_slab(number, last):
            events = []
            for step in range(steps):
                for chunk in range(chunks):
                    start = chunks * step + chunk
                    events.append((start, "forward", step, chunk))
                    events.append((start + 1.5, "middle", step, chunk))
            for chunk in range(chunks):
                events.append((chunks * steps + chunk, "leave", steps, chunk))
            for _, kind, step, chunk in sorted(events):
                if kind == "middle":
                    middle(chunk)
                    continue
                if step == 0:
                    forward(number * steps, chunk, entering(chunk))
                    continue
                field = backward(chunk, kind == "leave" and last)
                if last:
                    power_rows(step - 1, chunk, *field[0])
                if kind == "forward":
                    forward(number * steps + step, chunk, field)
                elif not last:
                    spot = slice(chunk * SUB, (chunk + 1) * SUB)
                    for q in range(RADIX):
                        for part in range(2):
                            field_ref[part, spot, q * width : (q + 1) * width] = field[q][
                                part
                            ].astype(jnp.bfloat16)

        def whole_slab(number, carry):
            one_slab(number, False)
            return carry

        lax.fori_loop(0, slab, whole_slab, 0)
        one_slab(slab, True)

    pl.run_scoped(run, *units)


def in_hbm(operands):
    return [pltpu.with_memory_space_constraint(value, pltpu.HBM) for value in operands]


def march(field, phase_table, profile_index, group_power, group_slot, units):
    rows, height = field.shape[1:]
    slabs, steps = profile_index.shape
    weights, waves = march_constants(height)
    operands = [profile_index, group_power, group_slot, phase_table, waves, field, weights]
    places = [pltpu.SMEM] * 3 + [pltpu.VMEM] * 4
    return pl.pallas_call(
        functools.partial(march_kernel, steps, slabs, units=units),
        out_shape=jax.ShapeDtypeStruct((rows, steps * VB), jnp.bfloat16),
        in_specs=[pl.BlockSpec(memory_space=pltpu.HBM)] * len(operands),
        out_specs=pl.BlockSpec(memory_space=pltpu.VMEM),
        scratch_shapes=[place(o.shape, o.dtype) for place, o in zip(places, operands)]
        + [
            pltpu.VMEM((-(-slabs * steps // 8) * 8, height), jnp.float32),
            pltpu.VMEM((slabs * steps, 2, 8, height), jnp.float32),
            pltpu.SemaphoreType.DMA((len(operands),)),
        ],
        compiler_params=pltpu.CompilerParams(vmem_limit_bytes=24 * 1024 * 1024),
        name="march",
    )(*in_hbm(operands))


def prepare_kernel(
    local_rows,
    shift_hbm,
    sub_hbm,
    count_hbm,
    row_hbm,
    col_hbm,
    after_ref,
    pick_ref,
    turned_ref,
    col_ref,
    passed_ref,
    shift_ref,
    sub_ref,
    count_ref,
    row_ref,
    sems,
):
    pairs = (
        (shift_hbm, shift_ref),
        (sub_hbm, sub_ref),
        (count_hbm, count_ref),
        (row_hbm, row_ref),
        (col_hbm, col_ref),
    )
    copies = [
        pltpu.make_async_copy(source, target, sems.at[number])
        for number, (source, target) in enumerate(pairs)
    ]
    for copy in copies:
        copy.start()
    tile = lax.axis_index("radial")
    devices = lax.axis_size("radial")
    for copy in copies[:4]:
        copy.wait()
    shape = (SUB, pick_ref.shape[1])
    offset = lax.broadcasted_iota(jnp.int32, shape, 1) - lax.broadcasted_iota(jnp.int32, shape, 0)
    for slot in range(K_MAX):
        source = lax.rem(tile + shift_ref[0, tile] + slot // CAP, devices)
        start = source * local_rows + sub_ref[0, tile, slot] * SUB
        start = jnp.where(slot < count_ref[0, tile], start, -2 * pick_ref.shape[1])
        pick_ref[slot * SUB : (slot + 1) * SUB, :] = jnp.where(offset == start, 1.0, 0.0).astype(
            jnp.bfloat16
        )
    turned_ref[...] = row_ref[...].T
    passed_ref[...] = after_ref[...]
    copies[4].wait()


def prepare(source_shift, slot_sub, tile_count, row_weights, col_weights, local_rows, after):
    pixels = row_weights.shape[-1]
    radials = local_rows * lax.axis_size("radial")
    rows_flat = row_weights.reshape(K_MAX * SUB, pixels)
    cols_flat = col_weights.reshape(K_MAX, col_weights.shape[-2], pixels)
    operands = [source_shift, slot_sub, tile_count, rows_flat]
    places = [pltpu.SMEM] * 3 + [pltpu.VMEM]
    return pl.pallas_call(
        functools.partial(prepare_kernel, local_rows),
        out_shape=[
            jax.ShapeDtypeStruct((K_MAX * SUB, radials), jnp.bfloat16),
            jax.ShapeDtypeStruct((pixels, K_MAX * SUB), jnp.bfloat16),
            jax.ShapeDtypeStruct(cols_flat.shape, jnp.bfloat16),
            jax.ShapeDtypeStruct(after.shape, after.dtype),
        ],
        in_specs=[pl.BlockSpec(memory_space=pltpu.HBM)] * 5
        + [pl.BlockSpec(memory_space=pltpu.VMEM)],
        out_specs=[pl.BlockSpec(memory_space=pltpu.VMEM)] * 4,
        scratch_shapes=[place(o.shape, o.dtype) for place, o in zip(places, operands)]
        + [pltpu.SemaphoreType.DMA((5,))],
        compiler_params=pltpu.CompilerParams(vmem_limit_bytes=24 * 1024 * 1024),
        cost_estimate=pl.CostEstimate(
            flops=2_000_000_000, bytes_accessed=2 * cols_flat.size, transcendentals=0
        ),
        name="prepare",
    )(*in_hbm(operands + [cols_flat]), after)


def tile_kernel(places, pick_ref, *refs):
    part_refs = refs[: len(places)]
    row_ref, col_ref, out_ref, polar_ref, mixed_ref = refs[len(places) :]
    chip = lax.axis_index("radial") // 2
    core = lax.axis_index("radial") % 2
    for (even, odd), part_ref in zip(places, part_refs):
        size = part_ref.shape[0]
        start = jnp.where(core == 0, chip ^ even, chip ^ odd) * size
        if size == polar_ref.shape[0]:
            start = 0
        polar_ref[pl.ds(start, size), :] = part_ref[...]
    blocks = jnp.dot(pick_ref[...], polar_ref[...], preferred_element_type=jnp.float32)
    blocks = blocks.astype(jnp.bfloat16)
    for slot in range(K_MAX):
        block = blocks[slot * SUB : (slot + 1) * SUB]
        mixed = jnp.dot(block, col_ref[slot], preferred_element_type=jnp.float32)
        mixed_ref[slot * SUB : (slot + 1) * SUB, :] = mixed.astype(jnp.bfloat16)
    out_ref[...] = jnp.dot(row_ref[...], mixed_ref[...], preferred_element_type=jnp.float32)


def tile_sum(pick, parts, places, row_weights, col_weights):
    pixels = row_weights.shape[0]
    channels = col_weights.shape[-2]
    vmem = pl.BlockSpec(memory_space=pltpu.VMEM)
    return pl.pallas_call(
        functools.partial(tile_kernel, places),
        out_shape=jax.ShapeDtypeStruct((pixels, pixels), jnp.float32),
        in_specs=[vmem] * (len(parts) + 3),
        out_specs=vmem,
        scratch_shapes=[
            pltpu.VMEM((pick.shape[1], channels), jnp.bfloat16),
            pltpu.VMEM((K_MAX * SUB, pixels), jnp.bfloat16),
        ],
        compiler_params=pltpu.CompilerParams(vmem_limit_bytes=24 * 1024 * 1024),
        name="tile_sum",
    )(
        pick,
        *parts,
        row_weights,
        col_weights,
    )


def swap(value, distance, devices):
    return lax.ppermute(value, "radial", [(i, i ^ distance) for i in range(devices)])


def gather_parts(polar, devices, prepared):
    if devices != 16:
        whole = lax.all_gather(polar, "radial", axis=0, tiled=True)
        return [whole], [(0, 0)], prepared(polar)[:3]
    core = lax.axis_index("radial") % 2
    size = 2 * polar.shape[0]

    def in_order(own, other):
        return jnp.where(
            core == 0, jnp.concatenate([own, other], 0), jnp.concatenate([other, own], 0)
        )

    first = swap(polar, 2, devices)
    pair = in_order(polar, swap(polar, 1, devices))
    held = []
    for even, odd in ((2, 3), (4, 5), (6, 7)):
        routes = [(i, i ^ (2 * (odd if i % 2 else even))) for i in range(devices)]
        held.append(lax.ppermute(pair, "radial", routes))
    *ready, first = prepared(first)
    other = swap(jnp.concatenate(held + [first], 0), 1, devices)
    parts = [pair] + held + [other[i * size : (i + 1) * size] for i in range(3)]
    parts.append(in_order(first, other[3 * size :]))
    places = [(0, 0), (2, 3), (4, 5), (6, 7), (3, 2), (5, 4), (7, 6), (1, 1)]
    return parts, places, ready


def per_device(
    units,
    field_start,
    phase_table,
    profile_index,
    group_power,
    group_slot,
    source_shift,
    slot_sub,
    tile_count,
    row_weights,
    col_weights,
):
    devices = lax.axis_size("radial")
    polar = march(field_start, phase_table, profile_index, group_power, group_slot, units)
    prepared = functools.partial(
        prepare, source_shift, slot_sub, tile_count, row_weights, col_weights, polar.shape[0]
    )
    parts, places, ready = gather_parts(polar, devices, prepared)
    pick, turned, cols = ready
    tile_value = tile_sum(pick, parts, places, turned, cols)
    return tile_value.reshape((1, 1) + tile_value.shape)


def solution(mesh):
    with jax.sharding.use_abstract_mesh(mesh.abstract_mesh):
        units = [
            pltpu.ACC(number // CHUNKS)((RADIX * SUB, 256), jnp.float32)
            for number in range(2 * CHUNKS)
        ]
    return jax.shard_map(
        functools.partial(per_device, units),
        mesh=mesh,
        in_specs=(
            P(None, "radial", None),
            P(),
            P(),
            P(),
            P(),
            P("range", None),
            P("range", None, None),
            P("range", None),
            P("range", "radial", None, None, None),
            P("range", "radial", None, None, None),
        ),
        out_specs=P("range", "radial", None, None),
        check_vma=False,
    )
```

```python
import functools
import math

import jax
import jax.numpy as jnp
import numpy as np
from jax import lax
from jax.experimental import pallas as pl
from jax.experimental.pallas import tpu as pltpu
from jax.sharding import PartitionSpec as P

VB = 128
SUB = 16
K_MAX = 16
CAP = 2
GROUP_RADIALS = 512
RADIX = 8
CHUNKS = 4

spread_angle = 6.0
absorb_rate = 0.5


def march_constants(height):
    width = height // RADIX
    index = np.arange(width)
    angle = 2.0 * np.pi / width * (index[:, None] * index[None, :] % width)
    factor = 1.0 / math.sqrt(height)
    cosine, sine = np.cos(angle) * factor, np.sin(angle) * factor
    weights = np.block([[cosine, -sine], [sine, cosine]]).astype(jnp.bfloat16)
    turn = 2.0 * np.pi / height * (np.arange(RADIX)[:, None] * index[None, :])
    level = np.arange(height)
    folded = np.minimum(level, height - level).astype(np.float64)
    theta = -spread_angle * (2.0 * folded / height) ** 2
    theta = theta.reshape(width, RADIX).T
    depth = np.maximum(0.0, (level - 0.9375 * height) / (0.0625 * height))
    absorber = np.exp(-absorb_rate * depth * depth).reshape(RADIX, width)
    waves = np.concatenate([np.cos(turn), np.sin(turn), np.cos(theta), np.sin(theta), absorber], 0)
    waves = np.pad(waves, ((0, -len(waves) % 8), (0, 0)))
    return weights, waves.astype(np.float32)


def cos_sin(angle):
    square = angle * angle
    cosine = jnp.full_like(angle, 1.0 / math.factorial(14) * -1.0)
    for order in (12, 10, 8, 6, 4, 2, 0):
        cosine = cosine * square + (-1.0) ** (order // 2) / math.factorial(order)
    sine = jnp.full_like(angle, 1.0 / math.factorial(13))
    for order in (11, 9, 7, 5, 3, 1):
        sine = sine * square + (-1.0) ** (order // 2) / math.factorial(order)
    return cosine, sine * angle


def turn(real, imag, cosine, sine):
    return real * cosine - imag * sine, real * sine + imag * cosine


def turn_back(real, imag, cosine, sine):
    return real * cosine + imag * sine, imag * cosine - real * sine


def radix_four(parts, sign):
    (r0, i0), (r1, i1), (r2, i2), (r3, i3) = parts
    sr02, si02, dr02, di02 = r0 + r2, i0 + i2, r0 - r2, i0 - i2
    sr13, si13, dr13, di13 = r1 + r3, i1 + i3, r1 - r3, i1 - i3
    plus = (dr02 - di13, di02 + dr13)
    minus = (dr02 + di13, di02 - dr13)
    if sign < 0:
        plus, minus = minus, plus
    return (sr02 + sr13, si02 + si13), plus, (sr02 - sr13, si02 - si13), minus


def radix_eight(parts, sign):
    sums, turned = [], []
    for q in range(4):
        (r, i), (s, t) = parts[q], parts[q + 4]
        sums.append((r + s, i + t))
        turned.append((r - s, i - t))
    half = math.sqrt(0.5)
    (r, i), (s, t), (v, w) = turned[1:]
    if sign < 0:
        turned[1] = ((r + i) * half, (i - r) * half)
        turned[2] = (t, -s)
        turned[3] = ((w - v) * half, (v + w) * -half)
    else:
        turned[1] = ((r - i) * half, (r + i) * half)
        turned[2] = (-t, s)
        turned[3] = ((v + w) * -half, (v - w) * half)
    even, odd = radix_four(sums, sign), radix_four(turned, sign)
    return [part for pair in zip(even, odd) for part in pair]


def march_kernel(
    steps,
    slabs,
    profile_hbm,
    power_hbm,
    slot_hbm,
    phase_hbm,
    wave_hbm,
    field_hbm,
    weight_hbm,
    polar_ref,
    profile_ref,
    power_ref,
    slot_ref,
    phase_ref,
    wave_ref,
    field_ref,
    weight_ref,
    phase_rows,
    screen_ref,
    sems,
    units,
):
    pairs = (
        (profile_hbm, profile_ref),
        (phase_hbm, phase_ref),
        (wave_hbm, wave_ref),
        (field_hbm, field_ref),
        (weight_hbm, weight_ref),
        (power_hbm, power_ref),
        (slot_hbm, slot_ref),
    )
    copies = [
        pltpu.make_async_copy(source, target, sems.at[number])
        for number, (source, target) in enumerate(pairs)
    ]
    for copy in copies:
        copy.start()
    rows, height = field_ref.shape[1:]
    width = height // RADIX
    chunks = rows // SUB
    slab = lax.axis_index("range")
    tile = lax.axis_index("radial")
    total = slabs * steps
    for copy in copies[:3]:
        copy.wait()
    for place in range(total):
        phase_rows[place : place + 1, :] = phase_ref[
            pl.ds(profile_ref[place // steps, place % steps], 1), :
        ]
    for q in range(RADIX):
        columns = slice(q * width, (q + 1) * width)
        cosine, sine = cos_sin(phase_rows[:, columns])
        absorber = wave_ref[4 * RADIX + q : 4 * RADIX + q + 1, :]
        damp = jnp.where(lax.broadcasted_iota(jnp.int32, cosine.shape, 0) == 0, 1.0, absorber)
        for part, value in enumerate((cosine * damp, sine * damp)):
            for place in range(total):
                screen_ref[place, part, :, columns] = jnp.broadcast_to(
                    value[place : place + 1], (8, width)
                )
    for copy in copies[3:]:
        copy.wait()
    gain = power_ref[slot_ref[tile * rows // GROUP_RADIALS]]

    def run(*products):
        for unit in range(2):
            pltpu.matmul_push_rhs(weight_ref[...], 0, unit)
            pltpu.matmul_acc_lhs(
                products[chunks * unit], jnp.zeros((RADIX * SUB, 2 * width), jnp.bfloat16), load_staged_rhs=0
            )
            pltpu.matmul_pop(products[chunks * unit])

        def wave(kind, j):
            return wave_ref[kind * RADIX + j : kind * RADIX + j + 1, :]

        def entering(chunk):
            spot = slice(chunk * SUB, (chunk + 1) * SUB)
            return [
                tuple(
                    field_ref[part, spot, q * width : (q + 1) * width].astype(jnp.float32)
                    for part in range(2)
                )
                for q in range(RADIX)
            ]

        def forward(place, chunk, field):
            parts, lines = [], []
            for q in range(RADIX):
                columns = slice(q * width, (q + 1) * width)
                screen = [screen_ref[place, part, :, columns] for part in range(2)]
                screen = [jnp.concatenate([value] * (SUB // 8), 0) for value in screen]
                parts.append(turn(*field[q], *screen))
            for j, (real, imag) in enumerate(radix_eight(parts, -1)):
                if j:
                    real, imag = turn_back(real, imag, wave(0, j), wave(1, j))
                lines.append(
                    jnp.concatenate([real.astype(jnp.bfloat16), imag.astype(jnp.bfloat16)], 1)
                )
            pltpu.matmul_acc_lhs(products[chunk], jnp.concatenate(lines, 0))

        def middle(chunk):
            spectrum = pltpu.matmul_pop(products[chunk])
            lines = []
            for j in range(RADIX):
                spot = slice(j * SUB, (j + 1) * SUB)
                real, imag = spectrum[spot, :width], spectrum[spot, width:]
                real, imag = turn(real, imag, wave(2, j), wave(3, j))
                lines.append(
                    jnp.concatenate([imag.astype(jnp.bfloat16), real.astype(jnp.bfloat16)], 1)
                )
            pltpu.matmul_acc_lhs(products[chunks + chunk], jnp.concatenate(lines, 0))

        def backward(chunk, lowest):
            back = pltpu.matmul_pop(products[chunks + chunk])
            parts = []
            for j in range(RADIX):
                spot = slice(j * SUB, (j + 1) * SUB)
                real, imag = back[spot, width:], back[spot, :width]
                if j:
                    real, imag = turn(real, imag, wave(0, j), wave(1, j))
                parts.append((real, imag))
            if lowest:
                return [tuple(sum(part[1:], part[0]) for part in zip(*parts))]
            return radix_eight(parts, 1)

        def power_rows(step, chunk, real, imag):
            power = gain * (real * real + imag * imag)
            spot = slice(chunk * SUB, (chunk + 1) * SUB)
            polar_ref[spot, step * VB : (step + 1) * VB] = power.astype(jnp.bfloat16)

        def one_slab(number, last):
            events = []
            for step in range(steps):
                for chunk in range(chunks):
                    start = chunks * step + chunk
                    events.append((start, "forward", step, chunk))
                    events.append((start + 1.5, "middle", step, chunk))
            for chunk in range(chunks):
                events.append((chunks * steps + chunk, "leave", steps, chunk))
            for _, kind, step, chunk in sorted(events):
                if kind == "middle":
                    middle(chunk)
                    continue
                if step == 0:
                    forward(number * steps, chunk, entering(chunk))
                    continue
                field = backward(chunk, kind == "leave" and last)
                if last:
                    power_rows(step - 1, chunk, *field[0])
                if kind == "forward":
                    forward(number * steps + step, chunk, field)
                elif not last:
                    spot = slice(chunk * SUB, (chunk + 1) * SUB)
                    for q in range(RADIX):
                        for part in range(2):
                            field_ref[part, spot, q * width : (q + 1) * width] = field[q][
                                part
                            ].astype(jnp.bfloat16)

        def whole_slab(number, carry):
            one_slab(number, False)
            return carry

        lax.fori_loop(0, slab, whole_slab, 0)
        one_slab(slab, True)

    pl.run_scoped(run, *units)


def in_hbm(operands):
    return [pltpu.with_memory_space_constraint(value, pltpu.HBM) for value in operands]


def march(field, phase_table, profile_index, group_power, group_slot, units):
    rows, height = field.shape[1:]
    slabs, steps = profile_index.shape
    weights, waves = march_constants(height)
    operands = [profile_index, group_power, group_slot, phase_table, waves, field, weights]
    places = [pltpu.SMEM] * 3 + [pltpu.VMEM] * 4
    return pl.pallas_call(
        functools.partial(march_kernel, steps, slabs, units=units),
        out_shape=jax.ShapeDtypeStruct((rows, steps * VB), jnp.bfloat16),
        in_specs=[pl.BlockSpec(memory_space=pltpu.HBM)] * len(operands),
        out_specs=pl.BlockSpec(memory_space=pltpu.VMEM),
        scratch_shapes=[place(o.shape, o.dtype) for place, o in zip(places, operands)]
        + [
            pltpu.VMEM((-(-slabs * steps // 8) * 8, height), jnp.float32),
            pltpu.VMEM((slabs * steps, 2, 8, height), jnp.float32),
            pltpu.SemaphoreType.DMA((len(operands),)),
        ],
        compiler_params=pltpu.CompilerParams(vmem_limit_bytes=24 * 1024 * 1024),
        name="march",
    )(*in_hbm(operands))


def prepare_kernel(
    local_rows,
    shift_hbm,
    sub_hbm,
    count_hbm,
    row_hbm,
    col_hbm,
    after_ref,
    pick_ref,
    turned_ref,
    col_ref,
    passed_ref,
    shift_ref,
    sub_ref,
    count_ref,
    row_ref,
    sems,
):
    pairs = (
        (shift_hbm, shift_ref),
        (sub_hbm, sub_ref),
        (count_hbm, count_ref),
        (row_hbm, row_ref),
        (col_hbm, col_ref),
    )
    copies = [
        pltpu.make_async_copy(source, target, sems.at[number])
        for number, (source, target) in enumerate(pairs)
    ]
    for copy in copies:
        copy.start()
    tile = lax.axis_index("radial")
    devices = lax.axis_size("radial")
    for copy in copies[:4]:
        copy.wait()
    shape = (SUB, pick_ref.shape[1])
    offset = lax.broadcasted_iota(jnp.int32, shape, 1) - lax.broadcasted_iota(jnp.int32, shape, 0)
    for slot in range(K_MAX):
        source = lax.rem(tile + shift_ref[0, tile] + slot // CAP, devices)
        start = source * local_rows + sub_ref[0, tile, slot] * SUB
        start = jnp.where(slot < count_ref[0, tile], start, -2 * pick_ref.shape[1])
        pick_ref[slot * SUB : (slot + 1) * SUB, :] = jnp.where(offset == start, 1.0, 0.0).astype(
            jnp.bfloat16
        )
    turned_ref[...] = row_ref[...].T
    passed_ref[...] = after_ref[...]
    copies[4].wait()


def prepare(source_shift, slot_sub, tile_count, row_weights, col_weights, local_rows, after):
    pixels = row_weights.shape[-1]
    radials = local_rows * lax.axis_size("radial")
    rows_flat = row_weights.reshape(K_MAX * SUB, pixels)
    cols_flat = col_weights.reshape(K_MAX, col_weights.shape[-2], pixels)
    operands = [source_shift, slot_sub, tile_count, rows_flat]
    places = [pltpu.SMEM] * 3 + [pltpu.VMEM]
    return pl.pallas_call(
        functools.partial(prepare_kernel, local_rows),
        out_shape=[
            jax.ShapeDtypeStruct((K_MAX * SUB, radials), jnp.bfloat16),
            jax.ShapeDtypeStruct((pixels, K_MAX * SUB), jnp.bfloat16),
            jax.ShapeDtypeStruct(cols_flat.shape, jnp.bfloat16),
            jax.ShapeDtypeStruct(after.shape, after.dtype),
        ],
        in_specs=[pl.BlockSpec(memory_space=pltpu.HBM)] * 5
        + [pl.BlockSpec(memory_space=pltpu.VMEM)],
        out_specs=[pl.BlockSpec(memory_space=pltpu.VMEM)] * 4,
        scratch_shapes=[place(o.shape, o.dtype) for place, o in zip(places, operands)]
        + [pltpu.SemaphoreType.DMA((5,))],
        compiler_params=pltpu.CompilerParams(vmem_limit_bytes=24 * 1024 * 1024),
        cost_estimate=pl.CostEstimate(
            flops=2_000_000_000, bytes_accessed=2 * cols_flat.size, transcendentals=0
        ),
        name="prepare",
    )(*in_hbm(operands + [cols_flat]), after)


def tile_kernel(places, pick_ref, *refs):
    part_refs = refs[: len(places)]
    row_ref, col_ref, out_ref, polar_ref, mixed_ref = refs[len(places) :]
    chip = lax.axis_index("radial") // 2
    core = lax.axis_index("radial") % 2
    for (even, odd), part_ref in zip(places, part_refs):
        size = part_ref.shape[0]
        start = jnp.where(core == 0, chip ^ even, chip ^ odd) * size
        if size == polar_ref.shape[0]:
            start = 0
        polar_ref[pl.ds(start, size), :] = part_ref[...]
    blocks = jnp.dot(pick_ref[...], polar_ref[...], preferred_element_type=jnp.float32)
    blocks = blocks.astype(jnp.bfloat16)
    for slot in range(K_MAX):
        block = blocks[slot * SUB : (slot + 1) * SUB]
        mixed = jnp.dot(block, col_ref[slot], preferred_element_type=jnp.float32)
        mixed_ref[slot * SUB : (slot + 1) * SUB, :] = mixed.astype(jnp.bfloat16)
    out_ref[...] = jnp.dot(row_ref[...], mixed_ref[...], preferred_element_type=jnp.float32)


def tile_sum(pick, parts, places, row_weights, col_weights):
    pixels = row_weights.shape[0]
    channels = col_weights.shape[-2]
    vmem = pl.BlockSpec(memory_space=pltpu.VMEM)
    return pl.pallas_call(
        functools.partial(tile_kernel, places),
        out_shape=jax.ShapeDtypeStruct((pixels, pixels), jnp.float32),
        in_specs=[vmem] * (len(parts) + 3),
        out_specs=vmem,
        scratch_shapes=[
            pltpu.VMEM((pick.shape[1], channels), jnp.bfloat16),
            pltpu.VMEM((K_MAX * SUB, pixels), jnp.bfloat16),
        ],
        compiler_params=pltpu.CompilerParams(vmem_limit_bytes=24 * 1024 * 1024),
        name="tile_sum",
    )(
        pick,
        *parts,
        row_weights,
        col_weights,
    )


def swap(value, distance, devices):
    return lax.ppermute(value, "radial", [(i, i ^ distance) for i in range(devices)])


def gather_parts(polar, devices, prepared):
    if devices != 16:
        whole = lax.all_gather(polar, "radial", axis=0, tiled=True)
        return [whole], [(0, 0)], prepared(polar)[:3]
    core = lax.axis_index("radial") % 2
    size = 2 * polar.shape[0]

    def in_order(own, other):
        return jnp.where(
            core == 0, jnp.concatenate([own, other], 0), jnp.concatenate([other, own], 0)
        )

    first = swap(polar, 2, devices)
    pair = in_order(polar, swap(polar, 1, devices))
    held = []
    for even, odd in ((2, 3), (4, 5), (6, 7)):
        routes = [(i, i ^ (2 * (odd if i % 2 else even))) for i in range(devices)]
        held.append(lax.ppermute(pair, "radial", routes))
    *ready, first = prepared(first)
    near, far, last = held
    early = swap(jnp.concatenate([last, first], 0), 1, devices)
    late = swap(jnp.concatenate([near, far], 0), 1, devices)
    parts = [pair] + held + [late[:size], late[size:], early[:size]]
    parts.append(in_order(first, early[size:]))
    places = [(0, 0), (2, 3), (4, 5), (6, 7), (3, 2), (5, 4), (7, 6), (1, 1)]
    return parts, places, ready


def per_device(
    units,
    field_start,
    phase_table,
    profile_index,
    group_power,
    group_slot,
    source_shift,
    slot_sub,
    tile_count,
    row_weights,
    col_weights,
):
    devices = lax.axis_size("radial")
    polar = march(field_start, phase_table, profile_index, group_power, group_slot, units)
    prepared = functools.partial(
        prepare, source_shift, slot_sub, tile_count, row_weights, col_weights, polar.shape[0]
    )
    parts, places, ready = gather_parts(polar, devices, prepared)
    pick, turned, cols = ready
    tile_value = tile_sum(pick, parts, places, turned, cols)
    return tile_value.reshape((1, 1) + tile_value.shape)


def solution(mesh):
    with jax.sharding.use_abstract_mesh(mesh.abstract_mesh):
        units = [
            pltpu.ACC(number // CHUNKS)((RADIX * SUB, 256), jnp.float32)
            for number in range(2 * CHUNKS)
        ]
    return jax.shard_map(
        functools.partial(per_device, units),
        mesh=mesh,
        in_specs=(
            P(None, "radial", None),
            P(),
            P(),
            P(),
            P(),
            P("range", None),
            P("range", None, None),
            P("range", None),
            P("range", "radial", None, None, None),
            P("range", "radial", None, None, None),
        ),
        out_specs=P("range", "radial", None, None),
        check_vma=False,
    )
```

```python
import functools
import math

import jax
import jax.numpy as jnp
import numpy as np
from jax import lax
from jax.experimental import pallas as pl
from jax.experimental.pallas import tpu as pltpu
from jax.sharding import PartitionSpec as P

VB = 128
SUB = 16
K_MAX = 16
CAP = 2
GROUP_RADIALS = 512
RADIX = 8
CHUNKS = 4

spread_angle = 6.0
absorb_rate = 0.5


def march_constants(height):
    width = height // RADIX
    index = np.arange(width)
    angle = 2.0 * np.pi / width * (index[:, None] * index[None, :] % width)
    factor = 1.0 / math.sqrt(height)
    cosine, sine = np.cos(angle) * factor, np.sin(angle) * factor
    weights = np.block([[cosine, -sine], [sine, cosine]]).astype(jnp.bfloat16)
    turn = 2.0 * np.pi / height * (np.arange(RADIX)[:, None] * index[None, :])
    level = np.arange(height)
    folded = np.minimum(level, height - level).astype(np.float64)
    theta = -spread_angle * (2.0 * folded / height) ** 2
    theta = theta.reshape(width, RADIX).T
    depth = np.maximum(0.0, (level - 0.9375 * height) / (0.0625 * height))
    absorber = np.exp(-absorb_rate * depth * depth).reshape(RADIX, width)
    waves = np.concatenate([np.cos(turn), np.sin(turn), np.cos(theta), np.sin(theta), absorber], 0)
    waves = np.pad(waves, ((0, -len(waves) % 8), (0, 0)))
    return weights, waves.astype(np.float32)


def cos_sin(angle):
    square = angle * angle
    cosine = jnp.full_like(angle, 1.0 / math.factorial(14) * -1.0)
    for order in (12, 10, 8, 6, 4, 2, 0):
        cosine = cosine * square + (-1.0) ** (order // 2) / math.factorial(order)
    sine = jnp.full_like(angle, 1.0 / math.factorial(13))
    for order in (11, 9, 7, 5, 3, 1):
        sine = sine * square + (-1.0) ** (order // 2) / math.factorial(order)
    return cosine, sine * angle


def turn(real, imag, cosine, sine):
    return real * cosine - imag * sine, real * sine + imag * cosine


def turn_back(real, imag, cosine, sine):
    return real * cosine + imag * sine, imag * cosine - real * sine


def radix_four(parts, sign):
    (r0, i0), (r1, i1), (r2, i2), (r3, i3) = parts
    sr02, si02, dr02, di02 = r0 + r2, i0 + i2, r0 - r2, i0 - i2
    sr13, si13, dr13, di13 = r1 + r3, i1 + i3, r1 - r3, i1 - i3
    plus = (dr02 - di13, di02 + dr13)
    minus = (dr02 + di13, di02 - dr13)
    if sign < 0:
        plus, minus = minus, plus
    return (sr02 + sr13, si02 + si13), plus, (sr02 - sr13, si02 - si13), minus


def radix_eight(parts, sign):
    sums, turned = [], []
    for q in range(4):
        (r, i), (s, t) = parts[q], parts[q + 4]
        sums.append((r + s, i + t))
        turned.append((r - s, i - t))
    half = math.sqrt(0.5)
    (r, i), (s, t), (v, w) = turned[1:]
    if sign < 0:
        turned[1] = ((r + i) * half, (i - r) * half)
        turned[2] = (t, -s)
        turned[3] = ((w - v) * half, (v + w) * -half)
    else:
        turned[1] = ((r - i) * half, (r + i) * half)
        turned[2] = (-t, s)
        turned[3] = ((v + w) * -half, (v - w) * half)
    even, odd = radix_four(sums, sign), radix_four(turned, sign)
    return [part for pair in zip(even, odd) for part in pair]


def march_kernel(
    steps,
    slabs,
    profile_hbm,
    power_hbm,
    slot_hbm,
    phase_hbm,
    wave_hbm,
    field_hbm,
    weight_hbm,
    polar_ref,
    profile_ref,
    power_ref,
    slot_ref,
    phase_ref,
    wave_ref,
    field_ref,
    weight_ref,
    phase_rows,
    screen_ref,
    sems,
    units,
):
    pairs = (
        (profile_hbm, profile_ref),
        (phase_hbm, phase_ref),
        (wave_hbm, wave_ref),
        (field_hbm, field_ref),
        (weight_hbm, weight_ref),
        (power_hbm, power_ref),
        (slot_hbm, slot_ref),
    )
    copies = [
        pltpu.make_async_copy(source, target, sems.at[number])
        for number, (source, target) in enumerate(pairs)
    ]
    for copy in copies:
        copy.start()
    rows, height = field_ref.shape[1:]
    width = height // RADIX
    chunks = rows // SUB
    slab = lax.axis_index("range")
    tile = lax.axis_index("radial")
    total = slabs * steps
    for copy in copies[:3]:
        copy.wait()
    for place in range(total):
        phase_rows[place : place + 1, :] = phase_ref[
            pl.ds(profile_ref[place // steps, place % steps], 1), :
        ]
    for q in range(RADIX):
        columns = slice(q * width, (q + 1) * width)
        cosine, sine = cos_sin(phase_rows[:, columns])
        absorber = wave_ref[4 * RADIX + q : 4 * RADIX + q + 1, :]
        damp = jnp.where(lax.broadcasted_iota(jnp.int32, cosine.shape, 0) == 0, 1.0, absorber)
        for part, value in enumerate((cosine * damp, sine * damp)):
            for place in range(total):
                screen_ref[place, part, :, columns] = jnp.broadcast_to(
                    value[place : place + 1], (8, width)
                )
    for copy in copies[3:]:
        copy.wait()
    gain = power_ref[slot_ref[tile * rows // GROUP_RADIALS]]

    def run(*products):
        for unit in range(2):
            pltpu.matmul_push_rhs(weight_ref[...], 0, unit)
            pltpu.matmul_acc_lhs(
                products[chunks * unit], jnp.zeros((RADIX * SUB, 2 * width), jnp.bfloat16), load_staged_rhs=0
            )
            pltpu.matmul_pop(products[chunks * unit])

        def wave(kind, j):
            return wave_ref[kind * RADIX + j : kind * RADIX + j + 1, :]

        def entering(chunk):
            spot = slice(chunk * SUB, (chunk + 1) * SUB)
            return [
                tuple(
                    field_ref[part, spot, q * width : (q + 1) * width].astype(jnp.float32)
                    for part in range(2)
                )
                for q in range(RADIX)
            ]

        def forward(place, chunk, field):
            parts, lines = [], []
            for q in range(RADIX):
                columns = slice(q * width, (q + 1) * width)
                screen = [screen_ref[place, part, :, columns] for part in range(2)]
                screen = [jnp.concatenate([value] * (SUB // 8), 0) for value in screen]
                parts.append(turn(*field[q], *screen))
            for j, (real, imag) in enumerate(radix_eight(parts, -1)):
                if j:
                    real, imag = turn_back(real, imag, wave(0, j), wave(1, j))
                lines.append(
                    jnp.concatenate([real.astype(jnp.bfloat16), imag.astype(jnp.bfloat16)], 1)
                )
            pltpu.matmul_acc_lhs(products[chunk], jnp.concatenate(lines, 0))

        def middle(chunk):
            spectrum = pltpu.matmul_pop(products[chunk])
            lines = []
            for j in range(RADIX):
                spot = slice(j * SUB, (j + 1) * SUB)
                real, imag = spectrum[spot, :width], spectrum[spot, width:]
                real, imag = turn(real, imag, wave(2, j), wave(3, j))
                lines.append(
                    jnp.concatenate([imag.astype(jnp.bfloat16), real.astype(jnp.bfloat16)], 1)
                )
            pltpu.matmul_acc_lhs(products[chunks + chunk], jnp.concatenate(lines, 0))

        def backward(chunk, lowest):
            back = pltpu.matmul_pop(products[chunks + chunk])
            parts = []
            for j in range(RADIX):
                spot = slice(j * SUB, (j + 1) * SUB)
                real, imag = back[spot, width:], back[spot, :width]
                if j:
                    real, imag = turn(real, imag, wave(0, j), wave(1, j))
                parts.append((real, imag))
            if lowest:
                return [tuple(sum(part[1:], part[0]) for part in zip(*parts))]
            return radix_eight(parts, 1)

        def power_rows(step, chunk, real, imag):
            power = gain * (real * real + imag * imag)
            spot = slice(chunk * SUB, (chunk + 1) * SUB)
            polar_ref[spot, step * VB : (step + 1) * VB] = power.astype(jnp.bfloat16)

        def one_slab(number, last):
            events = []
            for step in range(steps):
                for chunk in range(chunks):
                    start = chunks * step + chunk
                    events.append((start, "forward", step, chunk))
                    events.append((start + 1.5, "middle", step, chunk))
            for chunk in range(chunks):
                events.append((chunks * steps + chunk, "leave", steps, chunk))
            for _, kind, step, chunk in sorted(events):
                if kind == "middle":
                    middle(chunk)
                    continue
                if step == 0:
                    forward(number * steps, chunk, entering(chunk))
                    continue
                field = backward(chunk, kind == "leave" and last)
                if last:
                    power_rows(step - 1, chunk, *field[0])
                if kind == "forward":
                    forward(number * steps + step, chunk, field)
                elif not last:
                    spot = slice(chunk * SUB, (chunk + 1) * SUB)
                    for q in range(RADIX):
                        for part in range(2):
                            field_ref[part, spot, q * width : (q + 1) * width] = field[q][
                                part
                            ].astype(jnp.bfloat16)

        def whole_slab(number, carry):
            one_slab(number, False)
            return carry

        lax.fori_loop(0, slab, whole_slab, 0)
        one_slab(slab, True)

    pl.run_scoped(run, *units)


def in_hbm(operands):
    return [pltpu.with_memory_space_constraint(value, pltpu.HBM) for value in operands]


def march(field, phase_table, profile_index, group_power, group_slot, units):
    rows, height = field.shape[1:]
    slabs, steps = profile_index.shape
    weights, waves = march_constants(height)
    operands = [profile_index, group_power, group_slot, phase_table, waves, field, weights]
    places = [pltpu.SMEM] * 3 + [pltpu.VMEM] * 4
    return pl.pallas_call(
        functools.partial(march_kernel, steps, slabs, units=units),
        out_shape=jax.ShapeDtypeStruct((rows, steps * VB), jnp.bfloat16),
        in_specs=[pl.BlockSpec(memory_space=pltpu.HBM)] * len(operands),
        out_specs=pl.BlockSpec(memory_space=pltpu.VMEM),
        scratch_shapes=[place(o.shape, o.dtype) for place, o in zip(places, operands)]
        + [
            pltpu.VMEM((-(-slabs * steps // 8) * 8, height), jnp.float32),
            pltpu.VMEM((slabs * steps, 2, 8, height), jnp.float32),
            pltpu.SemaphoreType.DMA((len(operands),)),
        ],
        compiler_params=pltpu.CompilerParams(vmem_limit_bytes=24 * 1024 * 1024),
        name="march",
    )(*in_hbm(operands))


def prepare_kernel(
    local_rows,
    shift_hbm,
    sub_hbm,
    count_hbm,
    row_hbm,
    col_hbm,
    after_ref,
    starts_ref,
    turned_ref,
    col_ref,
    passed_ref,
    shift_ref,
    sub_ref,
    count_ref,
    row_ref,
    sems,
):
    pairs = (
        (shift_hbm, shift_ref),
        (sub_hbm, sub_ref),
        (count_hbm, count_ref),
        (row_hbm, row_ref),
        (col_hbm, col_ref),
    )
    copies = [
        pltpu.make_async_copy(source, target, sems.at[number])
        for number, (source, target) in enumerate(pairs)
    ]
    for copy in copies:
        copy.start()
    tile = lax.axis_index("radial")
    devices = lax.axis_size("radial")
    for copy in copies[:4]:
        copy.wait()
    column = lax.broadcasted_iota(jnp.int32, starts_ref.shape, 1)
    starts = jnp.full(starts_ref.shape, -1, jnp.int32)
    for slot in range(K_MAX):
        source = lax.rem(tile + shift_ref[0, tile] + slot // CAP, devices)
        start = source * local_rows + sub_ref[0, tile, slot] * SUB
        start = jnp.where(slot < count_ref[0, tile], start, -1)
        starts = jnp.where(column == slot, start, starts)
    starts_ref[...] = starts
    turned_ref[...] = row_ref[...].T
    passed_ref[...] = after_ref[...]
    copies[4].wait()


def prepare(source_shift, slot_sub, tile_count, row_weights, col_weights, local_rows, after):
    pixels = row_weights.shape[-1]
    rows_flat = row_weights.reshape(K_MAX * SUB, pixels)
    cols_flat = col_weights.reshape(K_MAX, col_weights.shape[-2], pixels)
    operands = [source_shift, slot_sub, tile_count, rows_flat]
    places = [pltpu.SMEM] * 3 + [pltpu.VMEM]
    return pl.pallas_call(
        functools.partial(prepare_kernel, local_rows),
        out_shape=[
            jax.ShapeDtypeStruct((8, 128), jnp.int32),
            jax.ShapeDtypeStruct((pixels, K_MAX * SUB), jnp.bfloat16),
            jax.ShapeDtypeStruct(cols_flat.shape, jnp.bfloat16),
            jax.ShapeDtypeStruct(after.shape, after.dtype),
        ],
        in_specs=[pl.BlockSpec(memory_space=pltpu.HBM)] * 5
        + [pl.BlockSpec(memory_space=pltpu.VMEM)],
        out_specs=[pl.BlockSpec(memory_space=pltpu.VMEM)] * 4,
        scratch_shapes=[place(o.shape, o.dtype) for place, o in zip(places, operands)]
        + [pltpu.SemaphoreType.DMA((5,))],
        compiler_params=pltpu.CompilerParams(vmem_limit_bytes=24 * 1024 * 1024),
        cost_estimate=pl.CostEstimate(
            flops=2_000_000_000, bytes_accessed=2 * cols_flat.size, transcendentals=0
        ),
        name="prepare",
    )(*in_hbm(operands + [cols_flat]), after)


def tile_kernel(places, starts_ref, *refs):
    part_refs = refs[: len(places)]
    row_ref, col_ref, out_ref, polar_ref, mixed_ref = refs[len(places) :]
    chip = lax.axis_index("radial") // 2
    core = lax.axis_index("radial") % 2
    for (even, odd), part_ref in zip(places, part_refs):
        size = part_ref.shape[0]
        start = jnp.where(core == 0, chip ^ even, chip ^ odd) * size
        if size == polar_ref.shape[0]:
            start = 0
        polar_ref[pl.ds(start, size), :] = part_ref[...]
    starts = [starts_ref[0:1, slot : slot + 1][0, 0] for slot in range(K_MAX)]
    for slot, start in enumerate(starts):
        block = polar_ref[pl.ds(pl.multiple_of(jnp.maximum(start, 0), SUB), SUB), :]
        block = jnp.where(start >= 0, block, jnp.zeros_like(block))
        mixed = jnp.dot(block, col_ref[slot], preferred_element_type=jnp.float32)
        mixed_ref[slot * SUB : (slot + 1) * SUB, :] = mixed.astype(jnp.bfloat16)
    out_ref[...] = jnp.dot(row_ref[...], mixed_ref[...], preferred_element_type=jnp.float32)


def tile_sum(starts, parts, places, row_weights, col_weights):
    pixels = row_weights.shape[0]
    channels = col_weights.shape[-2]
    radials = sum(part.shape[0] for part in parts)
    vmem = pl.BlockSpec(memory_space=pltpu.VMEM)
    return pl.pallas_call(
        functools.partial(tile_kernel, places),
        out_shape=jax.ShapeDtypeStruct((pixels, pixels), jnp.float32),
        in_specs=[vmem] * (len(parts) + 3),
        out_specs=vmem,
        scratch_shapes=[
            pltpu.VMEM((radials, channels), jnp.bfloat16),
            pltpu.VMEM((K_MAX * SUB, pixels), jnp.bfloat16),
        ],
        compiler_params=pltpu.CompilerParams(vmem_limit_bytes=24 * 1024 * 1024),
        name="tile_sum",
    )(
        starts,
        *parts,
        row_weights,
        col_weights,
    )


def swap(value, distance, devices):
    return lax.ppermute(value, "radial", [(i, i ^ distance) for i in range(devices)])


def gather_parts(polar, devices, prepared):
    if devices != 16:
        whole = lax.all_gather(polar, "radial", axis=0, tiled=True)
        return [whole], [(0, 0)], prepared(polar)[:3]
    core = lax.axis_index("radial") % 2
    size = 2 * polar.shape[0]

    def in_order(own, other):
        return jnp.where(
            core == 0, jnp.concatenate([own, other], 0), jnp.concatenate([other, own], 0)
        )

    first = swap(polar, 2, devices)
    pair = in_order(polar, swap(polar, 1, devices))
    held = []
    for even, odd in ((2, 3), (4, 5), (6, 7)):
        routes = [(i, i ^ (2 * (odd if i % 2 else even))) for i in range(devices)]
        held.append(lax.ppermute(pair, "radial", routes))
    *ready, first = prepared(first)
    near, far, last = held
    early = swap(jnp.concatenate([last, first], 0), 1, devices)
    late = swap(jnp.concatenate([near, far], 0), 1, devices)
    parts = [pair] + held + [late[:size], late[size:], early[:size]]
    parts.append(in_order(first, early[size:]))
    places = [(0, 0), (2, 3), (4, 5), (6, 7), (3, 2), (5, 4), (7, 6), (1, 1)]
    return parts, places, ready


def per_device(
    units,
    field_start,
    phase_table,
    profile_index,
    group_power,
    group_slot,
    source_shift,
    slot_sub,
    tile_count,
    row_weights,
    col_weights,
):
    devices = lax.axis_size("radial")
    polar = march(field_start, phase_table, profile_index, group_power, group_slot, units)
    prepared = functools.partial(
        prepare, source_shift, slot_sub, tile_count, row_weights, col_weights, polar.shape[0]
    )
    parts, places, ready = gather_parts(polar, devices, prepared)
    starts, turned, cols = ready
    tile_value = tile_sum(starts, parts, places, turned, cols)
    return tile_value.reshape((1, 1) + tile_value.shape)


def solution(mesh):
    with jax.sharding.use_abstract_mesh(mesh.abstract_mesh):
        units = [
            pltpu.ACC(number // CHUNKS)((RADIX * SUB, 256), jnp.float32)
            for number in range(2 * CHUNKS)
        ]
    return jax.shard_map(
        functools.partial(per_device, units),
        mesh=mesh,
        in_specs=(
            P(None, "radial", None),
            P(),
            P(),
            P(),
            P(),
            P("range", None),
            P("range", None, None),
            P("range", None),
            P("range", "radial", None, None, None),
            P("range", "radial", None, None, None),
        ),
        out_specs=P("range", "radial", None, None),
        check_vma=False,
    )
```

```python
import functools
import math

import jax
import jax.numpy as jnp
import numpy as np
from jax import lax
from jax.experimental import pallas as pl
from jax.experimental.pallas import tpu as pltpu
from jax.sharding import PartitionSpec as P

VB = 128
SUB = 16
K_MAX = 16
CAP = 2
GROUP_RADIALS = 512
RADIX = 8
CHUNKS = 4

spread_angle = 6.0
absorb_rate = 0.5


def march_constants(height):
    width = height // RADIX
    index = np.arange(width)
    angle = 2.0 * np.pi / width * (index[:, None] * index[None, :] % width)
    factor = 1.0 / math.sqrt(height)
    cosine, sine = np.cos(angle) * factor, np.sin(angle) * factor
    weights = np.block([[cosine, -sine], [sine, cosine]]).astype(jnp.bfloat16)
    turn = 2.0 * np.pi / height * (np.arange(RADIX)[:, None] * index[None, :])
    level = np.arange(height)
    folded = np.minimum(level, height - level).astype(np.float64)
    theta = -spread_angle * (2.0 * folded / height) ** 2
    theta = theta.reshape(width, RADIX).T
    depth = np.maximum(0.0, (level - 0.9375 * height) / (0.0625 * height))
    absorber = np.exp(-absorb_rate * depth * depth).reshape(RADIX, width)
    waves = np.concatenate([np.cos(turn), np.sin(turn), np.cos(theta), np.sin(theta), absorber], 0)
    waves = np.pad(waves, ((0, -len(waves) % 8), (0, 0)))
    return weights, waves.astype(np.float32)


def cos_sin(angle):
    square = angle * angle
    cosine = jnp.full_like(angle, 1.0 / math.factorial(14) * -1.0)
    for order in (12, 10, 8, 6, 4, 2, 0):
        cosine = cosine * square + (-1.0) ** (order // 2) / math.factorial(order)
    sine = jnp.full_like(angle, 1.0 / math.factorial(13))
    for order in (11, 9, 7, 5, 3, 1):
        sine = sine * square + (-1.0) ** (order // 2) / math.factorial(order)
    return cosine, sine * angle


def turn(real, imag, cosine, sine):
    return real * cosine - imag * sine, real * sine + imag * cosine


def turn_back(real, imag, cosine, sine):
    return real * cosine + imag * sine, imag * cosine - real * sine


def radix_four(parts, sign):
    (r0, i0), (r1, i1), (r2, i2), (r3, i3) = parts
    sr02, si02, dr02, di02 = r0 + r2, i0 + i2, r0 - r2, i0 - i2
    sr13, si13, dr13, di13 = r1 + r3, i1 + i3, r1 - r3, i1 - i3
    plus = (dr02 - di13, di02 + dr13)
    minus = (dr02 + di13, di02 - dr13)
    if sign < 0:
        plus, minus = minus, plus
    return (sr02 + sr13, si02 + si13), plus, (sr02 - sr13, si02 - si13), minus


def radix_eight(parts, sign):
    sums, turned = [], []
    for q in range(4):
        (r, i), (s, t) = parts[q], parts[q + 4]
        sums.append((r + s, i + t))
        turned.append((r - s, i - t))
    half = math.sqrt(0.5)
    (r, i), (s, t), (v, w) = turned[1:]
    if sign < 0:
        turned[1] = ((r + i) * half, (i - r) * half)
        turned[2] = (t, -s)
        turned[3] = ((w - v) * half, (v + w) * -half)
    else:
        turned[1] = ((r - i) * half, (r + i) * half)
        turned[2] = (-t, s)
        turned[3] = ((v + w) * -half, (v - w) * half)
    even, odd = radix_four(sums, sign), radix_four(turned, sign)
    return [part for pair in zip(even, odd) for part in pair]


def march_kernel(
    steps,
    slabs,
    profile_hbm,
    power_hbm,
    slot_hbm,
    phase_hbm,
    wave_hbm,
    field_hbm,
    weight_hbm,
    polar_ref,
    profile_ref,
    power_ref,
    slot_ref,
    phase_ref,
    wave_ref,
    field_ref,
    weight_ref,
    phase_rows,
    screen_ref,
    sems,
    units,
):
    pairs = (
        (profile_hbm, profile_ref),
        (phase_hbm, phase_ref),
        (wave_hbm, wave_ref),
        (field_hbm, field_ref),
        (weight_hbm, weight_ref),
        (power_hbm, power_ref),
        (slot_hbm, slot_ref),
    )
    copies = [
        pltpu.make_async_copy(source, target, sems.at[number])
        for number, (source, target) in enumerate(pairs)
    ]
    for copy in copies:
        copy.start()
    rows, height = field_ref.shape[1:]
    width = height // RADIX
    chunks = rows // SUB
    slab = lax.axis_index("range")
    tile = lax.axis_index("radial")
    total = slabs * steps
    for copy in copies[:3]:
        copy.wait()
    for place in range(total):
        phase_rows[place : place + 1, :] = phase_ref[
            pl.ds(profile_ref[place // steps, place % steps], 1), :
        ]
    for q in range(RADIX):
        columns = slice(q * width, (q + 1) * width)
        cosine, sine = cos_sin(phase_rows[:, columns])
        absorber = wave_ref[4 * RADIX + q : 4 * RADIX + q + 1, :]
        damp = jnp.where(lax.broadcasted_iota(jnp.int32, cosine.shape, 0) == 0, 1.0, absorber)
        for part, value in enumerate((cosine * damp, sine * damp)):
            for place in range(total):
                screen_ref[place, part, :, columns] = jnp.broadcast_to(
                    value[place : place + 1], (8, width)
                )
    for copy in copies[3:]:
        copy.wait()
    gain = power_ref[slot_ref[tile * rows // GROUP_RADIALS]]

    def run(*products):
        for unit in range(2):
            pltpu.matmul_push_rhs(weight_ref[...], 0, unit)
            pltpu.matmul_acc_lhs(
                products[chunks * unit], jnp.zeros((RADIX * SUB, 2 * width), jnp.bfloat16), load_staged_rhs=0
            )
            pltpu.matmul_pop(products[chunks * unit])

        def wave(kind, j):
            return wave_ref[kind * RADIX + j : kind * RADIX + j + 1, :]

        def entering(chunk):
            spot = slice(chunk * SUB, (chunk + 1) * SUB)
            return [
                tuple(
                    field_ref[part, spot, q * width : (q + 1) * width].astype(jnp.float32)
                    for part in range(2)
                )
                for q in range(RADIX)
            ]

        def forward(place, chunk, field):
            parts, lines = [], []
            for q in range(RADIX):
                columns = slice(q * width, (q + 1) * width)
                screen = [screen_ref[place, part, :, columns] for part in range(2)]
                screen = [jnp.concatenate([value] * (SUB // 8), 0) for value in screen]
                parts.append(turn(*field[q], *screen))
            for j, (real, imag) in enumerate(radix_eight(parts, -1)):
                if j:
                    real, imag = turn_back(real, imag, wave(0, j), wave(1, j))
                lines.append(
                    jnp.concatenate([real.astype(jnp.bfloat16), imag.astype(jnp.bfloat16)], 1)
                )
            pltpu.matmul_acc_lhs(products[chunk], jnp.concatenate(lines, 0))

        def middle(chunk):
            spectrum = pltpu.matmul_pop(products[chunk])
            lines = []
            for j in range(RADIX):
                spot = slice(j * SUB, (j + 1) * SUB)
                real, imag = spectrum[spot, :width], spectrum[spot, width:]
                real, imag = turn(real, imag, wave(2, j), wave(3, j))
                lines.append(
                    jnp.concatenate([imag.astype(jnp.bfloat16), real.astype(jnp.bfloat16)], 1)
                )
            pltpu.matmul_acc_lhs(products[chunks + chunk], jnp.concatenate(lines, 0))

        def backward(chunk, lowest):
            back = pltpu.matmul_pop(products[chunks + chunk])
            parts = []
            for j in range(RADIX):
                spot = slice(j * SUB, (j + 1) * SUB)
                real, imag = back[spot, width:], back[spot, :width]
                if j:
                    real, imag = turn(real, imag, wave(0, j), wave(1, j))
                parts.append((real, imag))
            if lowest:
                return [tuple(sum(part[1:], part[0]) for part in zip(*parts))]
            return radix_eight(parts, 1)

        def power_rows(step, chunk, real, imag):
            power = gain * (real * real + imag * imag)
            spot = slice(chunk * SUB, (chunk + 1) * SUB)
            polar_ref[spot, step * VB : (step + 1) * VB] = power.astype(jnp.bfloat16)

        def one_slab(number, last):
            events = []
            for step in range(steps):
                for chunk in range(chunks):
                    start = chunks * step + chunk
                    events.append((start, "forward", step, chunk))
                    events.append((start + 1.5, "middle", step, chunk))
            for chunk in range(chunks):
                events.append((chunks * steps + chunk, "leave", steps, chunk))
            for _, kind, step, chunk in sorted(events):
                if kind == "middle":
                    middle(chunk)
                    continue
                if step == 0:
                    forward(number * steps, chunk, entering(chunk))
                    continue
                field = backward(chunk, kind == "leave" and last)
                if last:
                    power_rows(step - 1, chunk, *field[0])
                if kind == "forward":
                    forward(number * steps + step, chunk, field)
                elif not last:
                    spot = slice(chunk * SUB, (chunk + 1) * SUB)
                    for q in range(RADIX):
                        for part in range(2):
                            field_ref[part, spot, q * width : (q + 1) * width] = field[q][
                                part
                            ].astype(jnp.bfloat16)

        def whole_slab(number, carry):
            one_slab(number, False)
            return carry

        lax.fori_loop(0, slab, whole_slab, 0)
        one_slab(slab, True)

    pl.run_scoped(run, *units)


def in_hbm(operands):
    return [pltpu.with_memory_space_constraint(value, pltpu.HBM) for value in operands]


def march(field, phase_table, profile_index, group_power, group_slot, units):
    rows, height = field.shape[1:]
    slabs, steps = profile_index.shape
    weights, waves = march_constants(height)
    operands = [profile_index, group_power, group_slot, phase_table, waves, field, weights]
    places = [pltpu.SMEM] * 3 + [pltpu.VMEM] * 4
    return pl.pallas_call(
        functools.partial(march_kernel, steps, slabs, units=units),
        out_shape=jax.ShapeDtypeStruct((rows, steps * VB), jnp.bfloat16),
        in_specs=[pl.BlockSpec(memory_space=pltpu.HBM)] * len(operands),
        out_specs=pl.BlockSpec(memory_space=pltpu.VMEM),
        scratch_shapes=[place(o.shape, o.dtype) for place, o in zip(places, operands)]
        + [
            pltpu.VMEM((-(-slabs * steps // 8) * 8, height), jnp.float32),
            pltpu.VMEM((slabs * steps, 2, 8, height), jnp.float32),
            pltpu.SemaphoreType.DMA((len(operands),)),
        ],
        compiler_params=pltpu.CompilerParams(vmem_limit_bytes=24 * 1024 * 1024),
        name="march",
    )(*in_hbm(operands))


def prepare_kernel(
    local_rows,
    shift_hbm,
    sub_hbm,
    count_hbm,
    row_hbm,
    col_hbm,
    after_ref,
    starts_ref,
    turned_ref,
    col_ref,
    passed_ref,
    shift_ref,
    sub_ref,
    count_ref,
    row_ref,
    sems,
):
    pairs = (
        (shift_hbm, shift_ref),
        (sub_hbm, sub_ref),
        (count_hbm, count_ref),
        (row_hbm, row_ref),
        (col_hbm, col_ref),
    )
    copies = [
        pltpu.make_async_copy(source, target, sems.at[number])
        for number, (source, target) in enumerate(pairs)
    ]
    for copy in copies:
        copy.start()
    tile = lax.axis_index("radial")
    devices = lax.axis_size("radial")
    for copy in copies[:4]:
        copy.wait()
    column = lax.broadcasted_iota(jnp.int32, starts_ref.shape, 1)
    starts = jnp.full(starts_ref.shape, -1, jnp.int32)
    for slot in range(K_MAX):
        source = lax.rem(tile + shift_ref[0, tile] + slot // CAP, devices)
        start = source * local_rows + sub_ref[0, tile, slot] * SUB
        start = jnp.where(slot < count_ref[0, tile], start, -1)
        starts = jnp.where(column == slot, start, starts)
    starts_ref[...] = starts
    turned_ref[...] = row_ref[...].T
    passed_ref[...] = after_ref[...]
    copies[4].wait()


def prepare(source_shift, slot_sub, tile_count, row_weights, col_weights, local_rows, after):
    pixels = row_weights.shape[-1]
    rows_flat = row_weights.reshape(K_MAX * SUB, pixels)
    cols_flat = col_weights.reshape(K_MAX, col_weights.shape[-2], pixels)
    operands = [source_shift, slot_sub, tile_count, rows_flat]
    places = [pltpu.SMEM] * 3 + [pltpu.VMEM]
    return pl.pallas_call(
        functools.partial(prepare_kernel, local_rows),
        out_shape=[
            jax.ShapeDtypeStruct((8, 128), jnp.int32),
            jax.ShapeDtypeStruct((pixels, K_MAX * SUB), jnp.bfloat16),
            jax.ShapeDtypeStruct(cols_flat.shape, jnp.bfloat16),
            jax.ShapeDtypeStruct(after.shape, after.dtype),
        ],
        in_specs=[pl.BlockSpec(memory_space=pltpu.HBM)] * 5
        + [pl.BlockSpec(memory_space=pltpu.VMEM)],
        out_specs=[pl.BlockSpec(memory_space=pltpu.VMEM)] * 4,
        scratch_shapes=[place(o.shape, o.dtype) for place, o in zip(places, operands)]
        + [pltpu.SemaphoreType.DMA((5,))],
        compiler_params=pltpu.CompilerParams(vmem_limit_bytes=24 * 1024 * 1024),
        cost_estimate=pl.CostEstimate(
            flops=2_000_000_000, bytes_accessed=2 * cols_flat.size, transcendentals=0
        ),
        name="prepare",
    )(*in_hbm(operands + [cols_flat]), after)


def tile_kernel(places, starts_ref, *refs):
    part_refs = refs[: len(places)]
    row_ref, col_ref, out_ref, polar_ref, mixed_ref = refs[len(places) :]
    chip = lax.axis_index("radial") // 2
    core = lax.axis_index("radial") % 2
    for (even, odd), part_ref in zip(places, part_refs):
        size = part_ref.shape[0]
        start = jnp.where(core == 0, chip ^ even, chip ^ odd) * size
        if size == polar_ref.shape[0]:
            start = 0
        polar_ref[pl.ds(start, size), :] = part_ref[...]
    starts = [starts_ref[0:1, slot : slot + 1][0, 0] for slot in range(K_MAX)]
    for slot, start in enumerate(starts):
        block = polar_ref[pl.ds(pl.multiple_of(jnp.maximum(start, 0), SUB), SUB), :]
        block = jnp.where(start >= 0, block, jnp.zeros_like(block))
        mixed = jnp.dot(block, col_ref[slot], preferred_element_type=jnp.float32)
        mixed_ref[slot * SUB : (slot + 1) * SUB, :] = mixed.astype(jnp.bfloat16)
    out_ref[...] = jnp.dot(row_ref[...], mixed_ref[...], preferred_element_type=jnp.float32)


def tile_sum(starts, parts, places, row_weights, col_weights):
    pixels = row_weights.shape[0]
    channels = col_weights.shape[-2]
    radials = sum(part.shape[0] for part in parts)
    vmem = pl.BlockSpec(memory_space=pltpu.VMEM)
    return pl.pallas_call(
        functools.partial(tile_kernel, places),
        out_shape=jax.ShapeDtypeStruct((pixels, pixels), jnp.float32),
        in_specs=[vmem] * (len(parts) + 3),
        out_specs=vmem,
        scratch_shapes=[
            pltpu.VMEM((radials, channels), jnp.bfloat16),
            pltpu.VMEM((K_MAX * SUB, pixels), jnp.bfloat16),
        ],
        compiler_params=pltpu.CompilerParams(vmem_limit_bytes=24 * 1024 * 1024),
        name="tile_sum",
    )(
        starts,
        *parts,
        row_weights,
        col_weights,
    )


def swap(value, distance, devices):
    return lax.ppermute(value, "radial", [(i, i ^ distance) for i in range(devices)])


def gather_parts(polar, devices, prepared):
    if devices != 16:
        whole = lax.all_gather(polar, "radial", axis=0, tiled=True)
        return [whole], [(0, 0)], prepared(polar)[:3]
    core = lax.axis_index("radial") % 2
    size = 2 * polar.shape[0]

    def in_order(own, other):
        return jnp.where(
            core == 0, jnp.concatenate([own, other], 0), jnp.concatenate([other, own], 0)
        )

    first = swap(polar, 2, devices)
    pair = in_order(polar, swap(polar, 1, devices))
    held = []
    for even, odd in ((4, 5), (2, 3), (6, 7)):
        routes = [(i, i ^ (2 * (odd if i % 2 else even))) for i in range(devices)]
        held.append(lax.ppermute(pair, "radial", routes))
    *ready, first = prepared(first)
    early = swap(jnp.concatenate([held[2], first], 0), 1, devices)
    late = swap(jnp.concatenate(held[:2], 0), 1, devices)
    parts = [pair] + held
    parts += [late[i * size : (i + 1) * size] for i in range(2)]
    parts += [early[i * size : (i + 1) * size] for i in range(1)]
    parts.append(in_order(first, early[1 * size :]))
    places = [(0, 0), (4, 5), (2, 3), (6, 7), (5, 4), (3, 2), (7, 6), (1, 1)]
    return parts, places, ready


def per_device(
    units,
    field_start,
    phase_table,
    profile_index,
    group_power,
    group_slot,
    source_shift,
    slot_sub,
    tile_count,
    row_weights,
    col_weights,
):
    devices = lax.axis_size("radial")
    polar = march(field_start, phase_table, profile_index, group_power, group_slot, units)
    prepared = functools.partial(
        prepare, source_shift, slot_sub, tile_count, row_weights, col_weights, polar.shape[0]
    )
    parts, places, ready = gather_parts(polar, devices, prepared)
    starts, turned, cols = ready
    tile_value = tile_sum(starts, parts, places, turned, cols)
    return tile_value.reshape((1, 1) + tile_value.shape)


def solution(mesh):
    with jax.sharding.use_abstract_mesh(mesh.abstract_mesh):
        units = [
            pltpu.ACC(number // CHUNKS)((RADIX * SUB, 256), jnp.float32)
            for number in range(2 * CHUNKS)
        ]
    return jax.shard_map(
        functools.partial(per_device, units),
        mesh=mesh,
        in_specs=(
            P(None, "radial", None),
            P(),
            P(),
            P(),
            P(),
            P("range", None),
            P("range", None, None),
            P("range", None),
            P("range", "radial", None, None, None),
            P("range", "radial", None, None, None),
        ),
        out_specs=P("range", "radial", None, None),
        check_vma=False,
    )
```

```python
import functools
import math

import jax
import jax.numpy as jnp
import numpy as np
from jax import lax
from jax.experimental import pallas as pl
from jax.experimental.pallas import tpu as pltpu
from jax.sharding import PartitionSpec as P

VB = 128
SUB = 16
K_MAX = 16
CAP = 2
GROUP_RADIALS = 512
RADIX = 8
CHUNKS = 4

spread_angle = 6.0
absorb_rate = 0.5


def march_constants(height):
    width = height // RADIX
    index = np.arange(width)
    angle = 2.0 * np.pi / width * (index[:, None] * index[None, :] % width)
    factor = 1.0 / math.sqrt(height)
    cosine, sine = np.cos(angle) * factor, np.sin(angle) * factor
    weights = np.block([[cosine, -sine], [sine, cosine]]).astype(jnp.bfloat16)
    turn = 2.0 * np.pi / height * (np.arange(RADIX)[:, None] * index[None, :])
    level = np.arange(height)
    folded = np.minimum(level, height - level).astype(np.float64)
    theta = -spread_angle * (2.0 * folded / height) ** 2
    theta = theta.reshape(width, RADIX).T
    depth = np.maximum(0.0, (level - 0.9375 * height) / (0.0625 * height))
    absorber = np.exp(-absorb_rate * depth * depth).reshape(RADIX, width)
    waves = np.concatenate([np.cos(turn), np.sin(turn), np.cos(theta), np.sin(theta), absorber], 0)
    waves = np.pad(waves, ((0, -len(waves) % 8), (0, 0)))
    return weights, waves.astype(np.float32)


def cos_sin(angle):
    square = angle * angle
    cosine = jnp.full_like(angle, 1.0 / math.factorial(14) * -1.0)
    for order in (12, 10, 8, 6, 4, 2, 0):
        cosine = cosine * square + (-1.0) ** (order // 2) / math.factorial(order)
    sine = jnp.full_like(angle, 1.0 / math.factorial(13))
    for order in (11, 9, 7, 5, 3, 1):
        sine = sine * square + (-1.0) ** (order // 2) / math.factorial(order)
    return cosine, sine * angle


def turn(real, imag, cosine, sine):
    return real * cosine - imag * sine, real * sine + imag * cosine


def turn_back(real, imag, cosine, sine):
    return real * cosine + imag * sine, imag * cosine - real * sine


def radix_four(parts, sign):
    (r0, i0), (r1, i1), (r2, i2), (r3, i3) = parts
    sr02, si02, dr02, di02 = r0 + r2, i0 + i2, r0 - r2, i0 - i2
    sr13, si13, dr13, di13 = r1 + r3, i1 + i3, r1 - r3, i1 - i3
    plus = (dr02 - di13, di02 + dr13)
    minus = (dr02 + di13, di02 - dr13)
    if sign < 0:
        plus, minus = minus, plus
    return (sr02 + sr13, si02 + si13), plus, (sr02 - sr13, si02 - si13), minus


def radix_eight(parts, sign):
    sums, turned = [], []
    for q in range(4):
        (r, i), (s, t) = parts[q], parts[q + 4]
        sums.append((r + s, i + t))
        turned.append((r - s, i - t))
    half = math.sqrt(0.5)
    (r, i), (s, t), (v, w) = turned[1:]
    if sign < 0:
        turned[1] = ((r + i) * half, (i - r) * half)
        turned[2] = (t, -s)
        turned[3] = ((w - v) * half, (v + w) * -half)
    else:
        turned[1] = ((r - i) * half, (r + i) * half)
        turned[2] = (-t, s)
        turned[3] = ((v + w) * -half, (v - w) * half)
    even, odd = radix_four(sums, sign), radix_four(turned, sign)
    return [part for pair in zip(even, odd) for part in pair]


def march_kernel(
    steps,
    slabs,
    profile_hbm,
    power_hbm,
    slot_hbm,
    phase_hbm,
    wave_hbm,
    field_hbm,
    weight_hbm,
    polar_ref,
    profile_ref,
    power_ref,
    slot_ref,
    phase_ref,
    wave_ref,
    field_ref,
    weight_ref,
    phase_rows,
    screen_ref,
    sems,
    units,
):
    pairs = (
        (profile_hbm, profile_ref),
        (phase_hbm, phase_ref),
        (wave_hbm, wave_ref),
        (field_hbm, field_ref),
        (weight_hbm, weight_ref),
        (power_hbm, power_ref),
        (slot_hbm, slot_ref),
    )
    copies = [
        pltpu.make_async_copy(source, target, sems.at[number])
        for number, (source, target) in enumerate(pairs)
    ]
    for copy in copies:
        copy.start()
    rows, height = field_ref.shape[1:]
    width = height // RADIX
    chunks = rows // SUB
    slab = lax.axis_index("range")
    tile = lax.axis_index("radial")
    total = slabs * steps
    for copy in copies[:3]:
        copy.wait()
    for place in range(total):
        phase_rows[place : place + 1, :] = phase_ref[
            pl.ds(profile_ref[place // steps, place % steps], 1), :
        ]
    for q in range(RADIX):
        columns = slice(q * width, (q + 1) * width)
        cosine, sine = cos_sin(phase_rows[:, columns])
        absorber = wave_ref[4 * RADIX + q : 4 * RADIX + q + 1, :]
        damp = jnp.where(lax.broadcasted_iota(jnp.int32, cosine.shape, 0) == 0, 1.0, absorber)
        for part, value in enumerate((cosine * damp, sine * damp)):
            for place in range(total):
                screen_ref[place, part, :, columns] = jnp.broadcast_to(
                    value[place : place + 1], (8, width)
                )
    for copy in copies[3:]:
        copy.wait()
    gain = power_ref[slot_ref[tile * rows // GROUP_RADIALS]]

    def run(*products):
        for unit in range(2):
            pltpu.matmul_push_rhs(weight_ref[...], 0, unit)
            pltpu.matmul_acc_lhs(
                products[chunks * unit], jnp.zeros((RADIX * SUB, 2 * width), jnp.bfloat16), load_staged_rhs=0
            )
            pltpu.matmul_pop(products[chunks * unit])

        def wave(kind, j):
            return wave_ref[kind * RADIX + j : kind * RADIX + j + 1, :]

        def entering(chunk):
            spot = slice(chunk * SUB, (chunk + 1) * SUB)
            return [
                tuple(
                    field_ref[part, spot, q * width : (q + 1) * width].astype(jnp.float32)
                    for part in range(2)
                )
                for q in range(RADIX)
            ]

        def forward(place, chunk, field):
            parts, lines = [], []
            for q in range(RADIX):
                columns = slice(q * width, (q + 1) * width)
                screen = [screen_ref[place, part, :, columns] for part in range(2)]
                screen = [jnp.concatenate([value] * (SUB // 8), 0) for value in screen]
                parts.append(turn(*field[q], *screen))
            for j, (real, imag) in enumerate(radix_eight(parts, -1)):
                if j:
                    real, imag = turn_back(real, imag, wave(0, j), wave(1, j))
                lines.append(
                    jnp.concatenate([real.astype(jnp.bfloat16), imag.astype(jnp.bfloat16)], 1)
                )
            pltpu.matmul_acc_lhs(products[chunk], jnp.concatenate(lines, 0))

        def middle(chunk):
            spectrum = pltpu.matmul_pop(products[chunk])
            lines = []
            for j in range(RADIX):
                spot = slice(j * SUB, (j + 1) * SUB)
                real, imag = spectrum[spot, :width], spectrum[spot, width:]
                real, imag = turn(real, imag, wave(2, j), wave(3, j))
                lines.append(
                    jnp.concatenate([imag.astype(jnp.bfloat16), real.astype(jnp.bfloat16)], 1)
                )
            pltpu.matmul_acc_lhs(products[chunks + chunk], jnp.concatenate(lines, 0))

        def backward(chunk, lowest):
            back = pltpu.matmul_pop(products[chunks + chunk])
            parts = []
            for j in range(RADIX):
                spot = slice(j * SUB, (j + 1) * SUB)
                real, imag = back[spot, width:], back[spot, :width]
                if j:
                    real, imag = turn(real, imag, wave(0, j), wave(1, j))
                parts.append((real, imag))
            if lowest:
                return [tuple(sum(part[1:], part[0]) for part in zip(*parts))]
            return radix_eight(parts, 1)

        def power_rows(step, chunk, real, imag):
            power = gain * (real * real + imag * imag)
            spot = slice(chunk * SUB, (chunk + 1) * SUB)
            polar_ref[spot, step * VB : (step + 1) * VB] = power.astype(jnp.bfloat16)

        def one_slab(number, last):
            events = []
            for step in range(steps):
                for chunk in range(chunks):
                    start = chunks * step + chunk
                    events.append((start, "forward", step, chunk))
                    events.append((start + 1.5, "middle", step, chunk))
            for chunk in range(chunks):
                events.append((chunks * steps + chunk, "leave", steps, chunk))
            for _, kind, step, chunk in sorted(events):
                if kind == "middle":
                    middle(chunk)
                    continue
                if step == 0:
                    forward(number * steps, chunk, entering(chunk))
                    continue
                field = backward(chunk, kind == "leave" and last)
                if last:
                    power_rows(step - 1, chunk, *field[0])
                if kind == "forward":
                    forward(number * steps + step, chunk, field)
                elif not last:
                    spot = slice(chunk * SUB, (chunk + 1) * SUB)
                    for q in range(RADIX):
                        for part in range(2):
                            field_ref[part, spot, q * width : (q + 1) * width] = field[q][
                                part
                            ].astype(jnp.bfloat16)

        def whole_slab(number, carry):
            one_slab(number, False)
            return carry

        lax.fori_loop(0, slab, whole_slab, 0)
        one_slab(slab, True)

    pl.run_scoped(run, *units)


def in_hbm(operands):
    return [pltpu.with_memory_space_constraint(value, pltpu.HBM) for value in operands]


def march(field, phase_table, profile_index, group_power, group_slot, units):
    rows, height = field.shape[1:]
    slabs, steps = profile_index.shape
    weights, waves = march_constants(height)
    operands = [profile_index, group_power, group_slot, phase_table, waves, field, weights]
    places = [pltpu.SMEM] * 3 + [pltpu.VMEM] * 4
    return pl.pallas_call(
        functools.partial(march_kernel, steps, slabs, units=units),
        out_shape=jax.ShapeDtypeStruct((rows, steps * VB), jnp.bfloat16),
        in_specs=[pl.BlockSpec(memory_space=pltpu.HBM)] * len(operands),
        out_specs=pl.BlockSpec(memory_space=pltpu.VMEM),
        scratch_shapes=[place(o.shape, o.dtype) for place, o in zip(places, operands)]
        + [
            pltpu.VMEM((-(-slabs * steps // 8) * 8, height), jnp.float32),
            pltpu.VMEM((slabs * steps, 2, 8, height), jnp.float32),
            pltpu.SemaphoreType.DMA((len(operands),)),
        ],
        compiler_params=pltpu.CompilerParams(vmem_limit_bytes=24 * 1024 * 1024),
        name="march",
    )(*in_hbm(operands))


def prepare_kernel(
    local_rows,
    shift_hbm,
    sub_hbm,
    count_hbm,
    row_hbm,
    col_hbm,
    after_ref,
    starts_ref,
    turned_ref,
    col_ref,
    passed_ref,
    shift_ref,
    sub_ref,
    count_ref,
    row_ref,
    sems,
):
    pairs = (
        (shift_hbm, shift_ref),
        (sub_hbm, sub_ref),
        (count_hbm, count_ref),
        (row_hbm, row_ref),
        (col_hbm, col_ref),
    )
    copies = [
        pltpu.make_async_copy(source, target, sems.at[number])
        for number, (source, target) in enumerate(pairs)
    ]
    for copy in copies:
        copy.start()
    tile = lax.axis_index("radial")
    devices = lax.axis_size("radial")
    for copy in copies[:4]:
        copy.wait()
    column = lax.broadcasted_iota(jnp.int32, starts_ref.shape, 1)
    starts = jnp.full(starts_ref.shape, -1, jnp.int32)
    for slot in range(K_MAX):
        source = lax.rem(tile + shift_ref[0, tile] + slot // CAP, devices)
        start = source * local_rows + sub_ref[0, tile, slot] * SUB
        start = jnp.where(slot < count_ref[0, tile], start, -1)
        starts = jnp.where(column == slot, start, starts)
    starts_ref[...] = starts
    turned_ref[...] = row_ref[...].T
    passed_ref[...] = after_ref[...]
    copies[4].wait()


def prepare(source_shift, slot_sub, tile_count, row_weights, col_weights, local_rows, after):
    pixels = row_weights.shape[-1]
    rows_flat = row_weights.reshape(K_MAX * SUB, pixels)
    cols_flat = col_weights.reshape(K_MAX, col_weights.shape[-2], pixels)
    operands = [source_shift, slot_sub, tile_count, rows_flat]
    places = [pltpu.SMEM] * 3 + [pltpu.VMEM]
    return pl.pallas_call(
        functools.partial(prepare_kernel, local_rows),
        out_shape=[
            jax.ShapeDtypeStruct((8, 128), jnp.int32),
            jax.ShapeDtypeStruct((pixels, K_MAX * SUB), jnp.bfloat16),
            jax.ShapeDtypeStruct(cols_flat.shape, jnp.bfloat16),
            jax.ShapeDtypeStruct(after.shape, after.dtype),
        ],
        in_specs=[pl.BlockSpec(memory_space=pltpu.HBM)] * 5
        + [pl.BlockSpec(memory_space=pltpu.VMEM)],
        out_specs=[pl.BlockSpec(memory_space=pltpu.VMEM)] * 4,
        scratch_shapes=[place(o.shape, o.dtype) for place, o in zip(places, operands)]
        + [pltpu.SemaphoreType.DMA((5,))],
        compiler_params=pltpu.CompilerParams(vmem_limit_bytes=24 * 1024 * 1024),
        cost_estimate=pl.CostEstimate(
            flops=2_000_000_000, bytes_accessed=2 * cols_flat.size, transcendentals=0
        ),
        name="prepare",
    )(*in_hbm(operands + [cols_flat]), after)


def tile_kernel(places, units, starts_ref, *refs):
    part_refs = refs[: len(places)]
    row_ref, col_ref, out_ref, polar_ref = refs[len(places) :]
    chip = lax.axis_index("radial") // 2
    core = lax.axis_index("radial") % 2
    half = out_ref.shape[0] // 2

    def run(*products):
        def stage(slot):
            pltpu.matmul_push_rhs(col_ref[slot], slot // 2 % 2, slot % 2)

        for slot in range(4):
            stage(slot)
        starts = [starts_ref[0:1, slot : slot + 1][0, 0] for slot in range(K_MAX)]
        for (even, odd), part_ref in zip(places, part_refs):
            size = part_ref.shape[0]
            start = jnp.where(core == 0, chip ^ even, chip ^ odd) * size
            if size == polar_ref.shape[0]:
                start = 0
            polar_ref[pl.ds(start, size), :] = part_ref[...]
        for slot, start in enumerate(starts):
            block = polar_ref[pl.ds(pl.multiple_of(jnp.maximum(start, 0), SUB), SUB), :]
            block = jnp.where(start >= 0, block, jnp.zeros_like(block))
            pltpu.matmul_acc_lhs(products[slot], block, load_staged_rhs=slot // 2 % 2)
            if slot + 4 < K_MAX:
                stage(slot + 4)
        mixed = [pltpu.matmul_pop(product).astype(jnp.bfloat16) for product in products[:K_MAX]]
        mixed = jnp.concatenate(mixed, 0)
        for unit, product in enumerate(products[K_MAX:]):
            pltpu.matmul_push_rhs(mixed, 0, unit)
            lines = slice(unit * half, (unit + 1) * half)
            pltpu.matmul_acc_lhs(product, row_ref[lines, :], load_staged_rhs=0)
        for unit, product in enumerate(products[K_MAX:]):
            out_ref[unit * half : (unit + 1) * half, :] = pltpu.matmul_pop(product)

    pl.run_scoped(run, *units)


def tile_sum(starts, parts, places, row_weights, col_weights, units):
    pixels = row_weights.shape[0]
    channels = col_weights.shape[-2]
    radials = sum(part.shape[0] for part in parts)
    vmem = pl.BlockSpec(memory_space=pltpu.VMEM)
    return pl.pallas_call(
        functools.partial(tile_kernel, places, units),
        out_shape=jax.ShapeDtypeStruct((pixels, pixels), jnp.float32),
        in_specs=[vmem] * (len(parts) + 3),
        out_specs=vmem,
        scratch_shapes=[
            pltpu.VMEM((radials, channels), jnp.bfloat16),
        ],
        compiler_params=pltpu.CompilerParams(vmem_limit_bytes=24 * 1024 * 1024),
        name="tile_sum",
    )(
        starts,
        *parts,
        row_weights,
        col_weights,
    )


def swap(value, distance, devices):
    return lax.ppermute(value, "radial", [(i, i ^ distance) for i in range(devices)])


def gather_parts(polar, devices, prepared):
    if devices != 16:
        whole = lax.all_gather(polar, "radial", axis=0, tiled=True)
        return [whole], [(0, 0)], prepared(polar)[:3]
    core = lax.axis_index("radial") % 2
    size = 2 * polar.shape[0]

    def in_order(own, other):
        return jnp.where(
            core == 0, jnp.concatenate([own, other], 0), jnp.concatenate([other, own], 0)
        )

    first = swap(polar, 2, devices)
    pair = in_order(polar, swap(polar, 1, devices))
    held = []
    for even, odd in ((4, 5), (2, 3), (6, 7)):
        routes = [(i, i ^ (2 * (odd if i % 2 else even))) for i in range(devices)]
        held.append(lax.ppermute(pair, "radial", routes))
    *ready, first = prepared(first)
    early = swap(jnp.concatenate([held[2], first], 0), 1, devices)
    late = swap(jnp.concatenate(held[:2], 0), 1, devices)
    parts = [pair] + held
    parts += [late[i * size : (i + 1) * size] for i in range(2)]
    parts += [early[i * size : (i + 1) * size] for i in range(1)]
    parts.append(in_order(first, early[1 * size :]))
    places = [(0, 0), (4, 5), (2, 3), (6, 7), (5, 4), (3, 2), (7, 6), (1, 1)]
    return parts, places, ready


def per_device(
    units,
    tile_units,
    field_start,
    phase_table,
    profile_index,
    group_power,
    group_slot,
    source_shift,
    slot_sub,
    tile_count,
    row_weights,
    col_weights,
):
    devices = lax.axis_size("radial")
    polar = march(field_start, phase_table, profile_index, group_power, group_slot, units)
    prepared = functools.partial(
        prepare, source_shift, slot_sub, tile_count, row_weights, col_weights, polar.shape[0]
    )
    parts, places, ready = gather_parts(polar, devices, prepared)
    starts, turned, cols = ready
    tile_value = tile_sum(starts, parts, places, turned, cols, tile_units)
    return tile_value.reshape((1, 1) + tile_value.shape)


def solution(mesh):
    with jax.sharding.use_abstract_mesh(mesh.abstract_mesh):
        units = [
            pltpu.ACC(number // CHUNKS)((RADIX * SUB, 256), jnp.float32)
            for number in range(2 * CHUNKS)
        ]
        tile_units = [pltpu.ACC(slot % 2)((SUB, 256), jnp.float32) for slot in range(K_MAX)]
        tile_units += [pltpu.ACC(unit)((128, 256), jnp.float32) for unit in range(2)]
    return jax.shard_map(
        functools.partial(per_device, units, tile_units),
        mesh=mesh,
        in_specs=(
            P(None, "radial", None),
            P(),
            P(),
            P(),
            P(),
            P("range", None),
            P("range", None, None),
            P("range", None),
            P("range", "radial", None, None, None),
            P("range", "radial", None, None, None),
        ),
        out_specs=P("range", "radial", None, None),
        check_vma=False,
    )
```

```python
import functools
import math

import jax
import jax.numpy as jnp
import numpy as np
from jax import lax
from jax.experimental import pallas as pl
from jax.experimental.pallas import tpu as pltpu
from jax.sharding import PartitionSpec as P

VB = 128
SUB = 16
K_MAX = 16
CAP = 2
GROUP_RADIALS = 512
RADIX = 8
CHUNKS = 4

spread_angle = 6.0
absorb_rate = 0.5


def march_constants(height):
    width = height // RADIX
    index = np.arange(width)
    angle = 2.0 * np.pi / width * (index[:, None] * index[None, :] % width)
    factor = 1.0 / math.sqrt(height)
    cosine, sine = np.cos(angle) * factor, np.sin(angle) * factor
    weights = np.block([[cosine, -sine], [sine, cosine]]).astype(jnp.bfloat16)
    turn = 2.0 * np.pi / height * (np.arange(RADIX)[:, None] * index[None, :])
    level = np.arange(height)
    folded = np.minimum(level, height - level).astype(np.float64)
    theta = -spread_angle * (2.0 * folded / height) ** 2
    theta = theta.reshape(width, RADIX).T
    depth = np.maximum(0.0, (level - 0.9375 * height) / (0.0625 * height))
    absorber = np.exp(-absorb_rate * depth * depth).reshape(RADIX, width)
    waves = np.concatenate([np.cos(turn), np.sin(turn), np.cos(theta), np.sin(theta), absorber], 0)
    waves = np.pad(waves, ((0, -len(waves) % 8), (0, 0)))
    return weights, waves.astype(np.float32)


def cos_sin(angle):
    square = angle * angle
    cosine = jnp.full_like(angle, 1.0 / math.factorial(14) * -1.0)
    for order in (12, 10, 8, 6, 4, 2, 0):
        cosine = cosine * square + (-1.0) ** (order // 2) / math.factorial(order)
    sine = jnp.full_like(angle, 1.0 / math.factorial(13))
    for order in (11, 9, 7, 5, 3, 1):
        sine = sine * square + (-1.0) ** (order // 2) / math.factorial(order)
    return cosine, sine * angle


def turn(real, imag, cosine, sine):
    return real * cosine - imag * sine, real * sine + imag * cosine


def turn_back(real, imag, cosine, sine):
    return real * cosine + imag * sine, imag * cosine - real * sine


def radix_four(parts, sign):
    (r0, i0), (r1, i1), (r2, i2), (r3, i3) = parts
    sr02, si02, dr02, di02 = r0 + r2, i0 + i2, r0 - r2, i0 - i2
    sr13, si13, dr13, di13 = r1 + r3, i1 + i3, r1 - r3, i1 - i3
    plus = (dr02 - di13, di02 + dr13)
    minus = (dr02 + di13, di02 - dr13)
    if sign < 0:
        plus, minus = minus, plus
    return (sr02 + sr13, si02 + si13), plus, (sr02 - sr13, si02 - si13), minus


def radix_eight(parts, sign):
    sums, turned = [], []
    for q in range(4):
        (r, i), (s, t) = parts[q], parts[q + 4]
        sums.append((r + s, i + t))
        turned.append((r - s, i - t))
    half = math.sqrt(0.5)
    (r, i), (s, t), (v, w) = turned[1:]
    if sign < 0:
        turned[1] = ((r + i) * half, (i - r) * half)
        turned[2] = (t, -s)
        turned[3] = ((w - v) * half, (v + w) * -half)
    else:
        turned[1] = ((r - i) * half, (r + i) * half)
        turned[2] = (-t, s)
        turned[3] = ((v + w) * -half, (v - w) * half)
    even, odd = radix_four(sums, sign), radix_four(turned, sign)
    return [part for pair in zip(even, odd) for part in pair]


def march_kernel(
    steps,
    slabs,
    profile_hbm,
    power_hbm,
    slot_hbm,
    phase_hbm,
    wave_hbm,
    field_hbm,
    weight_hbm,
    polar_ref,
    profile_ref,
    power_ref,
    slot_ref,
    phase_ref,
    wave_ref,
    field_ref,
    weight_ref,
    phase_rows,
    screen_ref,
    sems,
    units,
):
    pairs = (
        (profile_hbm, profile_ref),
        (phase_hbm, phase_ref),
        (wave_hbm, wave_ref),
        (field_hbm, field_ref),
        (weight_hbm, weight_ref),
        (power_hbm, power_ref),
        (slot_hbm, slot_ref),
    )
    copies = [
        pltpu.make_async_copy(source, target, sems.at[number])
        for number, (source, target) in enumerate(pairs)
    ]
    for copy in copies:
        copy.start()
    rows, height = field_ref.shape[1:]
    width = height // RADIX
    chunks = rows // SUB
    slab = lax.axis_index("range")
    tile = lax.axis_index("radial")
    total = slabs * steps
    for copy in copies[:3]:
        copy.wait()
    for place in range(total):
        phase_rows[place : place + 1, :] = phase_ref[
            pl.ds(profile_ref[place // steps, place % steps], 1), :
        ]
    for q in range(RADIX):
        columns = slice(q * width, (q + 1) * width)
        cosine, sine = cos_sin(phase_rows[:, columns])
        absorber = wave_ref[4 * RADIX + q : 4 * RADIX + q + 1, :]
        damp = jnp.where(lax.broadcasted_iota(jnp.int32, cosine.shape, 0) == 0, 1.0, absorber)
        for part, value in enumerate((cosine * damp, sine * damp)):
            for place in range(total):
                screen_ref[place, part, :, columns] = jnp.broadcast_to(
                    value[place : place + 1], (8, width)
                )
    for copy in copies[3:]:
        copy.wait()
    gain = power_ref[slot_ref[tile * rows // GROUP_RADIALS]]

    def run(*products):
        for unit in range(2):
            pltpu.matmul_push_rhs(weight_ref[...], 0, unit)
            pltpu.matmul_acc_lhs(
                products[chunks * unit], jnp.zeros((RADIX * SUB, 2 * width), jnp.bfloat16), load_staged_rhs=0
            )
            pltpu.matmul_pop(products[chunks * unit])

        def wave(kind, j):
            return wave_ref[kind * RADIX + j : kind * RADIX + j + 1, :]

        def entering(chunk):
            spot = slice(chunk * SUB, (chunk + 1) * SUB)
            return [
                tuple(
                    field_ref[part, spot, q * width : (q + 1) * width].astype(jnp.float32)
                    for part in range(2)
                )
                for q in range(RADIX)
            ]

        def forward(place, chunk, field):
            parts, lines = [], []
            for q in range(RADIX):
                columns = slice(q * width, (q + 1) * width)
                screen = [screen_ref[place, part, :, columns] for part in range(2)]
                screen = [jnp.concatenate([value] * (SUB // 8), 0) for value in screen]
                parts.append(turn(*field[q], *screen))
            for j, (real, imag) in enumerate(radix_eight(parts, -1)):
                if j:
                    real, imag = turn_back(real, imag, wave(0, j), wave(1, j))
                lines.append(
                    jnp.concatenate([real.astype(jnp.bfloat16), imag.astype(jnp.bfloat16)], 1)
                )
            pltpu.matmul_acc_lhs(products[chunk], jnp.concatenate(lines, 0))

        def middle(chunk):
            spectrum = pltpu.matmul_pop(products[chunk])
            lines = []
            for j in range(RADIX):
                spot = slice(j * SUB, (j + 1) * SUB)
                real, imag = spectrum[spot, :width], spectrum[spot, width:]
                real, imag = turn(real, imag, wave(2, j), wave(3, j))
                lines.append(
                    jnp.concatenate([imag.astype(jnp.bfloat16), real.astype(jnp.bfloat16)], 1)
                )
            pltpu.matmul_acc_lhs(products[chunks + chunk], jnp.concatenate(lines, 0))

        def backward(chunk, lowest):
            back = pltpu.matmul_pop(products[chunks + chunk])
            parts = []
            for j in range(RADIX):
                spot = slice(j * SUB, (j + 1) * SUB)
                real, imag = back[spot, width:], back[spot, :width]
                if j:
                    real, imag = turn(real, imag, wave(0, j), wave(1, j))
                parts.append((real, imag))
            if lowest:
                return [tuple(sum(part[1:], part[0]) for part in zip(*parts))]
            return radix_eight(parts, 1)

        def power_rows(step, chunk, real, imag):
            power = gain * (real * real + imag * imag)
            spot = slice(chunk * SUB, (chunk + 1) * SUB)
            polar_ref[spot, step * VB : (step + 1) * VB] = power.astype(jnp.bfloat16)

        def one_slab(number, last):
            events = []
            for step in range(steps):
                for chunk in range(chunks):
                    start = chunks * step + chunk
                    events.append((start, "forward", step, chunk))
                    events.append((start + 1.5, "middle", step, chunk))
            for chunk in range(chunks):
                events.append((chunks * steps + chunk, "leave", steps, chunk))
            for _, kind, step, chunk in sorted(events):
                if kind == "middle":
                    middle(chunk)
                    continue
                if step == 0:
                    forward(number * steps, chunk, entering(chunk))
                    continue
                field = backward(chunk, kind == "leave" and last)
                if last:
                    power_rows(step - 1, chunk, *field[0])
                if kind == "forward":
                    forward(number * steps + step, chunk, field)
                elif not last:
                    spot = slice(chunk * SUB, (chunk + 1) * SUB)
                    for q in range(RADIX):
                        for part in range(2):
                            field_ref[part, spot, q * width : (q + 1) * width] = field[q][
                                part
                            ].astype(jnp.bfloat16)

        def whole_slab(number, carry):
            one_slab(number, False)
            return carry

        lax.fori_loop(0, slab, whole_slab, 0)
        one_slab(slab, True)

    pl.run_scoped(run, *units)


def in_hbm(operands):
    return [pltpu.with_memory_space_constraint(value, pltpu.HBM) for value in operands]


def march(field, phase_table, profile_index, group_power, group_slot, units):
    rows, height = field.shape[1:]
    slabs, steps = profile_index.shape
    weights, waves = march_constants(height)
    operands = [profile_index, group_power, group_slot, phase_table, waves, field, weights]
    places = [pltpu.SMEM] * 3 + [pltpu.VMEM] * 4
    return pl.pallas_call(
        functools.partial(march_kernel, steps, slabs, units=units),
        out_shape=jax.ShapeDtypeStruct((rows, steps * VB), jnp.bfloat16),
        in_specs=[pl.BlockSpec(memory_space=pltpu.HBM)] * len(operands),
        out_specs=pl.BlockSpec(memory_space=pltpu.VMEM),
        scratch_shapes=[place(o.shape, o.dtype) for place, o in zip(places, operands)]
        + [
            pltpu.VMEM((-(-slabs * steps // 8) * 8, height), jnp.float32),
            pltpu.VMEM((slabs * steps, 2, 8, height), jnp.float32),
            pltpu.SemaphoreType.DMA((len(operands),)),
        ],
        compiler_params=pltpu.CompilerParams(vmem_limit_bytes=24 * 1024 * 1024),
        name="march",
    )(*in_hbm(operands))


def prepare_kernel(
    local_rows,
    shift_hbm,
    sub_hbm,
    count_hbm,
    row_hbm,
    col_hbm,
    after_ref,
    starts_ref,
    turned_ref,
    col_ref,
    passed_ref,
    shift_ref,
    sub_ref,
    count_ref,
    row_ref,
    sems,
):
    pairs = (
        (shift_hbm, shift_ref),
        (sub_hbm, sub_ref),
        (count_hbm, count_ref),
        (row_hbm, row_ref),
        (col_hbm, col_ref),
    )
    copies = [
        pltpu.make_async_copy(source, target, sems.at[number])
        for number, (source, target) in enumerate(pairs)
    ]
    for copy in copies:
        copy.start()
    tile = lax.axis_index("radial")
    devices = lax.axis_size("radial")
    for copy in copies[:4]:
        copy.wait()
    column = lax.broadcasted_iota(jnp.int32, starts_ref.shape, 1)
    starts = jnp.full(starts_ref.shape, -1, jnp.int32)
    for slot in range(K_MAX):
        source = lax.rem(tile + shift_ref[0, tile] + slot // CAP, devices)
        start = source * local_rows + sub_ref[0, tile, slot] * SUB
        start = jnp.where(slot < count_ref[0, tile], start, -1)
        starts = jnp.where(column == slot, start, starts)
    starts_ref[...] = starts
    turned_ref[...] = row_ref[...].T
    passed_ref[...] = after_ref[...]
    copies[4].wait()


def prepare(source_shift, slot_sub, tile_count, row_weights, col_weights, local_rows, after):
    pixels = row_weights.shape[-1]
    rows_flat = row_weights.reshape(K_MAX * SUB, pixels)
    cols_flat = col_weights.reshape(K_MAX, col_weights.shape[-2], pixels)
    operands = [source_shift, slot_sub, tile_count, rows_flat]
    places = [pltpu.SMEM] * 3 + [pltpu.VMEM]
    return pl.pallas_call(
        functools.partial(prepare_kernel, local_rows),
        out_shape=[
            jax.ShapeDtypeStruct((8, 128), jnp.int32),
            jax.ShapeDtypeStruct((pixels, K_MAX * SUB), jnp.bfloat16),
            jax.ShapeDtypeStruct(cols_flat.shape, jnp.bfloat16),
            jax.ShapeDtypeStruct(after.shape, after.dtype),
        ],
        in_specs=[pl.BlockSpec(memory_space=pltpu.HBM)] * 5
        + [pl.BlockSpec(memory_space=pltpu.VMEM)],
        out_specs=[pl.BlockSpec(memory_space=pltpu.VMEM)] * 4,
        scratch_shapes=[place(o.shape, o.dtype) for place, o in zip(places, operands)]
        + [pltpu.SemaphoreType.DMA((5,))],
        compiler_params=pltpu.CompilerParams(vmem_limit_bytes=24 * 1024 * 1024),
        cost_estimate=pl.CostEstimate(
            flops=2_000_000_000, bytes_accessed=2 * cols_flat.size, transcendentals=0
        ),
        name="prepare",
    )(*in_hbm(operands + [cols_flat]), after)


def tile_kernel(places, starts_ref, *refs):
    part_refs = refs[: len(places)]
    row_ref, col_ref, out_ref, polar_ref, mixed_ref = refs[len(places) :]
    chip = lax.axis_index("radial") // 2
    core = lax.axis_index("radial") % 2
    for pieces, part_ref in zip(places, part_refs):
        size = part_ref.shape[0] // len(pieces)
        for piece, (even, odd) in enumerate(pieces):
            start = jnp.where(core == 0, chip ^ even, chip ^ odd) * size
            if size == polar_ref.shape[0]:
                start = 0
            polar_ref[pl.ds(start, size), :] = part_ref[piece * size : (piece + 1) * size, :]
    starts = [starts_ref[0:1, slot : slot + 1][0, 0] for slot in range(K_MAX)]
    for slot, start in enumerate(starts):
        block = polar_ref[pl.ds(pl.multiple_of(jnp.maximum(start, 0), SUB), SUB), :]
        block = jnp.where(start >= 0, block, jnp.zeros_like(block))
        mixed = jnp.dot(block, col_ref[slot], preferred_element_type=jnp.float32)
        mixed_ref[slot * SUB : (slot + 1) * SUB, :] = mixed.astype(jnp.bfloat16)
    out_ref[...] = jnp.dot(row_ref[...], mixed_ref[...], preferred_element_type=jnp.float32)


def tile_sum(starts, parts, places, row_weights, col_weights):
    pixels = row_weights.shape[0]
    channels = col_weights.shape[-2]
    radials = sum(part.shape[0] for part in parts)
    vmem = pl.BlockSpec(memory_space=pltpu.VMEM)
    return pl.pallas_call(
        functools.partial(tile_kernel, places),
        out_shape=jax.ShapeDtypeStruct((pixels, pixels), jnp.float32),
        in_specs=[vmem] * (len(parts) + 3),
        out_specs=vmem,
        scratch_shapes=[
            pltpu.VMEM((radials, channels), jnp.bfloat16),
            pltpu.VMEM((K_MAX * SUB, pixels), jnp.bfloat16),
        ],
        compiler_params=pltpu.CompilerParams(vmem_limit_bytes=24 * 1024 * 1024),
        name="tile_sum",
    )(
        starts,
        *parts,
        row_weights,
        col_weights,
    )


def swap(value, distance, devices):
    return lax.ppermute(value, "radial", [(i, i ^ distance) for i in range(devices)])


def gather_parts(polar, devices, prepared):
    if devices != 16:
        whole = lax.all_gather(polar, "radial", axis=0, tiled=True)
        return [whole], [[(0, 0)]], prepared(polar)[:3]
    core = lax.axis_index("radial") % 2
    size = 2 * polar.shape[0]

    def in_order(own, other):
        return jnp.where(
            core == 0, jnp.concatenate([own, other], 0), jnp.concatenate([other, own], 0)
        )

    first = swap(polar, 2, devices)
    pair = in_order(polar, swap(polar, 1, devices))
    held = []
    for even, odd in ((4, 5), (2, 3), (6, 7)):
        routes = [(i, i ^ (2 * (odd if i % 2 else even))) for i in range(devices)]
        held.append(lax.ppermute(pair, "radial", routes))
    *ready, first = prepared(first)
    early = swap(jnp.concatenate([held[2], first], 0), 1, devices)
    late = swap(jnp.concatenate(held[:2], 0), 1, devices)
    parts = [pair] + held + [late, early[:size], in_order(first, early[size:])]
    places = [[(0, 0)], [(4, 5)], [(2, 3)], [(6, 7)], [(5, 4), (3, 2)], [(7, 6)], [(1, 1)]]
    return parts, places, ready


def per_device(
    units,
    field_start,
    phase_table,
    profile_index,
    group_power,
    group_slot,
    source_shift,
    slot_sub,
    tile_count,
    row_weights,
    col_weights,
):
    devices = lax.axis_size("radial")
    polar = march(field_start, phase_table, profile_index, group_power, group_slot, units)
    prepared = functools.partial(
        prepare, source_shift, slot_sub, tile_count, row_weights, col_weights, polar.shape[0]
    )
    parts, places, ready = gather_parts(polar, devices, prepared)
    starts, turned, cols = ready
    tile_value = tile_sum(starts, parts, places, turned, cols)
    return tile_value.reshape((1, 1) + tile_value.shape)


def solution(mesh):
    with jax.sharding.use_abstract_mesh(mesh.abstract_mesh):
        units = [
            pltpu.ACC(number // CHUNKS)((RADIX * SUB, 256), jnp.float32)
            for number in range(2 * CHUNKS)
        ]
    return jax.shard_map(
        functools.partial(per_device, units),
        mesh=mesh,
        in_specs=(
            P(None, "radial", None),
            P(),
            P(),
            P(),
            P(),
            P("range", None),
            P("range", None, None),
            P("range", None),
            P("range", "radial", None, None, None),
            P("range", "radial", None, None, None),
        ),
        out_specs=P("range", "radial", None, None),
        check_vma=False,
    )
```

```python
import functools
import math

import jax
import jax.numpy as jnp
import numpy as np
from jax import lax
from jax.experimental import pallas as pl
from jax.experimental.pallas import tpu as pltpu
from jax.sharding import PartitionSpec as P

VB = 128
SUB = 16
K_MAX = 16
CAP = 2
GROUP_RADIALS = 512
RADIX = 8
CHUNKS = 4

spread_angle = 6.0
absorb_rate = 0.5


def march_constants(height):
    width = height // RADIX
    index = np.arange(width)
    angle = 2.0 * np.pi / width * (index[:, None] * index[None, :] % width)
    factor = 1.0 / math.sqrt(height)
    cosine, sine = np.cos(angle) * factor, np.sin(angle) * factor
    weights = np.block([[cosine, -sine], [sine, cosine]]).astype(jnp.bfloat16)
    turn = 2.0 * np.pi / height * (np.arange(RADIX)[:, None] * index[None, :])
    level = np.arange(height)
    folded = np.minimum(level, height - level).astype(np.float64)
    theta = -spread_angle * (2.0 * folded / height) ** 2
    theta = theta.reshape(width, RADIX).T
    depth = np.maximum(0.0, (level - 0.9375 * height) / (0.0625 * height))
    absorber = np.exp(-absorb_rate * depth * depth).reshape(RADIX, width)
    waves = np.concatenate([np.cos(turn), np.sin(turn), np.cos(theta), np.sin(theta), absorber], 0)
    waves = np.pad(waves, ((0, -len(waves) % 8), (0, 0)))
    return weights, waves.astype(np.float32)


def cos_sin(angle):
    square = angle * angle
    cosine = jnp.full_like(angle, 1.0 / math.factorial(14) * -1.0)
    for order in (12, 10, 8, 6, 4, 2, 0):
        cosine = cosine * square + (-1.0) ** (order // 2) / math.factorial(order)
    sine = jnp.full_like(angle, 1.0 / math.factorial(13))
    for order in (11, 9, 7, 5, 3, 1):
        sine = sine * square + (-1.0) ** (order // 2) / math.factorial(order)
    return cosine, sine * angle


def turn(real, imag, cosine, sine):
    return real * cosine - imag * sine, real * sine + imag * cosine


def turn_back(real, imag, cosine, sine):
    return real * cosine + imag * sine, imag * cosine - real * sine


def radix_four(parts, sign):
    (r0, i0), (r1, i1), (r2, i2), (r3, i3) = parts
    sr02, si02, dr02, di02 = r0 + r2, i0 + i2, r0 - r2, i0 - i2
    sr13, si13, dr13, di13 = r1 + r3, i1 + i3, r1 - r3, i1 - i3
    plus = (dr02 - di13, di02 + dr13)
    minus = (dr02 + di13, di02 - dr13)
    if sign < 0:
        plus, minus = minus, plus
    return (sr02 + sr13, si02 + si13), plus, (sr02 - sr13, si02 - si13), minus


def radix_eight(parts, sign):
    sums, turned = [], []
    for q in range(4):
        (r, i), (s, t) = parts[q], parts[q + 4]
        sums.append((r + s, i + t))
        turned.append((r - s, i - t))
    half = math.sqrt(0.5)
    (r, i), (s, t), (v, w) = turned[1:]
    if sign < 0:
        turned[1] = ((r + i) * half, (i - r) * half)
        turned[2] = (t, -s)
        turned[3] = ((w - v) * half, (v + w) * -half)
    else:
        turned[1] = ((r - i) * half, (r + i) * half)
        turned[2] = (-t, s)
        turned[3] = ((v + w) * -half, (v - w) * half)
    even, odd = radix_four(sums, sign), radix_four(turned, sign)
    return [part for pair in zip(even, odd) for part in pair]


def march_kernel(
    steps,
    slabs,
    profile_hbm,
    power_hbm,
    slot_hbm,
    phase_hbm,
    wave_hbm,
    field_hbm,
    weight_hbm,
    polar_ref,
    profile_ref,
    power_ref,
    slot_ref,
    phase_ref,
    wave_ref,
    field_ref,
    weight_ref,
    phase_rows,
    screen_ref,
    sems,
    units,
):
    pairs = (
        (profile_hbm, profile_ref),
        (phase_hbm, phase_ref),
        (wave_hbm, wave_ref),
        (field_hbm, field_ref),
        (weight_hbm, weight_ref),
        (power_hbm, power_ref),
        (slot_hbm, slot_ref),
    )
    copies = [
        pltpu.make_async_copy(source, target, sems.at[number])
        for number, (source, target) in enumerate(pairs)
    ]
    for copy in copies:
        copy.start()
    rows, height = field_ref.shape[1:]
    width = height // RADIX
    chunks = rows // SUB
    slab = lax.axis_index("range")
    tile = lax.axis_index("radial")
    total = slabs * steps
    for copy in copies[:3]:
        copy.wait()
    for place in range(total):
        phase_rows[place : place + 1, :] = phase_ref[
            pl.ds(profile_ref[place // steps, place % steps], 1), :
        ]
    for q in range(RADIX):
        columns = slice(q * width, (q + 1) * width)
        cosine, sine = cos_sin(phase_rows[:, columns])
        absorber = wave_ref[4 * RADIX + q : 4 * RADIX + q + 1, :]
        damp = jnp.where(lax.broadcasted_iota(jnp.int32, cosine.shape, 0) == 0, 1.0, absorber)
        for part, value in enumerate((cosine * damp, sine * damp)):
            for place in range(total):
                screen_ref[place, part, :, columns] = jnp.broadcast_to(
                    value[place : place + 1], (8, width)
                )
    for copy in copies[3:]:
        copy.wait()
    gain = power_ref[slot_ref[tile * rows // GROUP_RADIALS]]

    def run(*products):
        for unit in range(2):
            pltpu.matmul_push_rhs(weight_ref[...], 0, unit)
            pltpu.matmul_acc_lhs(
                products[chunks * unit], jnp.zeros((RADIX * SUB, 2 * width), jnp.bfloat16), load_staged_rhs=0
            )
            pltpu.matmul_pop(products[chunks * unit])

        def wave(kind, j):
            return wave_ref[kind * RADIX + j : kind * RADIX + j + 1, :]

        def entering(chunk):
            spot = slice(chunk * SUB, (chunk + 1) * SUB)
            return [
                tuple(
                    field_ref[part, spot, q * width : (q + 1) * width].astype(jnp.float32)
                    for part in range(2)
                )
                for q in range(RADIX)
            ]

        def forward(place, chunk, field):
            parts, lines = [], []
            for q in range(RADIX):
                columns = slice(q * width, (q + 1) * width)
                screen = [screen_ref[place, part, :, columns] for part in range(2)]
                screen = [jnp.concatenate([value] * (SUB // 8), 0) for value in screen]
                parts.append(turn(*field[q], *screen))
            for j, (real, imag) in enumerate(radix_eight(parts, -1)):
                if j:
                    real, imag = turn_back(real, imag, wave(0, j), wave(1, j))
                lines.append(
                    jnp.concatenate([real.astype(jnp.bfloat16), imag.astype(jnp.bfloat16)], 1)
                )
            pltpu.matmul_acc_lhs(products[chunk], jnp.concatenate(lines, 0))

        def middle(chunk):
            spectrum = pltpu.matmul_pop(products[chunk])
            lines = []
            for j in range(RADIX):
                spot = slice(j * SUB, (j + 1) * SUB)
                real, imag = spectrum[spot, :width], spectrum[spot, width:]
                real, imag = turn(real, imag, wave(2, j), wave(3, j))
                lines.append(
                    jnp.concatenate([imag.astype(jnp.bfloat16), real.astype(jnp.bfloat16)], 1)
                )
            pltpu.matmul_acc_lhs(products[chunks + chunk], jnp.concatenate(lines, 0))

        def backward(chunk, lowest):
            back = pltpu.matmul_pop(products[chunks + chunk])
            parts = []
            for j in range(RADIX):
                spot = slice(j * SUB, (j + 1) * SUB)
                real, imag = back[spot, width:], back[spot, :width]
                if j:
                    real, imag = turn(real, imag, wave(0, j), wave(1, j))
                parts.append((real, imag))
            if lowest:
                return [tuple(sum(part[1:], part[0]) for part in zip(*parts))]
            return radix_eight(parts, 1)

        def power_rows(step, chunk, real, imag):
            power = gain * (real * real + imag * imag)
            spot = slice(chunk * SUB, (chunk + 1) * SUB)
            polar_ref[spot, step * VB : (step + 1) * VB] = power.astype(jnp.bfloat16)

        def one_slab(number, last):
            events = []
            for step in range(steps):
                for chunk in range(chunks):
                    start = chunks * step + chunk
                    events.append((start, "forward", step, chunk))
                    events.append((start + 0.6, "middle", step, chunk))
            for chunk in range(chunks):
                events.append((chunks * steps + chunk, "leave", steps, chunk))
            for _, kind, step, chunk in sorted(events):
                if kind == "middle":
                    middle(chunk)
                    continue
                if step == 0:
                    forward(number * steps, chunk, entering(chunk))
                    continue
                field = backward(chunk, kind == "leave" and last)
                if last:
                    power_rows(step - 1, chunk, *field[0])
                if kind == "forward":
                    forward(number * steps + step, chunk, field)
                elif not last:
                    spot = slice(chunk * SUB, (chunk + 1) * SUB)
                    for q in range(RADIX):
                        for part in range(2):
                            field_ref[part, spot, q * width : (q + 1) * width] = field[q][
                                part
                            ].astype(jnp.bfloat16)

        def whole_slab(number, carry):
            one_slab(number, False)
            return carry

        lax.fori_loop(0, slab, whole_slab, 0)
        one_slab(slab, True)

    pl.run_scoped(run, *units)


def in_hbm(operands):
    return [pltpu.with_memory_space_constraint(value, pltpu.HBM) for value in operands]


def march(field, phase_table, profile_index, group_power, group_slot, units):
    rows, height = field.shape[1:]
    slabs, steps = profile_index.shape
    weights, waves = march_constants(height)
    operands = [profile_index, group_power, group_slot, phase_table, waves, field, weights]
    places = [pltpu.SMEM] * 3 + [pltpu.VMEM] * 4
    return pl.pallas_call(
        functools.partial(march_kernel, steps, slabs, units=units),
        out_shape=jax.ShapeDtypeStruct((rows, steps * VB), jnp.bfloat16),
        in_specs=[pl.BlockSpec(memory_space=pltpu.HBM)] * len(operands),
        out_specs=pl.BlockSpec(memory_space=pltpu.VMEM),
        scratch_shapes=[place(o.shape, o.dtype) for place, o in zip(places, operands)]
        + [
            pltpu.VMEM((-(-slabs * steps // 8) * 8, height), jnp.float32),
            pltpu.VMEM((slabs * steps, 2, 8, height), jnp.float32),
            pltpu.SemaphoreType.DMA((len(operands),)),
        ],
        compiler_params=pltpu.CompilerParams(vmem_limit_bytes=24 * 1024 * 1024),
        name="march",
    )(*in_hbm(operands))


def prepare_kernel(
    local_rows,
    shift_hbm,
    sub_hbm,
    count_hbm,
    row_hbm,
    col_hbm,
    after_ref,
    starts_ref,
    turned_ref,
    col_ref,
    passed_ref,
    shift_ref,
    sub_ref,
    count_ref,
    row_ref,
    sems,
):
    pairs = (
        (shift_hbm, shift_ref),
        (sub_hbm, sub_ref),
        (count_hbm, count_ref),
        (row_hbm, row_ref),
        (col_hbm, col_ref),
    )
    copies = [
        pltpu.make_async_copy(source, target, sems.at[number])
        for number, (source, target) in enumerate(pairs)
    ]
    for copy in copies:
        copy.start()
    tile = lax.axis_index("radial")
    devices = lax.axis_size("radial")
    for copy in copies[:4]:
        copy.wait()
    column = lax.broadcasted_iota(jnp.int32, starts_ref.shape, 1)
    starts = jnp.full(starts_ref.shape, -1, jnp.int32)
    for slot in range(K_MAX):
        source = lax.rem(tile + shift_ref[0, tile] + slot // CAP, devices)
        start = source * local_rows + sub_ref[0, tile, slot] * SUB
        start = jnp.where(slot < count_ref[0, tile], start, -1)
        starts = jnp.where(column == slot, start, starts)
    starts_ref[...] = starts
    turned_ref[...] = row_ref[...].T
    passed_ref[...] = after_ref[...]
    copies[4].wait()


def prepare(source_shift, slot_sub, tile_count, row_weights, col_weights, local_rows, after):
    pixels = row_weights.shape[-1]
    rows_flat = row_weights.reshape(K_MAX * SUB, pixels)
    cols_flat = col_weights.reshape(K_MAX, col_weights.shape[-2], pixels)
    operands = [source_shift, slot_sub, tile_count, rows_flat]
    places = [pltpu.SMEM] * 3 + [pltpu.VMEM]
    return pl.pallas_call(
        functools.partial(prepare_kernel, local_rows),
        out_shape=[
            jax.ShapeDtypeStruct((8, 128), jnp.int32),
            jax.ShapeDtypeStruct((pixels, K_MAX * SUB), jnp.bfloat16),
            jax.ShapeDtypeStruct(cols_flat.shape, jnp.bfloat16),
            jax.ShapeDtypeStruct(after.shape, after.dtype),
        ],
        in_specs=[pl.BlockSpec(memory_space=pltpu.HBM)] * 5
        + [pl.BlockSpec(memory_space=pltpu.VMEM)],
        out_specs=[pl.BlockSpec(memory_space=pltpu.VMEM)] * 4,
        scratch_shapes=[place(o.shape, o.dtype) for place, o in zip(places, operands)]
        + [pltpu.SemaphoreType.DMA((5,))],
        compiler_params=pltpu.CompilerParams(vmem_limit_bytes=24 * 1024 * 1024),
        cost_estimate=pl.CostEstimate(
            flops=2_000_000_000, bytes_accessed=2 * cols_flat.size, transcendentals=0
        ),
        name="prepare",
    )(*in_hbm(operands + [cols_flat]), after)


def tile_kernel(places, starts_ref, *refs):
    part_refs = refs[: len(places)]
    row_ref, col_ref, out_ref, polar_ref, mixed_ref = refs[len(places) :]
    chip = lax.axis_index("radial") // 2
    core = lax.axis_index("radial") % 2
    for (even, odd), part_ref in zip(places, part_refs):
        size = part_ref.shape[0]
        start = jnp.where(core == 0, chip ^ even, chip ^ odd) * size
        if size == polar_ref.shape[0]:
            start = 0
        polar_ref[pl.ds(start, size), :] = part_ref[...]
    starts = [starts_ref[0:1, slot : slot + 1][0, 0] for slot in range(K_MAX)]
    for slot, start in enumerate(starts):
        block = polar_ref[pl.ds(pl.multiple_of(jnp.maximum(start, 0), SUB), SUB), :]
        block = jnp.where(start >= 0, block, jnp.zeros_like(block))
        mixed = jnp.dot(block, col_ref[slot], preferred_element_type=jnp.float32)
        mixed_ref[slot * SUB : (slot + 1) * SUB, :] = mixed.astype(jnp.bfloat16)
    out_ref[...] = jnp.dot(row_ref[...], mixed_ref[...], preferred_element_type=jnp.float32)


def tile_sum(starts, parts, places, row_weights, col_weights):
    pixels = row_weights.shape[0]
    channels = col_weights.shape[-2]
    radials = sum(part.shape[0] for part in parts)
    vmem = pl.BlockSpec(memory_space=pltpu.VMEM)
    return pl.pallas_call(
        functools.partial(tile_kernel, places),
        out_shape=jax.ShapeDtypeStruct((pixels, pixels), jnp.float32),
        in_specs=[vmem] * (len(parts) + 3),
        out_specs=vmem,
        scratch_shapes=[
            pltpu.VMEM((radials, channels), jnp.bfloat16),
            pltpu.VMEM((K_MAX * SUB, pixels), jnp.bfloat16),
        ],
        compiler_params=pltpu.CompilerParams(vmem_limit_bytes=24 * 1024 * 1024),
        name="tile_sum",
    )(
        starts,
        *parts,
        row_weights,
        col_weights,
    )


def swap(value, distance, devices):
    return lax.ppermute(value, "radial", [(i, i ^ distance) for i in range(devices)])


def gather_parts(polar, devices, prepared):
    if devices != 16:
        whole = lax.all_gather(polar, "radial", axis=0, tiled=True)
        return [whole], [(0, 0)], prepared(polar)[:3]
    core = lax.axis_index("radial") % 2
    size = 2 * polar.shape[0]

    def in_order(own, other):
        return jnp.where(
            core == 0, jnp.concatenate([own, other], 0), jnp.concatenate([other, own], 0)
        )

    first = swap(polar, 2, devices)
    pair = in_order(polar, swap(polar, 1, devices))
    held = []
    for even, odd in ((4, 5), (2, 3), (6, 7)):
        routes = [(i, i ^ (2 * (odd if i % 2 else even))) for i in range(devices)]
        held.append(lax.ppermute(pair, "radial", routes))
    *ready, first = prepared(first)
    early = swap(jnp.concatenate([held[2], first], 0), 1, devices)
    late = swap(jnp.concatenate(held[:2], 0), 1, devices)
    parts = [pair] + held
    parts += [late[i * size : (i + 1) * size] for i in range(2)]
    parts += [early[i * size : (i + 1) * size] for i in range(1)]
    parts.append(in_order(first, early[1 * size :]))
    places = [(0, 0), (4, 5), (2, 3), (6, 7), (5, 4), (3, 2), (7, 6), (1, 1)]
    return parts, places, ready


def per_device(
    units,
    field_start,
    phase_table,
    profile_index,
    group_power,
    group_slot,
    source_shift,
    slot_sub,
    tile_count,
    row_weights,
    col_weights,
):
    devices = lax.axis_size("radial")
    polar = march(field_start, phase_table, profile_index, group_power, group_slot, units)
    prepared = functools.partial(
        prepare, source_shift, slot_sub, tile_count, row_weights, col_weights, polar.shape[0]
    )
    parts, places, ready = gather_parts(polar, devices, prepared)
    starts, turned, cols = ready
    tile_value = tile_sum(starts, parts, places, turned, cols)
    return tile_value.reshape((1, 1) + tile_value.shape)


def solution(mesh):
    with jax.sharding.use_abstract_mesh(mesh.abstract_mesh):
        units = [
            pltpu.ACC(number // CHUNKS)((RADIX * SUB, 256), jnp.float32)
            for number in range(2 * CHUNKS)
        ]
    return jax.shard_map(
        functools.partial(per_device, units),
        mesh=mesh,
        in_specs=(
            P(None, "radial", None),
            P(),
            P(),
            P(),
            P(),
            P("range", None),
            P("range", None, None),
            P("range", None),
            P("range", "radial", None, None, None),
            P("range", "radial", None, None, None),
        ),
        out_specs=P("range", "radial", None, None),
        check_vma=False,
    )
```
